32 devices in a mesh: shard: 2 (over x), context: 4 (over y, core), tensor: 4 (over z).
Axes of the slice: x: 2, y: 2, z: 4, core: 2. Of those that a mesh axis runs over, the one named last changes fastest.
Arguments:
- clip_input: bfloat16 [4, 2, 8, 196, 768], P(None, 'shard', 'tensor', 'context'), may hold values from -6 to 6
- clip_slot: int32 [4, 2], P(None, 'shard'), may hold values from 0 to 1, as said below
- norm_gain: bfloat16 [3, 768], P(None, 'shard'), may hold values from 0.25 to 1.75
- norm_shift: bfloat16 [3, 768], P(None, 'shard'), may hold values from -2 to 2
- attention_in: bfloat16 [2, 768, 3, 768], P(None, 'shard', None, 'tensor'), may hold values from -0.21875 to 0.21875
- attention_bias: bfloat16 [2, 2, 12, 64], P(None, None, 'tensor', 'shard'), may hold values from -2 to 2
- attention_out: bfloat16 [2, 768, 768], P(None, 'tensor', 'shard'), may hold values from -0.625 to 0.625
- branch_bias: bfloat16 [4, 768], P(None, 'shard'), may hold values from -2 to 2
- temporal_fc: bfloat16 [768, 768], P('shard'), may hold values from -0.21875 to 0.21875
- hidden_in: bfloat16 [768, 3072], P('shard', 'tensor'), may hold values from -0.21875 to 0.21875
- hidden_bias: bfloat16 [24, 128], P('tensor', 'shard'), may hold values from -2 to 2
- hidden_out: bfloat16 [3072, 768], P('tensor', 'shard'), may hold values from -0.109375 to 0.109375
- output_grad: bfloat16 [4, 2, 8, 196, 768], P(None, 'shard', 'tensor', 'context'), may hold values from -6 to 6
Outputs:
- layer_out: bfloat16 [4, 2, 8, 196, 768], P(None, 'shard', 'tensor', 'context')
- input_grad: bfloat16 [4, 2, 8, 196, 768], P(None, 'shard', 'tensor', 'context')
- norm_gain_grad: float32 [3, 768], P(None, 'shard')
- norm_shift_grad: float32 [3, 768], P(None, 'shard')
- attention_in_grad: float32 [2, 768, 3, 768], P(None, 'shard', None, 'tensor')
- attention_bias_grad: float32 [2, 2, 12, 64], P(None, None, 'tensor', 'shard')
- attention_out_grad: float32 [2, 768, 768], P(None, 'tensor', 'shard')
- branch_bias_grad: float32 [4, 768], P(None, 'shard')
- temporal_fc_grad: float32 [768, 768], P('shard')
- hidden_in_grad: float32 [768, 3072], P('shard', 'tensor')
- hidden_bias_grad: float32 [24, 128], P('tensor', 'shard')
- hidden_out_grad: float32 [3072, 768], P('tensor', 'shard')
The draws below stay inside these ranges and needn't reach their ends.
Inputs may be any that keep to these rules, and one draw needn't show every extreme that they name: `clip_slot`: in micro-batch 0 every slot holds a clip; in every later micro-batch exactly 1 of the 2 slots do, which ones drawn from the seed.
All inputs are finite; a program needn't handle non-finite values.
Results may differ from the reference program's by a relative error of at most 0.03.
Values may be sent and summed in bfloat16 or wider, within the bound.
No kernel may reach another device: no remote copies, remote signals or barrier semaphores. Data moves between devices by JAX's collectives and lax.ppermute only.
A program may use at most 128 MiB of HBM per device.

```python
import jax
import jax.numpy as jnp
from jax import lax

D = 768
HEADS = 12
HEAD_DIM = 64
FF = 3072
FRAMES = 8
PLACES = 196
MB = 4
CLIPS = 2
LIVE = 1


def draw_clip_slot(key, part):
    key = jax.random.fold_in(key, 11)
    orders = jax.vmap(lambda single: jax.random.permutation(single, CLIPS))(jax.random.split(key, MB))
    counts = jnp.where(jnp.arange(MB) == 0, CLIPS, LIVE)
    return (orders < counts[:, None]).astype(jnp.int32)


def shard_levels(stream_key, dims, cuts, smallest, top_value):
    level, own = 1.0, jax.random.fold_in(stream_key, 6)
    for position, blocks in cuts:
        draws = jnp.exp(jax.random.uniform(jax.random.fold_in(own, position), (blocks,), jnp.float32, smallest / len(cuts), top_value / len(cuts)))
        level = level * jnp.repeat(draws, dims[position] // blocks).reshape([-1 if axis == position else 1 for axis in range(len(dims))])
    return level


def scatter_about(key, shape, scale, reach, pieces=(), kind=jnp.bfloat16):
    values = jax.random.normal(key, shape, jnp.float32) * scale
    if len(pieces) > 0:
        values = shard_levels(key, shape, pieces, -0.22, 0.18) * values
    return jnp.clip(values, min=-reach, max=reach).astype(kind)


def setup_inputs(seed: int = 0) -> dict:
    key_of = jax.random.split(jax.random.key(seed), 14)
    clip_input = scatter_about(key_of[0], (MB, CLIPS, FRAMES, PLACES, D), 1.0, 6.0, ((1, 2), (2, 4), (3, 4)))
    clip_slot = draw_clip_slot(jax.random.fold_in(key_of[13], 71), 0)
    norm_gain = jnp.clip(1.0 + 0.15 * jax.random.normal(key_of[2], (3, D), jnp.float32), 0.25, 1.75).astype(jnp.bfloat16)
    norm_shift = scatter_about(key_of[3], (3, D), 0.3, 2.0, ((1, 2),))
    attention_in = scatter_about(key_of[4], (2, D, 3, D), D ** -0.5, 0.21875, ((1, 2), (3, 4)))
    attention_bias = scatter_about(key_of[5], (2, 2, HEADS, HEAD_DIM), 0.3, 2.0, ((2, 4), (3, 2)))
    attention_out = scatter_about(key_of[6], (2, D, D), (D // 8) ** -0.5, 0.625, ((1, 4), (2, 2)))
    branch_bias = scatter_about(key_of[7], (4, D), 0.3, 2.0, ((1, 2),))
    temporal_fc = scatter_about(key_of[8], (D, D), D ** -0.5, 0.21875, ((0, 2),))
    hidden_in = scatter_about(key_of[9], (D, FF), D ** -0.5, 0.21875, ((0, 2), (1, 4)))
    hidden_bias = scatter_about(key_of[10], (FF // 128, 128), 0.3, 2.0, ((0, 4), (1, 2)))
    hidden_out = scatter_about(key_of[11], (FF, D), FF ** -0.5, 0.109375, ((0, 4), (1, 2)))
    output_grad = scatter_about(key_of[12], (MB, CLIPS, FRAMES, PLACES, D), 1.0, 6.0, ((1, 2), (2, 4), (3, 4)))
    return dict(clip_input=clip_input, clip_slot=clip_slot, norm_gain=norm_gain, norm_shift=norm_shift, attention_in=attention_in, attention_bias=attention_bias, attention_out=attention_out, branch_bias=branch_bias, temporal_fc=temporal_fc, hidden_in=hidden_in, hidden_bias=hidden_bias, hidden_out=hidden_out, output_grad=output_grad)


@jax.custom_vjp
def low(v):
    return lax.optimization_barrier(v.astype(jnp.bfloat16)).astype(jnp.float32)

@jax.custom_vjp
def low_back(v):
    return v

def low_keep(v):
    return (low(v), None)

def low_pass(kept, grad):
    return (grad,)

def back_keep(v):
    return (v, None)

def back_low(kept, grad):
    return (low(grad),)
low.defvjp(low_keep, low_pass)
low_back.defvjp(back_keep, back_low)
EPS = 1e-06
HIGH = lax.Precision.HIGHEST
TEMPORAL = ('iphd,jphd->phij', 'phij,jphd->iphd')
SPATIAL = ('fqhd,fkhd->fhqk', 'fhqk,fkhd->fqhd')

def layer_norm(values, gain, shift):
    centred = values - lax.optimization_barrier(jnp.mean(values, -1, keepdims=True))
    spread = lax.optimization_barrier(jnp.mean(centred * centred, -1, keepdims=True))
    return centred * lax.rsqrt(spread + EPS) * gain + shift

def project(normed, weight, pair):
    shift = jnp.stack([pair[0], jnp.zeros_like(pair[0]), pair[1]])
    mixed = jnp.einsum('fpd,dcw->fpcw', normed, weight, precision=HIGH) + shift
    return low(low_back(mixed))

def attention(query, key, value, forms):
    scores = low_back(jnp.einsum(forms[0], query, key, precision=HIGH) * HEAD_DIM ** (-0.5))
    probs = low(jax.nn.softmax(scores, axis=-1))
    return low(low_back(jnp.einsum(forms[1], probs, value, precision=HIGH)))

def layer(params, clip, live):
    gains, shifts, qkv_w, qv_bias, proj_w, branch, fc_w, up_w, up_bias, down_w = params
    frames, places, width = clip.shape
    pairs = qv_bias.reshape(2, 2, width)
    normed = low(layer_norm(clip, gains[0], shifts[0]))
    qkv = project(normed, qkv_w[0], pairs[0]).reshape(frames, places, 3, HEADS, HEAD_DIM)
    mixed = attention(qkv[:, :, 0], qkv[:, :, 1], qkv[:, :, 2], TEMPORAL).reshape(frames, places, width)
    temporal = low(low_back(jnp.einsum('fpk,kd->fpd', mixed, proj_w[0], precision=HIGH) + branch[0]))
    after_a = clip + low_back(jnp.einsum('fpk,kd->fpd', temporal, fc_w, precision=HIGH) + branch[1])
    normed = low(layer_norm(after_a, gains[1], shifts[1]))
    qkv = project(normed, qkv_w[1], pairs[1]).reshape(frames, places, 3, HEADS, HEAD_DIM)
    mixed = attention(qkv[:, :, 0], qkv[:, :, 1], qkv[:, :, 2], SPATIAL).reshape(frames, places, width)
    after_b = after_a + low_back(jnp.einsum('fpk,kd->fpd', mixed, proj_w[1], precision=HIGH) + branch[2])
    normed = low(layer_norm(after_b, gains[2], shifts[2]))
    hidden = low_back(jnp.einsum('fpd,dk->fpk', normed, up_w, precision=HIGH) + up_bias.reshape(-1))
    active = low(jax.nn.gelu(hidden, approximate=False))
    result = after_b + low_back(jnp.einsum('fpk,kd->fpd', active, down_w, precision=HIGH) + branch[3])
    return live * result

def reference(clip_input, clip_slot, norm_gain, norm_shift, attention_in, attention_bias, attention_out, branch_bias, temporal_fc, hidden_in, hidden_bias, hidden_out, output_grad):
    params = tuple((item.astype(jnp.float32) for item in (norm_gain, norm_shift, attention_in, attention_bias, attention_out, branch_bias, temporal_fc, hidden_in, hidden_bias, hidden_out)))
    total_clips = MB * CLIPS
    clips = clip_input.reshape(total_clips, FRAMES, PLACES, D).astype(jnp.float32)
    lives = clip_slot.reshape(total_clips).astype(jnp.float32)
    cotangents = output_grad.reshape(total_clips, FRAMES, PLACES, D).astype(jnp.float32)

    def step(totals, batch):
        clip, live, cotangent = batch
        result, pull = jax.vjp(lambda weights, values: layer(weights, values, live), params, clip)
        weight_grads, clip_grad = pull(cotangent)
        totals = jax.tree.map(jnp.add, totals, weight_grads)
        return (totals, (result.astype(jnp.bfloat16), clip_grad.astype(jnp.bfloat16)))
    zeros = jax.tree.map(jnp.zeros_like, params)
    totals, (results, clip_grads) = lax.scan(step, zeros, (clips, lives, cotangents))
    shape = clip_input.shape
    return (results.reshape(shape), clip_grads.reshape(shape), totals[0], totals[1], totals[2], totals[3], totals[4], totals[5], totals[6], totals[7], totals[8], totals[9])
```

```python
import jax
import jax.numpy as jnp
from jax import lax
from jax.sharding import PartitionSpec as P

HEAD_DIM = 64
EPS = 1e-06
SQRT_HALF = 0.7071067811865476
INV_ROOT_TAU = 0.3989422804014327
LOW = jnp.bfloat16
F32 = jnp.float32


def dot(form, first, second):
    return jnp.einsum(form, first, second, preferred_element_type=F32)


def hop(values, axis, step):
    count = lax.axis_size(axis)
    return lax.ppermute(values, axis, [(i, i ^ step) for i in range(count)])


def pick(values, index, axis=0):
    return lax.dynamic_index_in_dim(values, index, axis, keepdims=False)


def ordered(parts, me, axis=0):
    shape = list(parts[0].shape)
    shape.insert(axis, len(parts))
    out = jnp.zeros(shape, parts[0].dtype)
    for j, part in enumerate(parts):
        out = lax.dynamic_update_index_in_dim(out, part, me ^ j, axis)
    return out


def swap_halves(values):
    half = values.shape[-1] // 2
    return jnp.concatenate([values[..., half:], values[..., :half]], -1)


class Place:
    def __init__(self):
        self.shard = lax.axis_index("shard")
        self.context = lax.axis_index("context")
        self.tensor = lax.axis_index("tensor")
        self.paired = lax.axis_size("shard") == 2

    def relative(self, values):
        if not self.paired:
            return values
        return jnp.where(self.shard == 0, values, swap_halves(values))

    def beside(self, values):
        return swap_halves(hop(values, "shard", 1))


def gather_columns(place, part):
    if place.paired:
        return jnp.concatenate([part, hop(part, "shard", 1)], -1)
    return lax.all_gather(part, "shard", axis=part.ndim - 1, tiled=True)


def scatter_columns(place, total):
    if place.paired:
        half = total.shape[-1] // 2
        mine = total[..., :half].astype(F32) + hop(total[..., half:], "shard", 1).astype(F32)
        return mine.astype(LOW)
    return lax.psum_scatter(total, "shard", scatter_dimension=total.ndim - 1, tiled=True)


def gather_blocks(place, block, short):
    def spread(mine):
        ranks = lax.axis_size("tensor")
        blocks = [mine] + [hop(mine, "tensor", k) for k in range(1, ranks)]
        return jnp.stack([gather_columns(place, item) for item in blocks])

    first = spread(pick(block, place.context))
    if short:
        second = spread(pick(block, place.context ^ 2))
    else:
        second = hop(first, "context", 2)
    return [first, hop(first, "context", 1), second, hop(second, "context", 1)]


def reduce_blocks(place, pieces, short):
    def add(*terms):
        total = terms[0].astype(F32)
        for term in terms[1:]:
            total = total + term.astype(F32)
        return total.astype(LOW)

    def collapse(total):
        mine = scatter_columns(place, total)
        return add(*[mine[0]] + [hop(mine[k], "tensor", k) for k in range(1, mine.shape[0])])

    first = add(pieces[0], hop(pieces[1], "context", 1))
    second = add(pieces[2], hop(pieces[3], "context", 1))
    if short:
        first, second = collapse(first), collapse(second)
        first, second = add(first, hop(second, "context", 2)), add(second, hop(first, "context", 2))
    else:
        first = collapse(add(first, hop(second, "context", 2)))
        second = hop(first, "context", 2)
    parts = [first, hop(first, "context", 1), second, hop(second, "context", 1)]
    return ordered(parts, place.context).astype(F32)


def unit_of(values):
    centred = values - jnp.mean(values, -1, keepdims=True)
    inverse = lax.rsqrt(jnp.mean(centred * centred, -1, keepdims=True) + EPS)
    return (centred * inverse, inverse)


def norm_back(grad, unit, inverse, gain):
    scaled = grad * gain
    inner = (
        scaled
        - jnp.mean(scaled, -1, keepdims=True)
        - unit * jnp.mean(scaled * unit, -1, keepdims=True)
    )
    return (inverse * inner, jnp.sum(grad * unit, 0), jnp.sum(grad, 0))


def gelu_both(values):
    half = 0.5 * (1.0 + lax.erf(values * SQRT_HALF))
    return (values * half, half + values * jnp.exp(-0.5 * values * values) * INV_ROOT_TAU)


def attend(query, key, value, allowed):
    scores = dot("bqd,bkd->bqk", query, key) * HEAD_DIM ** (-0.5)
    if allowed is not None:
        scores = jnp.where(allowed, scores, -jnp.inf)
    weights = jnp.exp(scores - jnp.max(scores, -1, keepdims=True))
    probs = weights / jnp.sum(weights, -1, keepdims=True)
    mixed = dot("bqk,bkd->bqd", probs.astype(LOW), value)
    return (mixed.astype(LOW), probs)


def attend_back(query, key, value, probs, grad):
    value_grad = dot("bqk,bqd->bkd", probs.astype(LOW), grad)
    prob_grad = dot("bqd,bkd->bqk", grad, value)
    inner = jnp.sum(probs * prob_grad, -1, keepdims=True)
    score_grad = (probs * (prob_grad - inner)).astype(LOW)
    scale = HEAD_DIM ** (-0.5)
    query_grad = dot("bqk,bkd->bqd", score_grad, key) * scale
    key_grad = dot("bqk,bqd->bkd", score_grad, query) * scale
    return (query_grad.astype(LOW), key_grad.astype(LOW), value_grad.astype(LOW))


class Tokens:
    def __init__(self, place, clips, live):
        self.place = place
        self.batches, self.frames, self.places = clips.shape[:3]
        self.ranks = lax.axis_size("tensor")
        self.whole = 1 if place.paired else self.batches
        self.split = self.batches - self.whole
        self.live = live
        self.room_whole = -(-self.whole * self.places // self.ranks)
        self.room_split = -(-self.split * self.places // (2 * self.ranks))
        self.room = self.room_whole + self.room_split
        if self.split:
            self.mine = live[self.whole :] > 0
            flat = jnp.repeat(self.mine, self.places)
            flat = jnp.pad(flat, (0, 2 * self.ranks * self.room_split - flat.shape[0]))
            self.mine_flat = pick(flat.reshape(2, -1), place.shard)

    def frame_rows(self, clips):
        place = self.place
        width = clips.shape[-1]
        rows = clips[: self.whole].reshape(-1, self.places, width)
        if self.split:
            later = clips[self.whole :]
            other = hop(pick(later, 1 - place.shard, 1), "shard", 1)
            chosen = jnp.where(self.mine[:, None, None], pick(later, place.shard, 1), other)
            rows = jnp.concatenate([rows, chosen])
        return place.relative(rows)

    def natural_rows(self, rows):
        place = self.place
        rows = place.relative(rows)
        first = self.whole * self.frames
        width = rows.shape[-1]
        out = rows[:first].reshape(self.whole, self.frames, self.places, width)
        if self.split:
            mine = rows[first:]
            other = hop(mine, "shard", 1)
            zero = jnp.zeros((), rows.dtype)
            pair = jnp.where(
                place.shard == 0, jnp.stack([mine, other], 1), jnp.stack([other, mine], 1)
            )
            out = jnp.concatenate([out, jnp.where(self.mine[:, None, None, None], pair, zero)])
        return out

    def scatter_places(self, whole, split):
        width = whole.shape[-1]
        frames, ranks = self.frames, self.ranks
        whole = jnp.pad(whole, ((0, 0), (0, ranks * self.room_whole - whole.shape[1]), (0, 0)))
        rows = whole.reshape(frames, ranks, self.room_whole, width)
        if self.split:
            split = split.reshape(frames, ranks, self.room_split, width)
            rows = jnp.concatenate([rows, split], 2)
        me = self.place.tensor
        return jnp.stack(
            [pick(rows, me, 1)]
            + [hop(pick(rows, me ^ k, 1), "tensor", k) for k in range(1, ranks)]
        )

    def gather_places(self, rows):
        width = rows.shape[-1]
        parts = [rows[0]] + [hop(rows[k], "tensor", k) for k in range(1, self.ranks)]
        rows = ordered(parts, self.place.tensor, 1)
        whole = rows[:, :, : self.room_whole].reshape(self.frames, -1, width)
        whole = whole[:, : self.whole * self.places]
        split = rows[:, :, self.room_whole :].reshape(self.frames, -1, width)
        return (whole, split)

    def natural_to_places(self, clips):
        width = clips.shape[-1]
        place = self.place

        def flat(part, room):
            part = jnp.swapaxes(part, 0, 1).reshape(self.frames, -1, width)
            return jnp.pad(part, ((0, 0), (0, room - part.shape[1]), (0, 0)))

        whole = flat(clips[: self.whole], self.whole * self.places)
        split = None
        if self.split:
            later = flat(clips[self.whole :], 2 * self.ranks * self.room_split)
            later = later.reshape(self.frames, 2, -1, width)
            other = hop(pick(later, 1 - place.shard, 1), "shard", 1)
            split = jnp.where(self.mine_flat[:, None], pick(later, place.shard, 1), other)
        return place.relative(self.scatter_places(whole, split))

    def frames_to_places(self, rows):
        place = self.place
        width = rows.shape[-1]
        first = self.whole * self.frames
        whole = rows[:first].reshape(self.whole, self.frames, self.places, width)
        whole = jnp.swapaxes(whole, 0, 1).reshape(self.frames, -1, width)
        split = None
        if self.split:
            flat = rows[first:].reshape(-1, width)
            flat = jnp.pad(flat, ((0, 2 * self.ranks * self.room_split - flat.shape[0]), (0, 0)))
            flat = flat.reshape(2, -1, width)
            mine = pick(flat, place.shard)
            other = place.beside(pick(flat, 1 - place.shard))
            split = jnp.where(
                place.shard == 0, jnp.stack([mine, other]), jnp.stack([other, mine])
            )
        return self.scatter_places(whole, split)

    def places_to_frames(self, rows):
        place = self.place
        width = rows.shape[-1]
        whole, split = self.gather_places(rows)
        whole = jnp.swapaxes(whole.reshape(self.frames, self.whole, self.places, width), 0, 1)
        out = whole.reshape(-1, self.places, width)
        if self.split:
            mine = pick(split, place.shard)
            other = place.beside(pick(split, 1 - place.shard))
            flat = jnp.where(
                place.shard == 0, jnp.concatenate([mine, other]), jnp.concatenate([other, mine])
            )
            flat = flat[: self.split * self.places].reshape(self.split, self.places, width)
            out = jnp.concatenate([out, flat])
        return out


def body(
    clip_input,
    clip_slot,
    norm_gain,
    norm_shift,
    attention_in,
    attention_bias,
    attention_out,
    branch_bias,
    temporal_fc,
    hidden_in,
    hidden_bias,
    hidden_out,
    output_grad,
):
    place = Place()
    shards, quarters, ranks = (lax.axis_size(name) for name in ("shard", "context", "tensor"))
    clips, cotangents, live = clip_input[:, 0], output_grad[:, 0], clip_slot[:, 0]
    tokens = Tokens(place, clips, live)
    columns = attention_in.shape[1]
    width = columns * shards
    group = attention_in.shape[3]
    heads = group // HEAD_DIM
    hidden = hidden_in.shape[1]
    context = place.context

    def in_block(weight):
        block = jnp.transpose(weight, (1, 2, 0)).reshape(3, quarters, group // quarters, columns)
        return jnp.swapaxes(block, 0, 1)

    def quartered(block):
        return block.reshape(quarters, -1, block.shape[-1])

    vectors = jnp.concatenate(
        [norm_gain, norm_shift, branch_bias, attention_bias.reshape(-1, columns)]
        + [hidden_bias.reshape(-1, columns)]
    )
    vectors = lax.all_gather(lax.all_gather(vectors, "tensor"), "shard")
    rows = vectors[:, place.tensor].astype(F32)
    along = jnp.swapaxes(rows[:, :10], 0, 1).reshape(10, width)
    along = place.relative(along)
    gains, shifts, branch = along[:3], along[3:6], along[6:10]
    hops = place.tensor ^ jnp.arange(ranks)
    own = jnp.take(vectors, hops, axis=1).astype(F32)
    last = 10 + attention_bias.size // columns
    pairs = own[:, :, 10:last].reshape((shards, ranks) + attention_bias.shape)
    pairs = jnp.transpose(pairs, (2, 3, 1, 4, 0, 5)).reshape(2, 2, ranks, group)
    up_shift = own[:, :, last:].reshape((shards, ranks) + hidden_bias.shape)
    up_shift = jnp.transpose(up_shift, (1, 2, 0, 3)).reshape(ranks, quarters, -1)

    def assemble_in(pieces):
        whole = ordered(pieces, context, 2)
        return whole.reshape(ranks, 3 * group, width)

    def assemble_out(pieces):
        return ordered(pieces, context, 1).reshape(ranks, group, width)

    in_a = assemble_in(gather_blocks(place, in_block(attention_in[0]), False))
    out_a = assemble_out(gather_blocks(place, quartered(attention_out[0]), False))
    fc_rows = gather_columns(place, temporal_fc.T).T
    fc = place.relative(fc_rows)
    in_b = assemble_in(gather_blocks(place, in_block(attention_in[1]), False))
    out_b = assemble_out(gather_blocks(place, quartered(attention_out[1]), False))
    up = gather_blocks(place, quartered(hidden_in.T), False)
    down = gather_blocks(place, quartered(hidden_out), True)
    up = [item.reshape(-1, width) for item in up]
    down = [item.reshape(-1, width) for item in down]
    up_bias = [pick(up_shift, context ^ j, 1).reshape(-1) for j in range(quarters)]

    def project(normed, weight, pair):
        shift = jnp.stack([pair[0], jnp.zeros_like(pair[0]), pair[1]], 1).reshape(ranks, 1, -1)
        return (dot("td,knd->ktn", normed, weight) + shift).astype(LOW)

    start_p = tokens.natural_to_places(clips).astype(F32).reshape(-1, width)
    start = tokens.frame_rows(clips)
    units, places = start.shape[:2]
    start = start.astype(F32).reshape(-1, width)
    grad = tokens.frame_rows(cotangents * live[:, None, None, None].astype(LOW))
    grad = grad.reshape(-1, width)
    unit_a, inverse_a = unit_of(start_p)
    normed_a = (unit_a * gains[0] + shifts[0]).astype(LOW)
    count_p = start_p.shape[0]
    qkv_a = project(normed_a, in_a, pairs[0]).reshape(ranks, count_p, 3, heads, HEAD_DIM)
    qkv_a = jnp.transpose(qkv_a, (2, 0, 3, 1, 4)).reshape(3, ranks * heads, count_p, HEAD_DIM)
    spot = jnp.arange(count_p) % tokens.room
    allowed = spot[:, None] == spot[None]
    mixed_a, probs_a = attend(qkv_a[0], qkv_a[1], qkv_a[2], allowed)

    def side_by_side(values):
        values = values.reshape(ranks, heads, values.shape[1], HEAD_DIM)
        return jnp.swapaxes(values, 1, 2).reshape(ranks, values.shape[2], group)

    flat_a = side_by_side(mixed_a)
    temporal_p = (dot("ktn,knd->td", flat_a, out_a) + branch[0]).astype(LOW)
    temporal = tokens.places_to_frames(temporal_p.reshape(ranks, tokens.frames, -1, width))
    temporal = temporal.reshape(-1, width)
    after_a = start + dot("tk,kd->td", temporal, fc) + branch[1]

    unit_b, inverse_b = unit_of(after_a)
    normed_b = (unit_b * gains[1] + shifts[1]).astype(LOW)
    qkv_b = project(normed_b, in_b, pairs[1])

    def to_groups(values):
        return [pick(values, context)] + [
            hop(pick(values, context ^ j), "context", j) for j in range(1, quarters)
        ]

    def from_groups(parts):
        parts = [parts[0]] + [hop(parts[j], "context", j) for j in range(1, quarters)]
        return ordered(parts, context)

    def frame_heads(parts, kinds):
        values = jnp.stack(parts).reshape(quarters, units, places, kinds, heads, HEAD_DIM)
        values = jnp.transpose(values, (3, 1, 4, 0, 2, 5))
        return values.reshape(kinds, units * heads, quarters * places, HEAD_DIM)

    def frame_rows(values, kinds):
        values = values.reshape(kinds, units, heads, quarters, places, HEAD_DIM)
        values = jnp.transpose(values, (3, 1, 4, 0, 2, 5))
        return values.reshape(quarters, units * places, kinds * group)

    q_b, k_b, v_b = frame_heads(to_groups(qkv_b), 3)
    mixed_b, probs_b = attend(q_b, k_b, v_b, None)
    flat_b = from_groups(frame_rows(mixed_b[None], 1))
    after_b = after_a + dot("ktn,knd->td", flat_b, out_b) + branch[2]

    unit_c, inverse_c = unit_of(after_b)
    normed_c = (unit_c * gains[2] + shifts[2]).astype(LOW)
    result = after_b + branch[3]
    back = jnp.zeros_like(result)
    down_grad, up_grad, up_bias_grad = [], [], []
    for j in range(quarters):
        hidden_c = dot("td,kd->tk", normed_c, up[j]) + up_bias[j]
        active, slope = gelu_both(hidden_c)
        active = active.astype(LOW)
        result = result + dot("tk,kd->td", active, down[j])
        down_grad.append(dot("tk,td->kd", active, grad).astype(LOW).reshape(ranks, -1, width))
        hidden_grad = (dot("td,kd->tk", grad, down[j]) * slope).astype(LOW)
        up_grad.append(
            dot("tk,td->kd", hidden_grad, normed_c).astype(LOW).reshape(ranks, -1, width)
        )
        up_bias_grad.append(jnp.sum(hidden_grad.astype(F32), 0))
        back = back + dot("tk,kd->td", hidden_grad, up[j])
    layer_rows = result.astype(LOW).reshape(units, places, width)
    layer_out = tokens.natural_rows(layer_rows)
    layer_out = layer_out * live[:, None, None, None].astype(LOW)
    down_total = reduce_blocks(place, down_grad, True)
    up_total = reduce_blocks(place, up_grad, False)

    branch_3 = jnp.sum(grad.astype(F32), 0)
    back, gain_c, shift_c = norm_back(back, unit_c, inverse_c, gains[2])
    grad = grad.astype(F32) + back

    low_b = grad.astype(LOW)
    branch_2 = jnp.sum(low_b.astype(F32), 0)
    mixed_grad_b = dot("td,knd->ktn", low_b, out_b).astype(LOW)
    out_grad_b = dot("ktn,td->knd", flat_b, low_b).astype(LOW)
    (mixed_grad_b,) = frame_heads(to_groups(mixed_grad_b), 1)
    qkv_grad_b = attend_back(q_b, k_b, v_b, probs_b, mixed_grad_b)
    qkv_grad_b = from_groups(frame_rows(jnp.stack(qkv_grad_b), 3))

    def split_quarters(values, axis):
        return [pick(values, context ^ j, axis) for j in range(quarters)]

    def reduce_out(total):
        parts = split_quarters(total.reshape(ranks, quarters, -1, width), 1)
        return reduce_blocks(place, parts, False).reshape(group, columns)

    def reduce_in(total):
        parts = split_quarters(total.reshape(ranks, 3, quarters, -1, width), 2)
        total = reduce_blocks(place, parts, False)
        return jnp.transpose(total, (3, 1, 0, 2)).reshape(columns, 3, group)

    in_grad_b = dot("ktn,td->knd", qkv_grad_b, normed_b).astype(LOW)
    pair_b = jnp.sum(qkv_grad_b.astype(F32), 1).reshape(ranks, 3, group)
    back, gain_b, shift_b = norm_back(
        dot("ktn,knd->td", qkv_grad_b, in_b), unit_b, inverse_b, gains[1]
    )
    grad = grad + back

    low_fc = grad.astype(LOW)
    branch_1 = jnp.sum(low_fc.astype(F32), 0)
    fc_grad = dot("tk,td->kd", temporal, low_fc)
    temporal_grad = dot("td,kd->tk", low_fc, fc).astype(LOW)
    branch_0 = jnp.sum(temporal_grad.astype(F32), 0)
    temporal_grad = tokens.frames_to_places(temporal_grad.reshape(units, places, width))
    temporal_grad = temporal_grad.reshape(-1, width)
    out_grad_a = dot("ktn,td->knd", flat_a, temporal_grad).astype(LOW)
    mixed_grad_a = dot("td,knd->ktn", temporal_grad, out_a).astype(LOW)
    mixed_grad_a = mixed_grad_a.reshape(ranks, count_p, heads, HEAD_DIM)
    mixed_grad_a = jnp.swapaxes(mixed_grad_a, 1, 2).reshape(-1, count_p, HEAD_DIM)
    qkv_grad_a = attend_back(qkv_a[0], qkv_a[1], qkv_a[2], probs_a, mixed_grad_a)
    qkv_grad_a = jnp.concatenate([side_by_side(item) for item in qkv_grad_a], -1)
    in_grad_a = dot("ktn,td->knd", qkv_grad_a, normed_a).astype(LOW)
    pair_a = jnp.sum(qkv_grad_a.astype(F32), 1).reshape(ranks, 3, group)
    back, gain_a, shift_a = norm_back(
        dot("ktn,knd->td", qkv_grad_a, in_a), unit_a, inverse_a, gains[0]
    )
    back = tokens.places_to_frames(
        back.astype(LOW).reshape(ranks, tokens.frames, -1, width)
    ).reshape(-1, width)
    input_rows = (grad + back.astype(F32)).astype(LOW).reshape(units, places, width)
    input_grad = tokens.natural_rows(input_rows)

    in_total = jnp.stack([reduce_in(in_grad_a), reduce_in(in_grad_b)])
    out_total = jnp.stack([reduce_out(out_grad_a), reduce_out(out_grad_b)])
    fc_grad = place.relative(fc_grad).astype(LOW)
    fc_total = lax.psum(scatter_columns(place, fc_grad.T).T, ("context", "tensor")).astype(F32)

    along = jnp.stack(
        [gain_a, gain_b, gain_c, shift_a, shift_b, shift_c, branch_0, branch_1, branch_2, branch_3]
    )
    along = place.relative(along).reshape(-1)
    inner = jnp.stack([pair_a, pair_b])[:, :, ::2]
    inner = ordered([inner[:, k] for k in range(ranks)], place.tensor).reshape(-1)
    outer = ordered([item.reshape(ranks, -1) for item in up_bias_grad], context, 1)
    outer = ordered([outer[k] for k in range(ranks)], place.tensor).reshape(-1)
    sums = lax.psum(jnp.concatenate([along, inner, outer]), ("shard", "context", "tensor"))
    along, inner, outer = jnp.split(sums, [along.size, along.size + inner.size])
    along = lax.dynamic_slice_in_dim(along.reshape(10, width), place.shard * columns, columns, 1)
    inner = pick(inner.reshape(ranks, 2, 2, heads, HEAD_DIM), place.tensor)
    piece = HEAD_DIM // shards
    inner = lax.dynamic_slice_in_dim(inner, place.shard * piece, piece, 3)
    outer = pick(outer.reshape(ranks, -1, shards, hidden_bias.shape[1]), place.tensor)
    outer = pick(outer, place.shard, 1)
    return (
        layer_out[:, None],
        input_grad[:, None],
        along[:3],
        along[3:6],
        in_total,
        inner,
        out_total,
        along[6:],
        fc_total,
        up_total.reshape(hidden, columns).T,
        outer,
        down_total.reshape(hidden, columns),
    )


def solution(mesh):
    rows = P(None, "shard", "tensor", "context", None)
    weights = (
        P(None, "shard"),
        P(None, "shard"),
        P(None, "shard", None, "tensor"),
        P(None, None, "tensor", "shard"),
        P(None, "tensor", "shard"),
        P(None, "shard"),
        P("shard", None),
        P("shard", "tensor"),
        P("tensor", "shard"),
        P("tensor", "shard"),
    )
    return jax.shard_map(
        body,
        mesh=mesh,
        in_specs=(rows, P(None, "shard")) + weights + (rows,),
        out_specs=(rows, rows) + weights,
        check_vma=False,
    )
```

```python
import jax
import jax.numpy as jnp
import numpy as np
from jax import lax
from jax.experimental import pallas as pl
from jax.experimental.pallas import tpu as pltpu
from jax.sharding import PartitionSpec as P

HEAD_DIM = 64
WINDOW = 64
EPS = 1e-06
SQRT_HALF = 0.7071067811865476
INV_ROOT_TAU = 0.3989422804014327
SCALE = HEAD_DIM**-0.5
HIDE = -1e30
LOW = jnp.bfloat16
F32 = jnp.float32
VMEM_BYTES = 60 * 2**20


def hop(values, axis, step):
    count = lax.axis_size(axis)
    return lax.ppermute(values, axis, [(i, i ^ step) for i in range(count)])


def hop_pair(values, step):
    ranks = lax.axis_size("tensor")
    pairs = [
        (a * ranks + i, (1 - a) * ranks + (i ^ step)) for a in range(2) for i in range(ranks)
    ]
    return lax.ppermute(values, ("shard", "tensor"), pairs)


def pick(values, index, axis=0):
    return lax.dynamic_index_in_dim(values, index, axis, keepdims=False)


def ordered(parts, me, axis=0):
    shape = list(parts[0].shape)
    shape.insert(axis, len(parts))
    out = jnp.zeros(shape, parts[0].dtype)
    for j, part in enumerate(parts):
        out = lax.dynamic_update_index_in_dim(out, part, me ^ j, axis)
    return out


def round_up(value, step):
    return -(-value // step) * step


class Place:
    def __init__(self):
        self.shard = lax.axis_index("shard")
        self.context = lax.axis_index("context")
        self.tensor = lax.axis_index("tensor")
        self.shards = lax.axis_size("shard")
        self.ranks = lax.axis_size("tensor")
        self.quarters = lax.axis_size("context")
        self.paired = self.shards == 2


def gather_columns(place, part):
    if place.paired:
        return jnp.concatenate([part, hop(part, "shard", 1)], -1)
    return lax.all_gather(part, "shard", axis=part.ndim - 1, tiled=True)


def gather_blocks(place, mine, axis=0):
    blocks = [mine] + [hop(mine, "tensor", k) for k in range(1, place.ranks)]
    first = gather_columns(place, jnp.stack(blocks, axis))
    second = hop(first, "context", 2)
    return [first, hop(first, "context", 1), second, hop(second, "context", 1)]


def add(*terms):
    total = terms[0].astype(F32)
    for term in terms[1:]:
        total = total + term.astype(F32)
    return total.astype(LOW)


def reduce_blocks(place, pieces, axis=0):
    first = add(pieces[0], hop(pieces[1], "context", 1))
    second = add(pieces[2], hop(pieces[3], "context", 1))
    total = add(first, hop(second, "context", 2))
    if place.paired:
        half = total.shape[-1] // 2
        mine = add(total[..., :half], hop(total[..., half:], "shard", 1))
    else:
        mine = lax.psum_scatter(total, "shard", scatter_dimension=total.ndim - 1, tiled=True)
    block = lambda k: lax.index_in_dim(mine, k, axis, keepdims=False)
    first = add(block(0), *[hop(block(k), "tensor", k) for k in range(1, place.ranks)])
    second = hop(first, "context", 2)
    parts = [first, hop(first, "context", 1), second, hop(second, "context", 1)]
    return ordered(parts, place.context).astype(F32)


class Layout:
    def __init__(self, place, clips, live):
        self.place = place
        self.batches, self.frames, self.places = clips.shape[:3]
        ranks = place.ranks
        self.whole = 1 if place.paired else self.batches
        self.split = self.batches - self.whole
        self.alive = live > 0
        self.first = -(-self.whole * self.places // ranks)
        self.later = -(-self.split * self.places // (2 * ranks))
        self.room = max(32, round_up(self.first + self.later, 16))
        self.block = self.frames * self.room
        self.place_rows = ranks * self.block
        self.units = self.whole * self.frames + self.split
        self.frame_rows = round_up(self.units * self.places, 16)
        self.natural_blocks = self.batches * self.frames
        self.sent = round_up(self.frames * self.first + self.later, 16)
        self.sent_pair = round_up(self.later, 16)

    def label(self, batch, frame, spot):
        return (batch * self.frames * self.place.ranks + frame) * self.places + spot

    def place_labels(self, shard, tensor, k):
        frame = self.frames * (tensor ^ k) + jnp.arange(self.frames)[:, None]
        slot = jnp.arange(self.room)[None]
        spot = self.first * tensor + slot
        whole = slot < self.first
        labels = self.label(spot // self.places, frame, spot % self.places)
        labels = jnp.where(whole & (spot < self.whole * self.places), labels, -1)
        if self.split:
            flat = self.later * (self.place.ranks * shard + tensor) + slot - self.first
            inside = (slot >= self.first) & (slot < self.first + self.later)
            inside = inside & (flat < self.split * self.places)
            other = self.label(self.whole + flat // self.places, frame, flat % self.places)
            labels = jnp.where(inside, other, labels)
        return labels, jnp.broadcast_to(whole, labels.shape)

    def frame_labels(self, shard, tensor):
        row = jnp.arange(self.frame_rows)
        unit, spot = row // self.places, row % self.places
        whole = unit < self.whole * self.frames
        labels = self.label(
            unit // self.frames, self.frames * tensor + unit % self.frames, spot
        )
        later = self.label(
            self.whole + unit - self.whole * self.frames, self.frames * tensor + shard, spot
        )
        labels = jnp.where(whole, labels, later)
        return jnp.where(unit < self.units, labels, -1), whole

    def natural_labels(self, tensor):
        batch = jnp.arange(self.batches)[:, None, None]
        frame = self.frames * tensor + jnp.arange(self.frames)[None, :, None]
        spot = jnp.arange(WINDOW)[None, None]
        return jnp.where(spot < self.places, self.label(batch, frame, spot), -1)

    def held(self, labels):
        batch = jnp.maximum(labels, 0) // (self.frames * self.place.ranks * self.places)
        return self.living(labels) | (batch < self.whole)

    def living(self, labels):
        batch = jnp.maximum(labels, 0) // (self.frames * self.place.ranks * self.places)
        return jnp.any((batch[..., None] == jnp.arange(self.batches)) & self.alive, -1)


def one_hot(targets, sources):
    targets = jnp.concatenate([item.reshape(-1) for item in targets])
    sources = jnp.concatenate([item.reshape(-1) for item in sources])
    sources = jnp.where(sources < 0, -2, sources)
    return (targets[:, None] == sources[None]).astype(LOW)


def call(body, outs, ins, scalars, flops=0, scratch=()):
    moved = sum(item.size * item.dtype.itemsize for item in list(outs) + list(ins))
    spec = pl.BlockSpec(memory_space=pltpu.VMEM)
    return pl.pallas_call(
        body,
        out_shape=tuple(outs),
        in_specs=[pl.BlockSpec(memory_space=pltpu.SMEM)] + [spec] * len(ins),
        out_specs=(spec,) * len(outs),
        scratch_shapes=list(scratch),
        compiler_params=pltpu.CompilerParams(vmem_limit_bytes=VMEM_BYTES),
        cost_estimate=pl.CostEstimate(flops=flops, bytes_accessed=moved, transcendentals=0),
    )(scalars, *ins)


def shape(*dims, dtype=LOW):
    return jax.ShapeDtypeStruct(dims, dtype)


def nn(first, second):
    return lax.dot_general(first, second, (((1,), (0,)), ((), ())), preferred_element_type=F32)


def nt(first, second):
    return lax.dot_general(first, second, (((1,), (1,)), ((), ())), preferred_element_type=F32)


def tn(first, second):
    return lax.dot_general(first, second, (((0,), (0,)), ((), ())), preferred_element_type=F32)


def swapper(scalars, paired):
    def swap(values):
        if not paired:
            return values
        half = values.shape[-1] // 2
        other = jnp.concatenate([values[:, half:], values[:, :half]], -1)
        return jnp.where(scalars[0] == 0, values, other)

    return swap


def unit_of(values):
    centred = values - jnp.mean(values, -1, keepdims=True)
    inverse = lax.rsqrt(jnp.mean(centred * centred, -1, keepdims=True) + EPS)
    return (centred * inverse, inverse)


def norm_back(grad, unit, inverse, gain):
    scaled = grad * gain
    inner = (
        scaled
        - jnp.mean(scaled, -1, keepdims=True)
        - unit * jnp.mean(scaled * unit, -1, keepdims=True)
    )
    return (
        inverse * inner,
        jnp.sum(grad * unit, 0, keepdims=True),
        jnp.sum(grad, 0, keepdims=True),
    )


def softmax(scores):
    weights = jnp.exp(scores - jnp.max(scores, -1, keepdims=True))
    return weights / jnp.sum(weights, -1, keepdims=True)


def score_back(probs, prob_grad):
    inner = jnp.sum(probs * prob_grad, -1, keepdims=True)
    return (probs * (prob_grad - inner)).astype(LOW)


def half_lanes(width):
    lane = lax.broadcasted_iota(jnp.int32, (1, width), 1)
    return [(lane // HEAD_DIM == e).astype(F32) for e in range(2)]


def column_sum(values):
    return jnp.sum(values.astype(F32), 0, keepdims=True)


def rows_at(start, size):
    return pl.ds(pl.multiple_of(start, 16), size)


class Program:
    def __init__(self, place, layout, width, group, scalars):
        self.place, self.layout, self.width, self.group = place, layout, width, group
        self.scalars = scalars
        self.ranks, self.quarters = place.ranks, place.quarters
        self.piece = group // self.quarters
        self.heads = group // HEAD_DIM
        self.all_heads = group * self.ranks
        spot = np.arange(layout.place_rows) % layout.room
        self.same_place = jnp.asarray(
            np.where(spot[:, None] == spot[None], 0, HIDE).astype(np.float32)
        )

    def call(self, body, outs, ins, flops=0, scratch=()):
        return call(body, outs, ins, self.scalars, flops, scratch)


    def send_rows(self, clips, cotangents, matrix, targets):
        lay, width = self.layout, self.width
        count, split = lay.natural_blocks, lay.split
        first = lay.whole * lay.frames

        def body(scalars, clips_ref, grads_ref, matrix_ref, *refs):
            sent, refs = refs[:targets], refs[targets:]
            rows = refs[-1]
            rows[...] = jnp.zeros_like(rows)
            for item in range(count):
                rows[item * WINDOW : item * WINDOW + lay.places] = clips_ref[item]
            for item in range(targets):
                part = matrix_ref[item * lay.block : (item + 1) * lay.block]
                sent[item][...] = nn(part, rows[...]).astype(LOW)
            for index, source in enumerate((clips_ref, grads_ref) if split else ()):
                for item in range(split):
                    frame = first + lay.frames * item + 1 - scalars[0]
                    refs[index][item] = source[frame]

        outs = [shape(lay.block, width)] * targets
        if split:
            outs += [shape(split, lay.places, width)] * 2
        return self.call(
            body, outs, [clips, cotangents, matrix], scratch=[pltpu.VMEM((count * WINDOW, width), LOW)]
        )

    def frames_of(self, clips, others, matrix):
        lay, width = self.layout, self.width
        count, split = lay.natural_blocks, lay.split

        def body(scalars, clips_ref, *refs):
            matrix_ref, out_ref, rows = refs[-3:]
            rows[...] = jnp.zeros_like(rows)
            for item in range(count):
                rows[item * WINDOW : item * WINDOW + lay.places] = clips_ref[item]
            for item in range(split):
                start = (count + item) * WINDOW
                rows[start : start + lay.places] = refs[0][item]
            out_ref[...] = nn(matrix_ref[...], rows[...]).astype(LOW)

        return self.call(
            body,
            [shape(lay.frame_rows, width)],
            [clips] + ([others] if split else []) + [matrix],
            scratch=[pltpu.VMEM(((count + split) * WINDOW, width), LOW)],
        )[0]


    def temporal(self, blocks, pairs, keep, pieces, along, shift):
        lay, width = self.layout, self.width
        rows, ranks = lay.place_rows, self.ranks
        wide = 3 * self.all_heads
        split = lay.split > 0

        def body(scalars, *refs):
            refs = list(refs)
            take = lambda n: [refs.pop(0) for _ in range(n)]
            block_refs, pair_refs = take(ranks), take(ranks if split else 0)
            keep_ref, piece_refs, along_ref, shift_ref, same = (
                take(1)[0], take(self.quarters), take(1)[0], take(1)[0], take(1)[0],
            )
            sent, sent_pair = take(ranks), take(ranks if split else 0)
            normed_ref, rows_ref, qkv, mixed, win, wout = take(6)
            swap = swapper(scalars, self.place.paired)
            for j in range(self.quarters):
                spot = scalars[1] ^ j
                for k in range(ranks):
                    for c in range(3):
                        at = c * self.all_heads + k * self.group + spot * self.piece
                        win[rows_at(at, self.piece)] = piece_refs[j][
                            k, c * self.piece : (c + 1) * self.piece
                        ]
                    at = k * self.group + spot * self.piece
                    wout[rows_at(at, self.piece)] = piece_refs[j][
                        k, 3 * self.piece : 4 * self.piece
                    ]
            start = jnp.concatenate([ref[...] for ref in block_refs]).astype(F32)
            start = jnp.where(keep_ref[:, 0:1] > 0, start, 0)
            if split:
                other = jnp.concatenate([ref[...] for ref in pair_refs]).astype(F32)
                start = jnp.where(keep_ref[:, 1:2] > 0, other, start)
            rows_ref[...] = start.astype(LOW)
            unit, _ = unit_of(start)
            normed_ref[...] = swap(unit * along_ref[0:1] + along_ref[3:4]).astype(LOW)

            @pl.loop(0, wide // 256)
            def _(n):
                at = pl.ds(pl.multiple_of(n * 256, 256), 256)
                qkv[:, at] = (nt(normed_ref[...], win[at]) + shift_ref[:, at]).astype(LOW)

            @pl.loop(0, self.all_heads // 128)
            def _(n):
                lanes = lambda c: pl.ds(pl.multiple_of(c * self.all_heads + n * 128, 128), 128)
                query, key, value = (qkv[:, lanes(c)] for c in range(3))
                total = jnp.zeros((rows, 128), F32)
                for mask in half_lanes(128):
                    scores = nt(query * mask.astype(LOW), key) * SCALE + same[...]
                    total = total + nn(softmax(scores).astype(LOW), value) * mask
                mixed[:, lanes(0)] = total.astype(LOW)

            out = swap(nn(mixed[...], wout[...])) + along_ref[6:7]
            for k in range(ranks):
                part = out[k * lay.block : (k + 1) * lay.block]
                sent[k][...] = part.astype(LOW)
                if split:
                    pair = jnp.where(scalars[0] == 0, part[lay.room :], part[: lay.room])
                    sent_pair[k][...] = pair.astype(LOW)

        outs = [shape(lay.block, width)] * ranks
        if split:
            outs += [shape(lay.room, width)] * ranks
        outs += [
            shape(rows, width),
            shape(rows, width),
            shape(rows, wide),
            shape(rows, self.all_heads),
            shape(wide, width),
            shape(self.all_heads, width),
        ]
        ins = list(blocks) + list(pairs) + [keep] + list(pieces) + [along, shift, self.same_place]
        flops = 2 * rows * width * (wide + self.all_heads) + 4 * rows * rows * self.all_heads
        outs = self.call(body, outs, ins, flops)
        sent, outs = outs[:ranks], outs[ranks:]
        if split:
            sent_pair, outs = outs[:ranks], outs[ranks:]
        else:
            sent_pair = ()
        return sent, sent_pair, outs

    def temporal_back(self, sources, matrix, qkv, mixed, wout):
        lay, width = self.layout, self.width
        rows, wide = lay.place_rows, 3 * self.all_heads

        def body(scalars, *refs):
            source_refs = refs[: len(sources)]
            matrix_ref, qkv_ref, mixed_ref, wout_ref, same, grad_ref, out_ref, part = refs[
                len(sources) :
            ]
            swap = swapper(scalars, self.place.paired)
            source = jnp.concatenate([ref[...] for ref in source_refs])
            grad_ref[...] = swap(nn(matrix_ref[...], source)).astype(LOW)
            part[...] = nt(grad_ref[...], wout_ref[...]).astype(LOW)

            @pl.loop(0, self.all_heads // 128)
            def _(n):
                lanes = lambda c: pl.ds(pl.multiple_of(c * self.all_heads + n * 128, 128), 128)
                query, key, value = (qkv_ref[:, lanes(c)] for c in range(3))
                grad = part[:, lanes(0)]
                totals = [jnp.zeros((rows, 128), F32) for _ in range(3)]
                for mask in half_lanes(128):
                    low = mask.astype(LOW)
                    probs = softmax(nt(query * low, key) * SCALE + same[...])
                    scored = score_back(probs, nt(grad * low, value))
                    for c, item in enumerate(
                        (
                            nn(scored, key) * SCALE,
                            tn(scored, query) * SCALE,
                            tn(probs.astype(LOW), grad),
                        )
                    ):
                        totals[c] = totals[c] + item * mask
                for c in range(3):
                    out_ref[:, lanes(c)] = totals[c].astype(LOW)

        outs = [shape(rows, width), shape(rows, wide)]
        ins = list(sources) + [matrix, qkv, mixed, wout, self.same_place]
        flops = 2 * rows * width * self.all_heads + 10 * rows * rows * self.all_heads
        return self.call(
            body, outs, ins, flops, scratch=[pltpu.VMEM((rows, self.all_heads), LOW)]
        )

    def temporal_weights(self, qkv_grad, normed, mixed, out_grad):
        lay, width = self.layout, self.width
        rows, ranks = lay.place_rows, self.ranks

        def body(scalars, grad_ref, normed_ref, mixed_ref, out_ref, *pieces):
            pieces, sums = pieces[: self.quarters], pieces[self.quarters]
            sums[...] = column_sum(grad_ref[...])

            def put(total, k, c):
                for j in range(self.quarters):
                    at = rows_at((scalars[1] ^ j) * self.piece, self.piece)
                    pieces[j][k, c * self.piece : (c + 1) * self.piece] = total[at]

            def inner(total):
                for c in range(3):
                    for k in range(ranks):
                        at = c * self.all_heads + k * self.group
                        part = tn(grad_ref[:, at : at + self.group], normed_ref[...])
                        total[...] = part.astype(LOW)
                        put(total, k, c)
                for k in range(ranks):
                    at = k * self.group
                    part = tn(mixed_ref[:, at : at + self.group], out_ref[...])
                    total[...] = part.astype(LOW)
                    put(total, k, 3)

            pl.run_scoped(inner, pltpu.VMEM((self.group, width), LOW))

        outs = [shape(ranks, 4 * self.piece, width)] * self.quarters
        outs += [shape(1, 3 * self.all_heads, dtype=F32)]
        flops = 8 * rows * width * self.all_heads
        outs = self.call(body, outs, [qkv_grad, normed, mixed, out_grad], flops)
        return outs[:-1], outs[-1]

    def temporal_input(self, qkv_grad, win, start, along):
        lay, width = self.layout, self.width
        ranks = self.ranks

        def body(scalars, grad_ref, win_ref, start_ref, along_ref, *refs):
            sent, sums = refs[:ranks], refs[ranks]
            swap = swapper(scalars, self.place.paired)
            unit, inverse = unit_of(start_ref[...].astype(F32))
            grad = swap(nn(grad_ref[...], win_ref[...]))
            back, gain, shift = norm_back(grad, unit, inverse, along_ref[0:1])
            sums[0:1] = gain
            sums[1:2] = shift
            for k in range(ranks):
                sent[k][...] = back[k * lay.block : (k + 1) * lay.block].astype(LOW)

        outs = [shape(lay.block, width)] * ranks + [shape(2, width, dtype=F32)]
        flops = 6 * lay.place_rows * width * self.all_heads
        outs = self.call(body, outs, [qkv_grad, win, start, along], flops)
        return outs[:-1], outs[-1]


    def spatial_in(self, sources, matrix, start, pieces, along, shift):
        lay, width = self.layout, self.width
        rows, ranks, quarters = lay.frame_rows, self.ranks, self.quarters
        piece, group = self.piece, self.group

        def body(scalars, *refs):
            refs = list(refs)
            take = lambda n: [refs.pop(0) for _ in range(n)]
            source_refs = take(len(sources))
            matrix_ref, start_ref = take(2)
            piece_refs = take(quarters)
            along_ref, shift_ref = take(2)
            after_ref, temporal_ref, normed_ref = take(3)
            qkv_refs = take(quarters)
            win, wout, fc = take(3)
            swap = swapper(scalars, self.place.paired)
            for i in range(quarters):
                spot = scalars[1] ^ i
                for j in range(quarters):
                    k = scalars[1] ^ j
                    for c in range(3):
                        at = j * 3 * group + c * group + spot * piece
                        win[rows_at(at, piece)] = piece_refs[i][k, c * piece : (c + 1) * piece]
                    at = j * group + spot * piece
                    wout[rows_at(at, piece)] = piece_refs[i][k, 3 * piece : 4 * piece]
                for k in range(ranks):
                    at = (scalars[2] ^ k) * group + spot * piece
                    fc[rows_at(at, piece)] = piece_refs[i][k, 4 * piece : 5 * piece]
            source = jnp.concatenate([ref[...] for ref in source_refs])
            temporal = swap(nn(matrix_ref[...], source)).astype(LOW)
            temporal_ref[...] = temporal
            after = start_ref[...].astype(F32) + nt(temporal, fc[...]) + along_ref[7:8]
            after_ref[...] = after
            unit, _ = unit_of(after)
            normed = swap(unit * along_ref[1:2] + along_ref[4:5]).astype(LOW)
            normed_ref[...] = normed
            for j in range(quarters):
                at = slice(j * 3 * group, (j + 1) * 3 * group)
                qkv_refs[j][...] = (nt(normed, win[at]) + shift_ref[:, at]).astype(LOW)

        outs = [shape(rows, width, dtype=F32), shape(rows, width), shape(rows, width)]
        outs += [shape(rows, 3 * group)] * quarters
        outs += [
            shape(3 * self.all_heads, width),
            shape(self.all_heads, width),
            shape(width, width),
        ]
        ins = list(sources) + [matrix, start] + list(pieces) + [along, shift]
        flops = 2 * rows * width * (3 * self.all_heads + width)
        outs = self.call(body, outs, ins, flops)
        return outs[:3], outs[3 : 3 + quarters], outs[3 + quarters :]

    def windows(self, refs, n):
        at = rows_at(n * (WINDOW - 16), WINDOW)
        return jnp.concatenate([ref[at] for ref in refs])

    def window_mask(self, n, axis):
        size = self.quarters * WINDOW
        dims = (size, 1) if axis == 0 else (1, size)
        index = lax.broadcasted_iota(jnp.int32, dims, axis) & (WINDOW - 1)
        start = n * (self.layout.places - WINDOW + 16)
        return (index >= start) & (index < start + self.layout.places)

    def put_windows(self, refs, n, values, mask):
        for j, ref in enumerate(refs):
            at = rows_at(n * (WINDOW - 16), WINDOW)
            part = slice(j * WINDOW, (j + 1) * WINDOW)
            old = ref[at].astype(F32)
            ref[at] = jnp.where(mask[part], values[part], old).astype(LOW)

    def spatial(self, qkv):
        lay, quarters, group = self.layout, self.quarters, self.group

        def body(scalars, *refs):
            qkv_refs, out_refs = refs[:quarters], refs[quarters:]
            for ref in out_refs:
                ref[...] = jnp.zeros_like(ref)

            @pl.loop(0, lay.units)
            def _(n):
                rows = self.windows(qkv_refs, n)
                hide = jnp.where(self.window_mask(n, 1), 0.0, HIDE)
                parts = []
                for h in range(self.heads):
                    query, key, value = (
                        rows[:, c * group + h * HEAD_DIM : c * group + (h + 1) * HEAD_DIM]
                        for c in range(3)
                    )
                    probs = softmax(nt(query, key) * SCALE + hide)
                    parts.append(nn(probs.astype(LOW), value))
                mask = self.window_mask(n, 0)
                self.put_windows(out_refs, n, jnp.concatenate(parts, -1), mask)

        outs = [shape(lay.frame_rows, group)] * quarters
        size = quarters * WINDOW
        return self.call(body, outs, list(qkv), 4 * lay.units * size * size * group)

    def spatial_back(self, qkv, grads):
        lay, quarters, group = self.layout, self.quarters, self.group

        def body(scalars, *refs):
            qkv_refs, grad_refs = refs[:quarters], refs[quarters : 2 * quarters]
            out_refs = refs[2 * quarters :]
            for ref in out_refs:
                ref[...] = jnp.zeros_like(ref)

            @pl.loop(0, lay.units)
            def _(n):
                rows = self.windows(qkv_refs, n)
                mask = self.window_mask(n, 0)
                grads = self.windows(grad_refs, n) * mask.astype(F32).astype(LOW)
                hide = jnp.where(self.window_mask(n, 1), 0.0, HIDE)
                parts = [[], [], []]
                for h in range(self.heads):
                    query, key, value = (
                        rows[:, c * group + h * HEAD_DIM : c * group + (h + 1) * HEAD_DIM]
                        for c in range(3)
                    )
                    grad = grads[:, h * HEAD_DIM : (h + 1) * HEAD_DIM]
                    probs = softmax(nt(query, key) * SCALE + hide)
                    scored = score_back(probs, nt(grad, value))
                    parts[0].append(nn(scored, key) * SCALE)
                    parts[1].append(tn(scored, query) * SCALE)
                    parts[2].append(tn(probs.astype(LOW), grad))
                values = jnp.concatenate(parts[0] + parts[1] + parts[2], -1)
                self.put_windows(out_refs, n, values, mask)

        outs = [shape(lay.frame_rows, 3 * group)] * quarters
        size = quarters * WINDOW
        flops = 10 * lay.units * size * size * group
        return self.call(body, outs, list(qkv) + list(grads), flops)

    def spatial_out(self, mixed, wout, after, grad, along):
        lay, width, group = self.layout, self.width, self.group
        rows, quarters = lay.frame_rows, self.quarters

        def body(scalars, *refs):
            mixed_refs = refs[:quarters]
            wout_ref, after_ref, grad_ref, along_ref, out_ref, normed_ref, low_ref = refs[quarters:]
            swap = swapper(scalars, self.place.paired)
            total = jnp.zeros((rows, width), F32)
            for j in range(quarters):
                total = total + nn(mixed_refs[j][...], wout_ref[j * group : (j + 1) * group])
            after = after_ref[...] + swap(total) + along_ref[8:9]
            out_ref[...] = after
            unit, _ = unit_of(after)
            normed_ref[...] = swap(unit * along_ref[2:3] + along_ref[5:6]).astype(LOW)
            low_ref[...] = swap(grad_ref[...].astype(F32)).astype(LOW)

        outs = [shape(rows, width, dtype=F32), shape(rows, width), shape(rows, width)]
        ins = list(mixed) + [wout, after, grad, along]
        return self.call(body, outs, ins, 2 * rows * width * self.all_heads)

    def feed_forward(self, normed, grad, weights, shift, totals):
        lay, width = self.layout, self.width
        rows = lay.frame_rows
        hidden = weights.shape[1]
        tile = 256

        def body(scalars, normed_ref, grad_ref, weight_ref, shift_ref, *refs):
            out_ref, back_ref, weight_grad, sums = refs[-4:]
            if totals is None:
                out_ref[...] = jnp.zeros_like(out_ref)
                back_ref[...] = jnp.zeros_like(back_ref)
            else:
                out_ref[...] = refs[0][...]
                back_ref[...] = refs[1][...]

            @pl.loop(0, hidden // tile)
            def _(n):
                at = pl.ds(pl.multiple_of(n * tile, tile), tile)
                up, down = weight_ref[0, at], weight_ref[1, at]
                values = nt(normed_ref[...], up) + shift_ref[:, at]
                half = 0.5 * (1.0 + lax.erf(values * SQRT_HALF))
                active = (values * half).astype(LOW)
                slope = half + values * jnp.exp(-0.5 * values * values) * INV_ROOT_TAU
                out_ref[...] += nn(active, down)
                weight_grad[1, at] = tn(active, grad_ref[...]).astype(LOW)
                hidden_grad = (nt(grad_ref[...], down) * slope).astype(LOW)
                weight_grad[0, at] = tn(hidden_grad, normed_ref[...]).astype(LOW)
                back_ref[...] += nn(hidden_grad, up)
                sums[:, at] = column_sum(hidden_grad)

        outs = [
            shape(rows, width, dtype=F32),
            shape(rows, width, dtype=F32),
            shape(2, hidden, width),
            shape(1, hidden, dtype=F32),
        ]
        ins = [normed, grad, weights, shift] + ([] if totals is None else list(totals))
        return self.call(body, outs, ins, 12 * rows * width * hidden)

    def feed_forward_back(self, after, out, back, grad, mixed, wout, along):
        lay, width, group = self.layout, self.width, self.group
        rows, quarters = lay.frame_rows, self.quarters

        def body(scalars, after_ref, out_ref, back_ref, grad_ref, wout_ref, along_ref, *refs):
            mixed_refs, refs = refs[:quarters], refs[quarters:]
            layer_ref, total_ref, sums, wout_grad = refs[:4]
            mixed_grads = refs[4:]
            swap = swapper(scalars, self.place.paired)
            after = after_ref[...]
            layer_ref[...] = (after + swap(out_ref[...]) + along_ref[9:10]).astype(LOW)
            unit, inverse = unit_of(after)
            back, gain, shift = norm_back(swap(back_ref[...]), unit, inverse, along_ref[2:3])
            grad = grad_ref[...].astype(F32)
            total = grad + back
            total_ref[...] = total
            low = total.astype(LOW)
            sums[0:1] = gain
            sums[1:2] = shift
            sums[2:3] = column_sum(low)
            sums[3:4] = column_sum(grad)
            low = swap(low.astype(F32)).astype(LOW)
            for j in range(quarters):
                at = slice(j * group, (j + 1) * group)
                mixed_grads[j][...] = nt(low, wout_ref[at]).astype(LOW)
                wout_grad[at] = tn(mixed_refs[j][...], low).astype(LOW)

        outs = [
            shape(rows, width),
            shape(rows, width, dtype=F32),
            shape(4, width, dtype=F32),
            shape(self.all_heads, width),
        ] + [shape(rows, group)] * quarters
        ins = [after, out, back, grad, wout, along] + list(mixed)
        outs = self.call(body, outs, ins, 4 * rows * width * self.all_heads)
        return outs[:4], outs[4:]

    def spatial_input(self, qkv_grads, win, after, total, along, fc, matrix):
        lay, width, group = self.layout, self.width, self.group
        rows, quarters, ranks = lay.frame_rows, self.quarters, self.ranks
        split = lay.split > 0

        def body(scalars, *refs):
            grad_refs = refs[:quarters]
            win_ref, after_ref, total_ref, along_ref, fc_ref, matrix_ref = refs[
                quarters : quarters + 6
            ]
            out_ref, low_ref, sums = refs[quarters + 6 : quarters + 9]
            sent = refs[quarters + 9 :]
            swap = swapper(scalars, self.place.paired)
            grad = jnp.zeros((rows, width), F32)
            for j in range(quarters):
                at = slice(j * 3 * group, (j + 1) * 3 * group)
                grad = grad + nn(grad_refs[j][...], win_ref[at])
            unit, inverse = unit_of(after_ref[...])
            back, gain, shift = norm_back(swap(grad), unit, inverse, along_ref[1:2])
            total = total_ref[...] + back
            out_ref[...] = total
            low = total.astype(LOW)
            low_ref[...] = low
            temporal = swap(nn(low, fc_ref[...])).astype(LOW)
            sums[0:1] = gain
            sums[1:2] = shift
            sums[2:3] = column_sum(temporal)
            sums[3:4] = column_sum(low)
            at = 0
            for ref in sent:
                size = ref.shape[0]
                ref[...] = nn(matrix_ref[at : at + size], temporal).astype(LOW)
                at += size

        outs = [
            shape(rows, width, dtype=F32),
            shape(rows, width),
            shape(4, width, dtype=F32),
        ]
        outs += [shape(lay.sent, width)] * ranks
        outs += [shape(lay.sent_pair, width)] * (ranks if split else 0)
        ins = list(qkv_grads) + [win, after, total, along, fc, matrix]
        outs = self.call(body, outs, ins, 2 * rows * width * (3 * self.all_heads + width))
        return outs[:3], outs[3 : 3 + ranks], outs[3 + ranks :]

    def spatial_weights(self, qkv_grads, normed, wout_grad, low, temporal):
        lay, width, group, piece = self.layout, self.width, self.group, self.piece
        rows, quarters, ranks = lay.frame_rows, self.quarters, self.ranks

        def body(scalars, *refs):
            grad_refs = refs[:quarters]
            normed_ref, wout_ref, low_ref, temporal_ref = refs[quarters : quarters + 4]
            pieces = refs[quarters + 4 : 2 * quarters + 4]
            sums = refs[2 * quarters + 4]

            def inner(total, fc):
                for j in range(quarters):
                    k = scalars[1] ^ j
                    at = slice(j * 3 * group, (j + 1) * 3 * group)
                    sums[:, at] = column_sum(grad_refs[j][...])
                    total[...] = tn(grad_refs[j][...], normed_ref[...]).astype(LOW)
                    for i in range(quarters):
                        spot = (scalars[1] ^ i) * piece
                        for c in range(3):
                            pieces[i][k, c * piece : (c + 1) * piece] = total[
                                rows_at(c * group + spot, piece)
                            ]
                        pieces[i][k, 3 * piece : 4 * piece] = wout_ref[
                            rows_at(j * group + spot, piece)
                        ]
                fc[...] = tn(low_ref[...], temporal_ref[...]).astype(LOW)
                for i in range(quarters):
                    for k in range(ranks):
                        at = (scalars[2] ^ k) * group + (scalars[1] ^ i) * piece
                        pieces[i][k, 4 * piece : 5 * piece] = fc[rows_at(at, piece)]

            pl.run_scoped(
                inner,
                pltpu.VMEM((3 * group, width), LOW),
                pltpu.VMEM((width, width), LOW),
            )

        outs = [shape(ranks, 5 * piece, width)] * quarters
        outs += [shape(1, 3 * self.all_heads, dtype=F32)]
        ins = list(qkv_grads) + [normed, wout_grad, low, temporal]
        flops = 2 * rows * width * (3 * self.all_heads + width)
        outs = self.call(body, outs, ins, flops)
        return outs[:-1], outs[-1]

    def natural(self, parts):
        lay, width = self.layout, self.width
        count = lay.natural_blocks
        counts = [len(rows) for _, rows in parts]

        def body(scalars, *refs):
            refs = list(refs)
            out_ref = refs.pop()
            total = jnp.zeros((count * WINDOW, width), F32)
            for size in counts:
                matrix = refs.pop(0)
                source = jnp.concatenate([refs.pop(0)[...] for _ in range(size)])
                total = total + nn(matrix[...], source)
            total = total.astype(LOW)
            for item in range(count):
                out_ref[item] = total[item * WINDOW : item * WINDOW + lay.places]

        ins = []
        for matrix, rows in parts:
            ins += [matrix] + list(rows)
        return self.call(body, [shape(count, lay.places, width)], ins)[0]


def body(
    clip_input,
    clip_slot,
    norm_gain,
    norm_shift,
    attention_in,
    attention_bias,
    attention_out,
    branch_bias,
    temporal_fc,
    hidden_in,
    hidden_bias,
    hidden_out,
    output_grad,
):
    place = Place()
    shards, quarters, ranks = place.shards, place.quarters, place.ranks
    shard, context, tensor = place.shard, place.context, place.tensor
    clips, live = clip_input[:, 0], clip_slot[:, 0]
    lay = Layout(place, clips, live)
    mask = live[:, None, None, None].astype(LOW)
    cotangents = output_grad[:, 0] * mask
    columns = attention_in.shape[1]
    width = columns * shards
    group = attention_in.shape[3]
    hidden = hidden_in.shape[1]
    piece = group // quarters
    split = lay.split > 0
    scalars = jnp.stack([shard, context, tensor]).astype(jnp.int32)
    prog = Program(place, lay, width, group, scalars)

    vectors = jnp.concatenate(
        [norm_gain, norm_shift, branch_bias, attention_bias.reshape(-1, columns)]
        + [hidden_bias.reshape(-1, columns)]
    )
    if place.paired:
        both = jnp.stack([vectors, hop(vectors, "shard", 1)])
        both = jnp.where(shard == 0, both, both[::-1])
    else:
        both = lax.all_gather(vectors, "shard")
    along = jnp.swapaxes(both[:, :10], 0, 1).reshape(10, width).astype(F32)
    last = 10 + attention_bias.size // columns
    own = both[:, 10:]
    own = jnp.stack([own] + [hop(own, "tensor", k) for k in range(1, ranks)], 1).astype(F32)
    biases = own[:, :, : last - 10].reshape((shards, ranks) + attention_bias.shape)
    biases = jnp.transpose(biases, (2, 3, 1, 4, 0, 5)).reshape(2, 2, ranks, group)
    biases = jnp.stack([biases[:, 0], jnp.zeros_like(biases[:, 0]), biases[:, 1]], 1)
    shift_a = biases[0].reshape(1, -1)
    shift_b = jnp.swapaxes(biases[1], 0, 1)
    shift_b = jnp.stack([pick(shift_b, context ^ j) for j in range(quarters)]).reshape(1, -1)
    up_shift = own[:, :, last - 10 :].reshape((shards, ranks) + hidden_bias.shape)
    up_shift = jnp.transpose(up_shift, (1, 2, 0, 3)).reshape(ranks, quarters, -1)
    up_shift = [pick(up_shift, context ^ j, 1).reshape(1, -1) for j in range(quarters)]

    def quarter_in(weight):
        part = pick(weight.reshape(columns, 3, quarters, piece), context, 2)
        return jnp.transpose(part, (1, 2, 0)).reshape(3 * piece, columns)

    def quarter(rows):
        return pick(rows.reshape(quarters, -1, rows.shape[-1]), context)

    fc_part = lax.dynamic_slice_in_dim(
        temporal_fc, (tensor * quarters + context) * piece, piece, 1
    ).T
    block_a = jnp.concatenate([quarter_in(attention_in[0]), quarter(attention_out[0])])
    block_b = jnp.concatenate([quarter_in(attention_in[1]), quarter(attention_out[1]), fc_part])
    up_part = pick(hidden_in.reshape(columns, quarters, -1), context, 1).T
    block_c = jnp.stack([up_part, quarter(hidden_out)])
    pieces_a = gather_blocks(place, block_a)
    pieces_b = gather_blocks(place, block_b)
    pieces_c = gather_blocks(place, block_c, 1)
    pieces_c = [item.reshape(2, -1, width) for item in pieces_c]

    steps = [(0, k) for k in range(ranks)] + [(1, k) for k in range(ranks if split else 0)]

    def across(values, step):
        pair, k = step
        if pair:
            return hop_pair(values, k)
        return values if k == 0 else hop(values, "tensor", k)

    flip = lambda pair: 1 - shard if pair else shard
    natural = lay.natural_labels(tensor)
    alive = lay.held(natural)
    frame, frame_whole = lay.frame_labels(shard, tensor)
    sending = one_hot(
        [lay.place_labels(flip(pair), tensor ^ k, k)[0] for pair, k in steps], [natural]
    )
    here = [lay.place_labels(shard, tensor, k) for k in range(ranks)]
    here_labels = jnp.stack([labels for labels, _ in here])
    here_whole = jnp.stack([whole for _, whole in here])
    here_mine = (here_whole | lay.held(here_labels)) & (here_labels >= 0)
    keep = jnp.stack([here_mine, (here_labels >= 0) & ~here_mine], -1)
    keep = keep.reshape(-1, 2).astype(F32)
    start_sources = [jnp.where(alive, natural, -1)]
    if split:
        spot = jnp.arange(WINDOW)
        batch = jnp.arange(lay.whole, lay.batches)[:, None]
        others = lay.label(batch, lay.frames * tensor + shard, spot)
        others = jnp.where((spot < lay.places) & ~lay.held(others), others, -1)
        start_sources.append(others)
    starting = one_hot([frame], start_sources)

    def source_labels(step):
        pair, k = step
        labels, whole = lay.place_labels(flip(pair), tensor ^ k, k)
        return jnp.where(whole, -1, labels) if pair else labels

    returning = one_hot(
        [frame],
        [source_labels((0, k)) for k in range(ranks)]
        + [pick(source_labels((1, k)), shard) for k in range(ranks if split else 0)],
    )

    def packed(labels, whole_too, index):
        parts = [labels[:, : lay.first].reshape(-1)] if whole_too else []
        if split:
            parts.append(pick(labels, index)[lay.first : lay.first + lay.later])
        parts = jnp.concatenate(parts)
        size = lay.sent if whole_too else lay.sent_pair
        return jnp.pad(parts, (0, size - parts.shape[0]), constant_values=-1)

    leaving = one_hot(
        [
            packed(lay.place_labels(flip(pair), tensor ^ k, k)[0], not pair, shard)
            for pair, k in steps
        ],
        [frame],
    )
    arriving = one_hot(
        [labels for labels, _ in here],
        [packed(here[k][0], not pair, flip(pair)) for pair, k in steps],
    )
    home = jnp.where(lay.living(natural), natural, -1)
    homing = one_hot([home], [source_labels(step) for step in steps])
    ending = [one_hot([home], [frame])]
    if split:
        far, far_whole = lay.frame_labels(1 - shard, tensor)
        ending.append(one_hot([home], [jnp.where(far_whole, -1, far)]))

    flat = lambda rows: rows.reshape((-1,) + rows.shape[2:])
    clips, cotangents = flat(clips), flat(cotangents)
    sent = prog.send_rows(clips, cotangents, sending, len(steps))
    blocks = [across(rows, step) for rows, step in zip(sent, steps)]
    other_clips, other_grads = [hop(rows, "shard", 1) for rows in sent[len(steps) :]] or (None,) * 2
    start = prog.frames_of(clips, other_clips, starting)
    grad = prog.frames_of(cotangents, other_grads, starting)

    sent, sent_pair, kept = prog.temporal(
        blocks[:ranks], blocks[ranks:], keep, pieces_a, along, shift_a
    )
    normed_a, start_a, qkv_a, mixed_a, win_a, wout_a = kept
    sources = [across(rows, step) for rows, step in zip(list(sent) + list(sent_pair), steps)]

    def to_groups(parts):
        return [parts[0]] + [hop(parts[j], "context", j) for j in range(1, quarters)]

    kept, qkv, weights_b = prog.spatial_in(sources, returning, start, pieces_b, along, shift_b)
    after_a, temporal, normed_b = kept
    win_b, wout_b, fc = weights_b
    qkv = to_groups(qkv)
    mixed = to_groups(prog.spatial(qkv))
    after_b, normed_c, low = prog.spatial_out(mixed, wout_b, after_a, grad, along)

    totals, piece_grads, up_bias_grads = None, [None] * quarters, [None] * quarters
    for j in (1, 3, 0, 2):
        out, back, piece_grads[j], up_bias_grads[j] = prog.feed_forward(
            normed_c, low, pieces_c[j], up_shift[j], totals
        )
        totals = (out, back)
    kept, mixed_grads = prog.feed_forward_back(
        after_b, totals[0], totals[1], grad, mixed, wout_b, along
    )
    layer_rows, total, sums_c, wout_grad = kept
    total_c = reduce_blocks(
        place, [item.reshape(2, ranks, -1, width) for item in piece_grads], 1
    )
    layer_out = [(ending[0], [layer_rows])]
    if split:
        layer_out.append((ending[1], [hop(layer_rows, "shard", 1)]))
    layer_out = prog.natural(layer_out)

    qkv_grads = to_groups(prog.spatial_back(qkv, to_groups(mixed_grads)))
    kept, sent, sent_pair = prog.spatial_input(
        qkv_grads, win_b, after_a, total, along, fc, leaving
    )
    total, low_fc, sums_b = kept
    pieces, pair_b = prog.spatial_weights(qkv_grads, normed_b, wout_grad, low_fc, temporal)
    total_b = reduce_blocks(place, pieces)
    sources = [across(rows, step) for rows, step in zip(list(sent) + list(sent_pair), steps)]
    out_grad_a, qkv_grad_a = prog.temporal_back(sources, arriving, qkv_a, mixed_a, wout_a)
    pieces, pair_a = prog.temporal_weights(qkv_grad_a, normed_a, mixed_a, out_grad_a)
    total_a = reduce_blocks(place, pieces)
    sent, sums_a = prog.temporal_input(qkv_grad_a, win_a, start_a, along)
    back = [across(sent[k], (pair, k)) for pair, k in steps]
    low_total = total.astype(LOW)
    input_grad = [(ending[0], [low_total])]
    if split:
        input_grad.append((ending[1], [hop(low_total, "shard", 1)]))
    input_grad.append((homing, back))
    input_grad = prog.natural(input_grad)

    def in_grad(total):
        part = total[:, : 3 * piece].reshape(quarters, 3, piece, columns)
        return jnp.transpose(part, (3, 1, 0, 2)).reshape(columns, 3, group)

    def out_grad(total):
        return total[:, 3 * piece : 4 * piece].reshape(group, columns)

    in_total = jnp.stack([in_grad(total_a), in_grad(total_b)])
    out_total = jnp.stack([out_grad(total_a), out_grad(total_b)])
    fc_total = total_b[:, 4 * piece :].reshape(group, columns).astype(LOW)
    fc_total = [fc_total] + [hop(fc_total, "tensor", k) for k in range(1, ranks)]
    fc_total = ordered(fc_total, tensor).reshape(width, columns).T.astype(F32)

    sums = jnp.concatenate([sums_a, sums_b, sums_c])
    sums = sums[jnp.asarray([0, 2, 6, 1, 3, 7, 4, 5, 8, 9])].reshape(-1)
    pair_a = jnp.swapaxes(pair_a.reshape(3, ranks, group), 0, 1)
    pair_b = pair_b.reshape(quarters, 3, group)
    pair_b = ordered([pair_b[j] for j in range(quarters)], context)
    inner = jnp.stack([pair_a, pair_b], 1)[:, :, ::2]
    inner = ordered([inner[k] for k in range(ranks)], tensor).reshape(-1)
    outer = ordered([item.reshape(ranks, -1) for item in up_bias_grads], context, 1)
    outer = ordered([outer[k] for k in range(ranks)], tensor).reshape(-1)
    sums = jnp.concatenate([sums, inner, outer])
    ends = [10 * width, 10 * width + inner.size]
    sums = lax.psum(sums, ("shard", "context", "tensor"))
    along, inner, outer = jnp.split(sums, ends)
    along = lax.dynamic_slice_in_dim(along.reshape(10, width), shard * columns, columns, 1)
    inner = pick(inner.reshape((ranks,) + attention_bias.shape[:3] + (HEAD_DIM,)), tensor)
    part = HEAD_DIM // shards
    inner = lax.dynamic_slice_in_dim(inner, shard * part, part, 3)
    outer = pick(outer.reshape(ranks, -1, shards, hidden_bias.shape[1]), tensor)
    outer = pick(outer, shard, 1)
    rows_shape = clip_input.shape
    return (
        layer_out.reshape(rows_shape),
        input_grad.reshape(rows_shape),
        along[:3],
        along[3:6],
        in_total,
        inner,
        out_total,
        along[6:],
        fc_total,
        total_c[:, 0].reshape(hidden, columns).T,
        outer,
        total_c[:, 1].reshape(hidden, columns),
    )


def solution(mesh):
    rows = P(None, "shard", "tensor", "context", None)
    weights = (
        P(None, "shard"),
        P(None, "shard"),
        P(None, "shard", None, "tensor"),
        P(None, None, "tensor", "shard"),
        P(None, "tensor", "shard"),
        P(None, "shard"),
        P("shard", None),
        P("shard", "tensor"),
        P("tensor", "shard"),
        P("tensor", "shard"),
    )
    return jax.shard_map(
        body,
        mesh=mesh,
        in_specs=(rows, P(None, "shard")) + weights + (rows,),
        out_specs=(rows, rows) + weights,
        check_vma=False,
    )
```

```python
import jax
import jax.numpy as jnp
import numpy as np
from jax import lax
from jax.experimental import pallas as pl
from jax.experimental.pallas import tpu as pltpu
from jax.sharding import PartitionSpec as P

HEAD_DIM = 64
WINDOW = 64
EPS = 1e-06
SQRT_HALF = 0.7071067811865476
INV_ROOT_TAU = 0.3989422804014327
SCALE = HEAD_DIM**-0.5
HIDE = -1e30
LOW = jnp.bfloat16
F32 = jnp.float32
VMEM_BYTES = 60 * 2**20


def hop(values, axis, step):
    count = lax.axis_size(axis)
    return lax.ppermute(values, axis, [(i, i ^ step) for i in range(count)])


def hop_pair(values, step):
    ranks = lax.axis_size("tensor")
    pairs = [
        (a * ranks + i, (1 - a) * ranks + (i ^ step)) for a in range(2) for i in range(ranks)
    ]
    return lax.ppermute(values, ("shard", "tensor"), pairs)


def pick(values, index, axis=0):
    return lax.dynamic_index_in_dim(values, index, axis, keepdims=False)


def ordered(parts, me, axis=0):
    shape = list(parts[0].shape)
    shape.insert(axis, len(parts))
    out = jnp.zeros(shape, parts[0].dtype)
    for j, part in enumerate(parts):
        out = lax.dynamic_update_index_in_dim(out, part, me ^ j, axis)
    return out


def round_up(value, step):
    return -(-value // step) * step


class Place:
    def __init__(self):
        self.shard = lax.axis_index("shard")
        self.context = lax.axis_index("context")
        self.tensor = lax.axis_index("tensor")
        self.shards = lax.axis_size("shard")
        self.ranks = lax.axis_size("tensor")
        self.quarters = lax.axis_size("context")
        self.paired = self.shards == 2


def gather_columns(place, part):
    if place.paired:
        return jnp.concatenate([part, hop(part, "shard", 1)], -1)
    return lax.all_gather(part, "shard", axis=part.ndim - 1, tiled=True)


def tie(values, *others):
    return lax.optimization_barrier((values,) + others)[0]


class Gather:
    def __init__(self, place, block, short=False):
        self.place, self.short = place, short
        mine = pick(block, place.context)
        self.mine = jnp.stack([mine, pick(block, place.context ^ 2)]) if short else mine

    def hops(self):
        parts = [self.mine] + [hop(self.mine, "tensor", k) for k in range(1, self.place.ranks)]
        self.blocks = jnp.stack(parts, 1 if self.short else 0)

    def columns(self):
        self.first = gather_columns(self.place, self.blocks)

    def rows(self):
        if not self.short:
            self.second = hop(self.first, "context", 2)

    def cores(self):
        if self.short:
            return [self.first, hop(self.first, "context", 1)]
        return [
            self.first,
            hop(self.first, "context", 1),
            self.second,
            hop(self.second, "context", 1),
        ]


def add(*terms):
    total = terms[0].astype(F32)
    for term in terms[1:]:
        total = total + term.astype(F32)
    return total.astype(LOW)


class Reduce:
    def __init__(self, place, pieces, short=False):
        self.place, self.short = place, short
        self.kept = [pieces[0], pieces[2]]
        self.come = [hop(pieces[1], "context", 1), hop(pieces[3], "context", 1)]

    def cores(self):
        self.first, self.second = [add(*pair) for pair in zip(self.kept, self.come)]
        return [self.first, self.second]

    def rows(self):
        if self.short:
            self.total = jnp.stack([self.first, self.second])
        else:
            self.total = add(self.first, hop(self.second, "context", 2))
        return [self.total]

    def columns(self):
        total = self.total
        if self.place.paired:
            half = total.shape[-1] // 2
            self.mine = add(total[..., :half], hop(total[..., half:], "shard", 1))
        else:
            axis = total.ndim - 1
            self.mine = lax.psum_scatter(total, "shard", scatter_dimension=axis, tiled=True)
        return [self.mine]

    def hops(self):
        axis = 1 if self.short else 0
        block = lambda k: lax.index_in_dim(self.mine, k, axis, keepdims=False)
        parts = [hop(block(k), "tensor", k) for k in range(1, self.place.ranks)]
        self.sum = add(block(0), *parts)
        return [self.sum]

    def finish(self):
        total = self.sum
        if self.short:
            other = hop(total, "context", 2)
            both = add(total, other[::-1])
            far = hop(both, "context", 1)
            parts = [both[0], far[0], both[1], far[1]]
        else:
            second = hop(total, "context", 2)
            parts = [total, hop(total, "context", 1), second, hop(second, "context", 1)]
        return ordered(parts, self.place.context).astype(F32)


class Layout:
    def __init__(self, place, clips, live):
        self.place = place
        self.batches, self.frames, self.places = clips.shape[:3]
        ranks = place.ranks
        self.whole = 1 if place.paired else self.batches
        self.split = self.batches - self.whole
        self.alive = live > 0
        self.first = -(-self.whole * self.places // ranks)
        self.later = -(-self.split * self.places // (2 * ranks))
        self.room = max(32, round_up(self.first + self.later, 16))
        self.block = self.frames * self.room
        self.place_rows = ranks * self.block
        self.units = self.whole * self.frames + self.split
        self.frame_rows = round_up(self.units * self.places, 16)
        self.natural_blocks = self.batches * self.frames
        self.sent = round_up(self.frames * self.first + self.later, 16)
        self.sent_pair = round_up(self.later, 16)

    def label(self, batch, frame, spot):
        return (batch * self.frames * self.place.ranks + frame) * self.places + spot

    def place_labels(self, shard, tensor, k):
        frame = self.frames * (tensor ^ k) + jnp.arange(self.frames)[:, None]
        slot = jnp.arange(self.room)[None]
        spot = self.first * tensor + slot
        whole = slot < self.first
        labels = self.label(spot // self.places, frame, spot % self.places)
        labels = jnp.where(whole & (spot < self.whole * self.places), labels, -1)
        if self.split:
            flat = self.later * (self.place.ranks * shard + tensor) + slot - self.first
            inside = (slot >= self.first) & (slot < self.first + self.later)
            inside = inside & (flat < self.split * self.places)
            other = self.label(self.whole + flat // self.places, frame, flat % self.places)
            labels = jnp.where(inside, other, labels)
        return labels, jnp.broadcast_to(whole, labels.shape)

    def frame_labels(self, shard, tensor):
        row = jnp.arange(self.frame_rows)
        unit, spot = row // self.places, row % self.places
        whole = unit < self.whole * self.frames
        labels = self.label(
            unit // self.frames, self.frames * tensor + unit % self.frames, spot
        )
        later = self.label(
            self.whole + unit - self.whole * self.frames, self.frames * tensor + shard, spot
        )
        labels = jnp.where(whole, labels, later)
        return jnp.where(unit < self.units, labels, -1), whole

    def natural_labels(self, tensor):
        batch = jnp.arange(self.batches)[:, None, None]
        frame = self.frames * tensor + jnp.arange(self.frames)[None, :, None]
        spot = jnp.arange(WINDOW)[None, None]
        return jnp.where(spot < self.places, self.label(batch, frame, spot), -1)

    def held(self, labels):
        batch = jnp.maximum(labels, 0) // (self.frames * self.place.ranks * self.places)
        return self.living(labels) | (batch < self.whole)

    def living(self, labels):
        batch = jnp.maximum(labels, 0) // (self.frames * self.place.ranks * self.places)
        return jnp.any((batch[..., None] == jnp.arange(self.batches)) & self.alive, -1)


def one_hot(targets, sources):
    targets = jnp.concatenate([item.reshape(-1) for item in targets])
    sources = jnp.concatenate([item.reshape(-1) for item in sources])
    sources = jnp.where(sources < 0, -2, sources)
    return (targets[:, None] == sources[None]).astype(LOW)


def call(body, outs, ins, scalars, flops=0, scratch=(), after=(), name=None):
    given, count = body, len(ins)
    if after:
        body = lambda scalars, *refs: given(scalars, *refs[:count], *refs[count + len(after) :])
    moved = sum(item.size * item.dtype.itemsize for item in list(outs) + list(ins))
    spec = pl.BlockSpec(memory_space=pltpu.VMEM)
    return pl.pallas_call(
        body,
        name=name,
        out_shape=tuple(outs),
        in_specs=[pl.BlockSpec(memory_space=pltpu.SMEM)]
        + [spec] * len(ins)
        + [pl.BlockSpec(memory_space=pl.ANY)] * len(after),
        out_specs=(spec,) * len(outs),
        scratch_shapes=list(scratch),
        compiler_params=pltpu.CompilerParams(vmem_limit_bytes=VMEM_BYTES),
        cost_estimate=pl.CostEstimate(flops=flops, bytes_accessed=moved, transcendentals=0),
    )(scalars, *ins, *after)


def shape(*dims, dtype=LOW):
    return jax.ShapeDtypeStruct(dims, dtype)


def nn(first, second):
    return lax.dot_general(first, second, (((1,), (0,)), ((), ())), preferred_element_type=F32)


def nt(first, second):
    return lax.dot_general(first, second, (((1,), (1,)), ((), ())), preferred_element_type=F32)


def tn(first, second):
    return lax.dot_general(first, second, (((0,), (0,)), ((), ())), preferred_element_type=F32)


def swapper(scalars, paired):
    def swap(values):
        if not paired:
            return values
        half = values.shape[-1] // 2
        other = jnp.concatenate([values[:, half:], values[:, :half]], -1)
        return jnp.where(scalars[0] == 0, values, other)

    return swap


def unit_of(values):
    centred = values - jnp.mean(values, -1, keepdims=True)
    inverse = lax.rsqrt(jnp.mean(centred * centred, -1, keepdims=True) + EPS)
    return (centred * inverse, inverse)


def norm_back(grad, unit, inverse, gain):
    scaled = grad * gain
    inner = (
        scaled
        - jnp.mean(scaled, -1, keepdims=True)
        - unit * jnp.mean(scaled * unit, -1, keepdims=True)
    )
    return (
        inverse * inner,
        jnp.sum(grad * unit, 0, keepdims=True),
        jnp.sum(grad, 0, keepdims=True),
    )


def softmax(scores):
    weights = jnp.exp(scores - jnp.max(scores, -1, keepdims=True))
    return weights / jnp.sum(weights, -1, keepdims=True)


def score_back(probs, prob_grad):
    inner = jnp.sum(probs * prob_grad, -1, keepdims=True)
    return (probs * (prob_grad - inner)).astype(LOW)


def half_lanes(width):
    lane = lax.broadcasted_iota(jnp.int32, (1, width), 1)
    return [(lane // HEAD_DIM == e).astype(F32) for e in range(2)]


def column_sum(values):
    return jnp.sum(values.astype(F32), 0, keepdims=True)


def rows_at(start, size):
    return pl.ds(pl.multiple_of(start, 16), size)


class Program:
    def __init__(self, place, layout, width, group, scalars):
        self.place, self.layout, self.width, self.group = place, layout, width, group
        self.scalars = scalars
        self.ranks, self.quarters = place.ranks, place.quarters
        self.piece = group // self.quarters
        self.heads = group // HEAD_DIM
        self.all_heads = group * self.ranks
        spot = np.arange(layout.place_rows) % layout.room
        self.same_place = jnp.asarray(
            np.where(spot[:, None] == spot[None], 0, HIDE).astype(np.float32)
        )

    def call(self, body, outs, ins, flops=0, scratch=(), after=()):
        name = body.__qualname__.split(".")[1]
        return call(body, outs, ins, self.scalars, flops, scratch, after, name)


    def send_rows(self, clips, cotangents, matrix, targets):
        lay, width = self.layout, self.width
        count, split = lay.natural_blocks, lay.split
        first = lay.whole * lay.frames

        def body(scalars, clips_ref, grads_ref, matrix_ref, *refs):
            sent, refs = refs[:targets], refs[targets:]
            rows = refs[-1]
            rows[...] = jnp.zeros_like(rows)
            for item in range(count):
                rows[item * WINDOW : item * WINDOW + lay.places] = clips_ref[item]
            for item in range(targets):
                part = matrix_ref[item * lay.block : (item + 1) * lay.block]
                sent[item][...] = nn(part, rows[...]).astype(LOW)
            for index, source in enumerate((clips_ref, grads_ref) if split else ()):
                for item in range(split):
                    frame = first + lay.frames * item + 1 - scalars[0]
                    refs[index][item] = source[frame]

        outs = [shape(lay.block, width)] * targets
        if split:
            outs += [shape(split, lay.places, width)] * 2
        return self.call(
            body, outs, [clips, cotangents, matrix], scratch=[pltpu.VMEM((count * WINDOW, width), LOW)]
        )

    def frames_of(self, clips, others, matrix):
        lay, width = self.layout, self.width
        count, split = lay.natural_blocks, lay.split

        def body(scalars, clips_ref, *refs):
            matrix_ref, out_ref, rows = refs[-3:]
            rows[...] = jnp.zeros_like(rows)
            for item in range(count):
                rows[item * WINDOW : item * WINDOW + lay.places] = clips_ref[item]
            for item in range(split):
                start = (count + item) * WINDOW
                rows[start : start + lay.places] = refs[0][item]
            out_ref[...] = nn(matrix_ref[...], rows[...]).astype(LOW)

        return self.call(
            body,
            [shape(lay.frame_rows, width)],
            [clips] + ([others] if split else []) + [matrix],
            scratch=[pltpu.VMEM(((count + split) * WINDOW, width), LOW)],
        )[0]


    def temporal(self, blocks, pairs, keep, pieces, along, shift, wait=()):
        lay, width = self.layout, self.width
        rows, ranks = lay.place_rows, self.ranks
        wide = 3 * self.all_heads
        split = lay.split > 0

        def body(scalars, *refs):
            refs = list(refs)
            take = lambda n: [refs.pop(0) for _ in range(n)]
            block_refs, pair_refs = take(ranks), take(ranks if split else 0)
            keep_ref, piece_refs, along_ref, shift_ref, same = (
                take(1)[0], take(self.quarters), take(1)[0], take(1)[0], take(1)[0],
            )
            sent, sent_pair = take(ranks), take(ranks if split else 0)
            normed_ref, rows_ref, qkv, mixed, win, wout = take(6)
            swap = swapper(scalars, self.place.paired)
            for j in range(self.quarters):
                spot = scalars[1] ^ j
                for k in range(ranks):
                    for c in range(3):
                        at = c * self.all_heads + k * self.group + spot * self.piece
                        win[rows_at(at, self.piece)] = piece_refs[j][
                            k, c * self.piece : (c + 1) * self.piece
                        ]
                    at = k * self.group + spot * self.piece
                    wout[rows_at(at, self.piece)] = piece_refs[j][
                        k, 3 * self.piece : 4 * self.piece
                    ]
            start = jnp.concatenate([ref[...] for ref in block_refs]).astype(F32)
            start = jnp.where(keep_ref[:, 0:1] > 0, start, 0)
            if split:
                other = jnp.concatenate([ref[...] for ref in pair_refs]).astype(F32)
                start = jnp.where(keep_ref[:, 1:2] > 0, other, start)
            rows_ref[...] = start.astype(LOW)
            unit, _ = unit_of(start)
            normed_ref[...] = swap(unit * along_ref[0:1] + along_ref[3:4]).astype(LOW)

            @pl.loop(0, wide // 256)
            def _(n):
                at = pl.ds(pl.multiple_of(n * 256, 256), 256)
                qkv[:, at] = (nt(normed_ref[...], win[at]) + shift_ref[:, at]).astype(LOW)

            @pl.loop(0, self.all_heads // 128)
            def _(n):
                lanes = lambda c: pl.ds(pl.multiple_of(c * self.all_heads + n * 128, 128), 128)
                query, key, value = (qkv[:, lanes(c)] for c in range(3))
                total = jnp.zeros((rows, 128), F32)
                for mask in half_lanes(128):
                    scores = nt(query * mask.astype(LOW), key) * SCALE + same[...]
                    total = total + nn(softmax(scores).astype(LOW), value) * mask
                mixed[:, lanes(0)] = total.astype(LOW)

            out = swap(nn(mixed[...], wout[...])) + along_ref[6:7]
            for k in range(ranks):
                part = out[k * lay.block : (k + 1) * lay.block]
                sent[k][...] = part.astype(LOW)
                if split:
                    pair = jnp.where(scalars[0] == 0, part[lay.room :], part[: lay.room])
                    sent_pair[k][...] = pair.astype(LOW)

        outs = [shape(lay.block, width)] * ranks
        if split:
            outs += [shape(lay.room, width)] * ranks
        outs += [
            shape(rows, width),
            shape(rows, width),
            shape(rows, wide),
            shape(rows, self.all_heads),
            shape(wide, width),
            shape(self.all_heads, width),
        ]
        ins = list(blocks) + list(pairs) + [keep] + list(pieces) + [along, shift, self.same_place]
        flops = 2 * rows * width * (wide + self.all_heads) + 4 * rows * rows * self.all_heads
        outs = self.call(body, outs, ins, flops, after=wait)
        sent, outs = outs[:ranks], outs[ranks:]
        if split:
            sent_pair, outs = outs[:ranks], outs[ranks:]
        else:
            sent_pair = ()
        return sent, sent_pair, outs

    def temporal_back(self, sources, matrix, qkv, mixed, wout, wait=()):
        lay, width = self.layout, self.width
        rows, wide = lay.place_rows, 3 * self.all_heads

        def body(scalars, *refs):
            source_refs = refs[: len(sources)]
            matrix_ref, qkv_ref, mixed_ref, wout_ref, same, grad_ref, out_ref, part = refs[
                len(sources) :
            ]
            swap = swapper(scalars, self.place.paired)
            source = jnp.concatenate([ref[...] for ref in source_refs])
            grad_ref[...] = swap(nn(matrix_ref[...], source)).astype(LOW)
            part[...] = nt(grad_ref[...], wout_ref[...]).astype(LOW)

            @pl.loop(0, self.all_heads // 128)
            def _(n):
                lanes = lambda c: pl.ds(pl.multiple_of(c * self.all_heads + n * 128, 128), 128)
                query, key, value = (qkv_ref[:, lanes(c)] for c in range(3))
                grad = part[:, lanes(0)]
                totals = [jnp.zeros((rows, 128), F32) for _ in range(3)]
                for mask in half_lanes(128):
                    low = mask.astype(LOW)
                    probs = softmax(nt(query * low, key) * SCALE + same[...])
                    scored = score_back(probs, nt(grad * low, value))
                    for c, item in enumerate(
                        (
                            nn(scored, key) * SCALE,
                            tn(scored, query) * SCALE,
                            tn(probs.astype(LOW), grad),
                        )
                    ):
                        totals[c] = totals[c] + item * mask
                for c in range(3):
                    out_ref[:, lanes(c)] = totals[c].astype(LOW)

        outs = [shape(rows, width), shape(rows, wide)]
        ins = list(sources) + [matrix, qkv, mixed, wout, self.same_place]
        flops = 2 * rows * width * self.all_heads + 10 * rows * rows * self.all_heads
        return self.call(
            body, outs, ins, flops, [pltpu.VMEM((rows, self.all_heads), LOW)], wait
        )

    def temporal_weights(self, qkv_grad, normed, mixed, out_grad, vectors):
        lay, width = self.layout, self.width
        rows, ranks = lay.place_rows, self.ranks

        extra = vectors.shape[1]

        def body(scalars, grad_ref, normed_ref, mixed_ref, out_ref, vectors_ref, *pieces):
            for j in range(self.quarters):
                pieces[j][:, 4 * self.piece :] = vectors_ref[...]

            def put(total, k, c):
                for j in range(self.quarters):
                    at = rows_at((scalars[1] ^ j) * self.piece, self.piece)
                    pieces[j][k, c * self.piece : (c + 1) * self.piece] = total[at]

            def inner(total):
                for c in range(3):
                    for k in range(ranks):
                        at = c * self.all_heads + k * self.group
                        part = tn(grad_ref[:, at : at + self.group], normed_ref[...])
                        total[...] = part.astype(LOW)
                        put(total, k, c)
                for k in range(ranks):
                    at = k * self.group
                    part = tn(mixed_ref[:, at : at + self.group], out_ref[...])
                    total[...] = part.astype(LOW)
                    put(total, k, 3)

            pl.run_scoped(inner, pltpu.VMEM((self.group, width), LOW))

        outs = [shape(ranks, 4 * self.piece + extra, width)] * self.quarters
        flops = 8 * rows * width * self.all_heads
        return self.call(body, outs, [qkv_grad, normed, mixed, out_grad, vectors], flops)

    def temporal_input(self, qkv_grad, win, start, along):
        lay, width = self.layout, self.width
        ranks = self.ranks

        def body(scalars, grad_ref, win_ref, start_ref, along_ref, *refs):
            sent, sums, pair_sums = refs[:ranks], refs[ranks], refs[ranks + 1]
            pair_sums[...] = column_sum(grad_ref[...])
            swap = swapper(scalars, self.place.paired)
            unit, inverse = unit_of(start_ref[...].astype(F32))
            grad = swap(nn(grad_ref[...], win_ref[...]))
            back, gain, shift = norm_back(grad, unit, inverse, along_ref[0:1])
            sums[0:1] = gain
            sums[1:2] = shift
            for k in range(ranks):
                sent[k][...] = back[k * lay.block : (k + 1) * lay.block].astype(LOW)

        outs = [shape(lay.block, width)] * ranks + [shape(2, width, dtype=F32)]
        outs += [shape(1, 3 * self.all_heads, dtype=F32)]
        flops = 6 * lay.place_rows * width * self.all_heads
        outs = self.call(body, outs, [qkv_grad, win, start, along], flops)
        return outs[:-2], outs[-2], outs[-1]


    def spatial_in(self, sources, matrix, start, pieces, along, shift, wait=()):
        lay, width = self.layout, self.width
        rows, ranks, quarters = lay.frame_rows, self.ranks, self.quarters
        piece, group = self.piece, self.group

        def body(scalars, *refs):
            refs = list(refs)
            take = lambda n: [refs.pop(0) for _ in range(n)]
            source_refs = take(len(sources))
            matrix_ref, start_ref = take(2)
            piece_refs = take(quarters)
            along_ref, shift_ref = take(2)
            after_ref, temporal_ref, normed_ref = take(3)
            qkv_refs = take(quarters)
            win, wout, fc = take(3)
            swap = swapper(scalars, self.place.paired)
            for i in range(quarters):
                spot = scalars[1] ^ i
                for j in range(quarters):
                    k = scalars[1] ^ j
                    for c in range(3):
                        at = j * 3 * group + c * group + spot * piece
                        win[rows_at(at, piece)] = piece_refs[i][k, c * piece : (c + 1) * piece]
                    at = j * group + spot * piece
                    wout[rows_at(at, piece)] = piece_refs[i][k, 3 * piece : 4 * piece]
                for k in range(ranks):
                    at = (scalars[2] ^ k) * group + spot * piece
                    fc[rows_at(at, piece)] = piece_refs[i][k, 4 * piece : 5 * piece]
            source = jnp.concatenate([ref[...] for ref in source_refs])
            temporal = swap(nn(matrix_ref[...], source)).astype(LOW)
            temporal_ref[...] = temporal
            after = start_ref[...].astype(F32) + nt(temporal, fc[...]) + along_ref[7:8]
            after_ref[...] = after
            unit, _ = unit_of(after)
            normed = swap(unit * along_ref[1:2] + along_ref[4:5]).astype(LOW)
            normed_ref[...] = normed
            for j in range(quarters):
                at = slice(j * 3 * group, (j + 1) * 3 * group)
                qkv_refs[j][...] = (nt(normed, win[at]) + shift_ref[:, at]).astype(LOW)

        outs = [shape(rows, width, dtype=F32), shape(rows, width), shape(rows, width)]
        outs += [shape(rows, 3 * group)] * quarters
        outs += [
            shape(3 * self.all_heads, width),
            shape(self.all_heads, width),
            shape(width, width),
        ]
        ins = list(sources) + [matrix, start] + list(pieces) + [along, shift]
        flops = 2 * rows * width * (3 * self.all_heads + width)
        outs = self.call(body, outs, ins, flops, after=wait)
        return outs[:3], outs[3 : 3 + quarters], outs[3 + quarters :]

    def windows(self, refs, n):
        at = rows_at(n * (WINDOW - 16), WINDOW)
        return jnp.concatenate([ref[at] for ref in refs])

    def window_mask(self, n, axis):
        size = self.quarters * WINDOW
        dims = (size, 1) if axis == 0 else (1, size)
        index = lax.broadcasted_iota(jnp.int32, dims, axis) & (WINDOW - 1)
        start = n * (self.layout.places - WINDOW + 16)
        return (index >= start) & (index < start + self.layout.places)

    def put_windows(self, refs, n, values, mask):
        for j, ref in enumerate(refs):
            at = rows_at(n * (WINDOW - 16), WINDOW)
            part = slice(j * WINDOW, (j + 1) * WINDOW)
            old = ref[at].astype(F32)
            ref[at] = jnp.where(mask[part], values[part], old).astype(LOW)

    def spatial(self, qkv, wait=()):
        lay, quarters, group = self.layout, self.quarters, self.group

        def body(scalars, *refs):
            qkv_refs, out_refs = refs[:quarters], refs[quarters:]
            for ref in out_refs:
                ref[...] = jnp.zeros_like(ref)

            @pl.loop(0, lay.units)
            def _(n):
                rows = self.windows(qkv_refs, n)
                hide = jnp.where(self.window_mask(n, 1), 0.0, HIDE)
                parts = []
                for h in range(self.heads):
                    query, key, value = (
                        rows[:, c * group + h * HEAD_DIM : c * group + (h + 1) * HEAD_DIM]
                        for c in range(3)
                    )
                    probs = softmax(nt(query, key) * SCALE + hide)
                    parts.append(nn(probs.astype(LOW), value))
                mask = self.window_mask(n, 0)
                self.put_windows(out_refs, n, jnp.concatenate(parts, -1), mask)

        outs = [shape(lay.frame_rows, group)] * quarters
        size = quarters * WINDOW
        return self.call(body, outs, list(qkv), 4 * lay.units * size * size * group, after=wait)

    def spatial_back(self, qkv, grads, wait=()):
        lay, quarters, group = self.layout, self.quarters, self.group

        def body(scalars, *refs):
            qkv_refs, grad_refs = refs[:quarters], refs[quarters : 2 * quarters]
            out_refs = refs[2 * quarters :]
            for ref in out_refs:
                ref[...] = jnp.zeros_like(ref)

            @pl.loop(0, lay.units)
            def _(n):
                rows = self.windows(qkv_refs, n)
                mask = self.window_mask(n, 0)
                grads = self.windows(grad_refs, n) * mask.astype(F32).astype(LOW)
                hide = jnp.where(self.window_mask(n, 1), 0.0, HIDE)
                parts = [[], [], []]
                for h in range(self.heads):
                    query, key, value = (
                        rows[:, c * group + h * HEAD_DIM : c * group + (h + 1) * HEAD_DIM]
                        for c in range(3)
                    )
                    grad = grads[:, h * HEAD_DIM : (h + 1) * HEAD_DIM]
                    probs = softmax(nt(query, key) * SCALE + hide)
                    scored = score_back(probs, nt(grad, value))
                    parts[0].append(nn(scored, key) * SCALE)
                    parts[1].append(tn(scored, query) * SCALE)
                    parts[2].append(tn(probs.astype(LOW), grad))
                values = jnp.concatenate(parts[0] + parts[1] + parts[2], -1)
                self.put_windows(out_refs, n, values, mask)

        outs = [shape(lay.frame_rows, 3 * group)] * quarters
        size = quarters * WINDOW
        flops = 10 * lay.units * size * size * group
        return self.call(body, outs, list(qkv) + list(grads), flops, after=wait)

    def spatial_out(self, mixed, wout, after, grad, along, wait=()):
        lay, width, group = self.layout, self.width, self.group
        rows, quarters = lay.frame_rows, self.quarters

        def body(scalars, *refs):
            mixed_refs = refs[:quarters]
            wout_ref, after_ref, grad_ref, along_ref, out_ref, normed_ref, low_ref = refs[quarters:]
            swap = swapper(scalars, self.place.paired)
            total = jnp.zeros((rows, width), F32)
            for j in range(quarters):
                total = total + nn(mixed_refs[j][...], wout_ref[j * group : (j + 1) * group])
            after = after_ref[...] + swap(total) + along_ref[8:9]
            out_ref[...] = after
            unit, _ = unit_of(after)
            normed_ref[...] = swap(unit * along_ref[2:3] + along_ref[5:6]).astype(LOW)
            low_ref[...] = swap(grad_ref[...].astype(F32)).astype(LOW)

        outs = [shape(rows, width, dtype=F32), shape(rows, width), shape(rows, width)]
        ins = list(mixed) + [wout, after, grad, along]
        return self.call(body, outs, ins, 2 * rows * width * self.all_heads, after=wait)

    def feed_forward(self, normed, grad, ups, downs, shifts, totals):
        lay, width = self.layout, self.width
        rows, count = lay.frame_rows, len(ups)
        hidden = ups[0].shape[0]
        tile = 256
        steps = hidden // tile
        at = lambda n, item: jnp.clip(n - item * steps, 0, steps - 1)

        def body(scalars, normed_ref, grad_ref, *refs):
            refs = list(refs)
            take = lambda n: [refs.pop(0) for _ in range(n)]
            up_refs, down_refs, shift_refs = take(count), take(count), take(count)
            before = take(2 if totals else 0)
            out_ref, back_ref = take(2)
            up_grads, down_grads, sums = take(count), take(count), take(count)
            n = pl.program_id(0)

            @pl.when(n == 0)
            def _():
                out_ref[...] = before[0][...] if totals else jnp.zeros_like(out_ref)
                back_ref[...] = before[1][...] if totals else jnp.zeros_like(back_ref)

            def work(item):
                up, down = up_refs[item][...], down_refs[item][0]
                values = nt(normed_ref[...], up) + shift_refs[item][...]
                half = 0.5 * (1.0 + lax.erf(values * SQRT_HALF))
                active = (values * half).astype(LOW)
                slope = half + values * jnp.exp(-0.5 * values * values) * INV_ROOT_TAU
                out_ref[...] += nn(active, down)
                down_grads[item][...] = tn(active, grad_ref[...]).astype(LOW)
                hidden_grad = (nt(grad_ref[...], down) * slope).astype(LOW)
                up_grads[item][...] = tn(hidden_grad, normed_ref[...]).astype(LOW)
                back_ref[...] += nn(hidden_grad, up)
                sums[item][...] = column_sum(hidden_grad)

            for item in range(count):
                pl.when(n // steps == item)(lambda item=item: work(item))

        whole = pl.BlockSpec((rows, width), lambda n: (0, 0))
        up_specs = [pl.BlockSpec((tile, width), lambda n, i=i: (at(n, i), 0)) for i in range(count)]
        down_specs = [
            pl.BlockSpec((1, tile, width), lambda n, i=i, k=k: (k, at(n, i), 0))
            for i, (_, k) in enumerate(downs)
        ]
        line_specs = [pl.BlockSpec((1, tile), lambda n, i=i: (0, at(n, i))) for i in range(count)]
        outs = [shape(rows, width, dtype=F32)] * 2
        outs += [shape(hidden, width)] * (2 * count) + [shape(1, hidden, dtype=F32)] * count
        ins = [normed, grad] + list(ups) + [item for item, _ in downs] + list(shifts)
        ins += list(totals or ())
        got = pl.pallas_call(
            body,
            name="feed_forward",
            grid=(count * steps,),
            out_shape=tuple(outs),
            in_specs=[pl.BlockSpec(memory_space=pltpu.SMEM), whole, whole]
            + up_specs
            + down_specs
            + line_specs
            + [whole] * (2 if totals else 0),
            out_specs=tuple([whole, whole] + up_specs + up_specs + line_specs),
            compiler_params=pltpu.CompilerParams(vmem_limit_bytes=VMEM_BYTES),
            cost_estimate=pl.CostEstimate(
                flops=12 * rows * width * hidden * count,
                bytes_accessed=2 * sum(item.size * 2 for item in ins),
                transcendentals=0,
            ),
        )(self.scalars, *ins)
        return got[:2], got[2 : 2 + count], got[2 + count : 2 + 2 * count], got[2 + 2 * count :]

    def feed_forward_back(self, after, out, back, grad, mixed, wout, along):
        lay, width, group = self.layout, self.width, self.group
        rows, quarters = lay.frame_rows, self.quarters

        def body(scalars, after_ref, out_ref, back_ref, grad_ref, wout_ref, along_ref, *refs):
            mixed_refs, refs = refs[:quarters], refs[quarters:]
            layer_ref, total_ref, sums, wout_grad = refs[:4]
            mixed_grads = refs[4:]
            swap = swapper(scalars, self.place.paired)
            after = after_ref[...]
            layer_ref[...] = (after + swap(out_ref[...]) + along_ref[9:10]).astype(LOW)
            unit, inverse = unit_of(after)
            back, gain, shift = norm_back(swap(back_ref[...]), unit, inverse, along_ref[2:3])
            grad = grad_ref[...].astype(F32)
            total = grad + back
            total_ref[...] = total
            low = total.astype(LOW)
            sums[0:1] = gain
            sums[1:2] = shift
            sums[2:3] = column_sum(low)
            sums[3:4] = column_sum(grad)
            low = swap(low.astype(F32)).astype(LOW)
            for j in range(quarters):
                at = slice(j * group, (j + 1) * group)
                mixed_grads[j][...] = nt(low, wout_ref[at]).astype(LOW)
                wout_grad[at] = tn(mixed_refs[j][...], low).astype(LOW)

        outs = [
            shape(rows, width),
            shape(rows, width, dtype=F32),
            shape(4, width, dtype=F32),
            shape(self.all_heads, width),
        ] + [shape(rows, group)] * quarters
        ins = [after, out, back, grad, wout, along] + list(mixed)
        outs = self.call(body, outs, ins, 4 * rows * width * self.all_heads)
        return outs[:4], outs[4:]

    def spatial_input(self, qkv_grads, win, after, total, along, fc, matrix, wait=()):
        lay, width, group = self.layout, self.width, self.group
        rows, quarters, ranks = lay.frame_rows, self.quarters, self.ranks
        split = lay.split > 0

        def body(scalars, *refs):
            grad_refs = refs[:quarters]
            win_ref, after_ref, total_ref, along_ref, fc_ref, matrix_ref = refs[
                quarters : quarters + 6
            ]
            out_ref, low_ref, sums = refs[quarters + 6 : quarters + 9]
            sent = refs[quarters + 9 :]
            swap = swapper(scalars, self.place.paired)
            grad = jnp.zeros((rows, width), F32)
            for j in range(quarters):
                at = slice(j * 3 * group, (j + 1) * 3 * group)
                grad = grad + nn(grad_refs[j][...], win_ref[at])
            unit, inverse = unit_of(after_ref[...])
            back, gain, shift = norm_back(swap(grad), unit, inverse, along_ref[1:2])
            total = total_ref[...] + back
            out_ref[...] = total
            low = total.astype(LOW)
            low_ref[...] = low
            temporal = swap(nn(low, fc_ref[...])).astype(LOW)
            sums[0:1] = gain
            sums[1:2] = shift
            sums[2:3] = column_sum(temporal)
            sums[3:4] = column_sum(low)
            at = 0
            for ref in sent:
                size = ref.shape[0]
                ref[...] = nn(matrix_ref[at : at + size], temporal).astype(LOW)
                at += size

        outs = [
            shape(rows, width, dtype=F32),
            shape(rows, width),
            shape(4, width, dtype=F32),
        ]
        outs += [shape(lay.sent, width)] * ranks
        outs += [shape(lay.sent_pair, width)] * (ranks if split else 0)
        ins = list(qkv_grads) + [win, after, total, along, fc, matrix]
        outs = self.call(body, outs, ins, 2 * rows * width * (3 * self.all_heads + width), after=wait)
        return outs[:3], outs[3 : 3 + ranks], outs[3 + ranks :]

    def spatial_weights(self, qkv_grads, normed, wout_grad, low, temporal):
        lay, width, group, piece = self.layout, self.width, self.group, self.piece
        rows, quarters, ranks = lay.frame_rows, self.quarters, self.ranks

        def body(scalars, *refs):
            grad_refs = refs[:quarters]
            normed_ref, wout_ref, low_ref, temporal_ref = refs[quarters : quarters + 4]
            pieces = refs[quarters + 4 : 2 * quarters + 4]
            sums = refs[2 * quarters + 4]

            def inner(total, fc):
                for j in range(quarters):
                    k = scalars[1] ^ j
                    at = slice(j * 3 * group, (j + 1) * 3 * group)
                    sums[:, at] = column_sum(grad_refs[j][...])
                    total[...] = tn(grad_refs[j][...], normed_ref[...]).astype(LOW)
                    for i in range(quarters):
                        spot = (scalars[1] ^ i) * piece
                        for c in range(3):
                            pieces[i][k, c * piece : (c + 1) * piece] = total[
                                rows_at(c * group + spot, piece)
                            ]
                        pieces[i][k, 3 * piece : 4 * piece] = wout_ref[
                            rows_at(j * group + spot, piece)
                        ]
                fc[...] = tn(low_ref[...], temporal_ref[...]).astype(LOW)
                for i in range(quarters):
                    for k in range(ranks):
                        at = (scalars[2] ^ k) * group + (scalars[1] ^ i) * piece
                        pieces[i][k, 4 * piece : 5 * piece] = fc[rows_at(at, piece)]

            pl.run_scoped(
                inner,
                pltpu.VMEM((3 * group, width), LOW),
                pltpu.VMEM((width, width), LOW),
            )

        outs = [shape(ranks, 5 * piece, width)] * quarters
        outs += [shape(1, 3 * self.all_heads, dtype=F32)]
        ins = list(qkv_grads) + [normed, wout_grad, low, temporal]
        flops = 2 * rows * width * (3 * self.all_heads + width)
        outs = self.call(body, outs, ins, flops)
        return outs[:-1], outs[-1]

    def natural(self, parts):
        lay, width = self.layout, self.width
        count = lay.natural_blocks
        counts = [len(rows) for _, rows in parts]

        def body(scalars, *refs):
            refs = list(refs)
            out_ref = refs.pop()
            total = jnp.zeros((count * WINDOW, width), F32)
            for size in counts:
                matrix = refs.pop(0)
                source = jnp.concatenate([refs.pop(0)[...] for _ in range(size)])
                total = total + nn(matrix[...], source)
            total = total.astype(LOW)
            for item in range(count):
                out_ref[item] = total[item * WINDOW : item * WINDOW + lay.places]

        ins = []
        for matrix, rows in parts:
            ins += [matrix] + list(rows)
        return self.call(body, [shape(count, lay.places, width)], ins)[0]


def body(
    clip_input,
    clip_slot,
    norm_gain,
    norm_shift,
    attention_in,
    attention_bias,
    attention_out,
    branch_bias,
    temporal_fc,
    hidden_in,
    hidden_bias,
    hidden_out,
    output_grad,
):
    place = Place()
    shards, quarters, ranks = place.shards, place.quarters, place.ranks
    shard, context, tensor = place.shard, place.context, place.tensor
    clips, live = clip_input[:, 0], clip_slot[:, 0]
    lay = Layout(place, clips, live)
    mask = live[:, None, None, None].astype(LOW)
    cotangents = output_grad[:, 0] * mask
    columns = attention_in.shape[1]
    width = columns * shards
    group = attention_in.shape[3]
    heads = group // HEAD_DIM
    hidden = hidden_in.shape[1]
    piece = group // quarters
    split = lay.split > 0
    scalars = jnp.stack([shard, context, tensor]).astype(jnp.int32)
    prog = Program(place, lay, width, group, scalars)

    vectors = jnp.concatenate(
        [norm_gain, norm_shift, branch_bias, attention_bias.reshape(-1, columns)]
        + [hidden_bias.reshape(-1, columns)]
    )
    if place.paired:
        both = jnp.stack([vectors, hop(vectors, "shard", 1)])
        both = jnp.where(shard == 0, both, both[::-1])
    else:
        both = lax.all_gather(vectors, "shard")
    along = jnp.swapaxes(both[:, :10], 0, 1).reshape(10, width).astype(F32)
    last = 10 + attention_bias.size // columns
    own = both[:, 10:]
    own = jnp.stack([own] + [hop(own, "tensor", k) for k in range(1, ranks)], 1).astype(F32)
    biases = own[:, :, : last - 10].reshape((shards, ranks) + attention_bias.shape)
    biases = jnp.transpose(biases, (2, 3, 1, 4, 0, 5)).reshape(2, 2, ranks, group)
    biases = jnp.stack([biases[:, 0], jnp.zeros_like(biases[:, 0]), biases[:, 1]], 1)
    shift_a = biases[0].reshape(1, -1)
    shift_b = jnp.swapaxes(biases[1], 0, 1)
    shift_b = jnp.stack([pick(shift_b, context ^ j) for j in range(quarters)]).reshape(1, -1)
    up_shift = own[:, :, last - 10 :].reshape((shards, ranks) + hidden_bias.shape)
    up_shift = jnp.transpose(up_shift, (1, 2, 0, 3)).reshape(ranks, quarters, -1)
    up_shift = [pick(up_shift, context ^ j, 1).reshape(1, -1) for j in range(quarters)]

    def in_block(weight):
        block = weight.reshape(columns, 3, quarters, piece)
        return jnp.transpose(block, (2, 1, 3, 0)).reshape(quarters, 3 * piece, columns)

    def in_quarters(rows):
        return rows.reshape(quarters, -1, rows.shape[-1])

    fc_block = lax.dynamic_slice_in_dim(temporal_fc, tensor * group, group, 1).T
    fc_block = in_quarters(fc_block)
    block_a = jnp.concatenate([in_block(attention_in[0]), in_quarters(attention_out[0])], 1)
    block_b = jnp.concatenate(
        [in_block(attention_in[1]), in_quarters(attention_out[1]), fc_block], 1
    )
    block_up = jnp.transpose(hidden_in.reshape(columns, quarters, -1), (1, 2, 0))
    gather_a, gather_b = Gather(place, block_a), Gather(place, block_b)
    gather_down = Gather(place, in_quarters(hidden_out), True)
    gather_up = Gather(place, block_up)
    gather_a.hops()
    gather_b.mine = tie(gather_b.mine, gather_a.blocks)
    gather_b.hops()
    gather_down.mine = tie(gather_down.mine, gather_b.blocks)
    gather_down.hops()
    gather_up.mine = tie(gather_up.mine, gather_down.blocks)
    gather_up.hops()
    for item in (gather_a, gather_b, gather_down, gather_up):
        item.columns()
        item.rows()
    pieces_a, pieces_b = gather_a.cores(), gather_b.cores()

    steps = [(0, k) for k in range(ranks)] + [(1, k) for k in range(ranks if split else 0)]

    def across(values, step):
        pair, k = step
        if pair:
            return hop_pair(values, k)
        return values if k == 0 else hop(values, "tensor", k)

    flip = lambda pair: 1 - shard if pair else shard
    natural = lay.natural_labels(tensor)
    alive = lay.held(natural)
    frame, frame_whole = lay.frame_labels(shard, tensor)
    sending = one_hot(
        [lay.place_labels(flip(pair), tensor ^ k, k)[0] for pair, k in steps], [natural]
    )
    here = [lay.place_labels(shard, tensor, k) for k in range(ranks)]
    here_labels = jnp.stack([labels for labels, _ in here])
    here_whole = jnp.stack([whole for _, whole in here])
    here_mine = (here_whole | lay.held(here_labels)) & (here_labels >= 0)
    keep = jnp.stack([here_mine, (here_labels >= 0) & ~here_mine], -1)
    keep = keep.reshape(-1, 2).astype(F32)
    start_sources = [jnp.where(alive, natural, -1)]
    if split:
        spot = jnp.arange(WINDOW)
        batch = jnp.arange(lay.whole, lay.batches)[:, None]
        others = lay.label(batch, lay.frames * tensor + shard, spot)
        others = jnp.where((spot < lay.places) & ~lay.held(others), others, -1)
        start_sources.append(others)
    starting = one_hot([frame], start_sources)

    def source_labels(step):
        pair, k = step
        labels, whole = lay.place_labels(flip(pair), tensor ^ k, k)
        return jnp.where(whole, -1, labels) if pair else labels

    returning = one_hot(
        [frame],
        [source_labels((0, k)) for k in range(ranks)]
        + [pick(source_labels((1, k)), shard) for k in range(ranks if split else 0)],
    )

    def packed(labels, whole_too, index):
        parts = [labels[:, : lay.first].reshape(-1)] if whole_too else []
        if split:
            parts.append(pick(labels, index)[lay.first : lay.first + lay.later])
        parts = jnp.concatenate(parts)
        size = lay.sent if whole_too else lay.sent_pair
        return jnp.pad(parts, (0, size - parts.shape[0]), constant_values=-1)

    leaving = one_hot(
        [
            packed(lay.place_labels(flip(pair), tensor ^ k, k)[0], not pair, shard)
            for pair, k in steps
        ],
        [frame],
    )
    arriving = one_hot(
        [labels for labels, _ in here],
        [packed(here[k][0], not pair, flip(pair)) for pair, k in steps],
    )
    home = jnp.where(lay.living(natural), natural, -1)
    homing = one_hot([home], [source_labels(step) for step in steps])
    ending = [one_hot([home], [frame])]
    if split:
        far, far_whole = lay.frame_labels(1 - shard, tensor)
        ending.append(one_hot([home], [jnp.where(far_whole, -1, far)]))

    flat = lambda rows: rows.reshape((-1,) + rows.shape[2:])
    clips, cotangents = flat(clips), flat(cotangents)
    sent = prog.send_rows(clips, cotangents, sending, len(steps))
    blocks = [across(rows, step) for rows, step in zip(sent, steps)]
    other_clips, other_grads = [hop(rows, "shard", 1) for rows in sent[len(steps) :]] or (None,) * 2
    start = prog.frames_of(clips, other_clips, starting)
    grad = prog.frames_of(cotangents, other_grads, starting)

    sent, sent_pair, kept = prog.temporal(
        blocks[:ranks], blocks[ranks:], keep, pieces_a, along, shift_a, [gather_b.first]
    )
    normed_a, start_a, qkv_a, mixed_a, win_a, wout_a = kept
    sources = [across(rows, step) for rows, step in zip(list(sent) + list(sent_pair), steps)]

    def to_groups(parts):
        return [parts[0]] + [hop(parts[j], "context", j) for j in range(1, quarters)]

    kept, qkv, weights_b = prog.spatial_in(
        sources, returning, start, pieces_b, along, shift_b, [gather_down.first, gather_up.blocks]
    )
    after_a, temporal, normed_b = kept
    win_b, wout_b, fc = weights_b
    qkv = to_groups(qkv)
    mixed = to_groups(prog.spatial(qkv, [gather_up.first]))
    downs, ups = gather_down.cores(), gather_up.cores()
    downs = [item.reshape(2, -1, width) for item in downs]
    ups = [item.reshape(-1, width) for item in ups]
    after_b, normed_c, low = prog.spatial_out(mixed, wout_b, after_a, grad, along)

    totals = None
    up_grads, down_grads, up_bias_grads = ([None] * quarters for _ in range(3))
    for pair in ((1, 3), (0, 2)):
        totals, *got = prog.feed_forward(
            normed_c,
            low,
            [ups[j] for j in pair],
            [(downs[j % 2], j // 2) for j in pair],
            [up_shift[j] for j in pair],
            totals,
        )
        for index, j in enumerate(pair):
            up_grads[j] = got[0][index].reshape(ranks, -1, width)
            down_grads[j] = got[1][index].reshape(ranks, -1, width)
            up_bias_grads[j] = got[2][index]
    reduce_down, reduce_up = Reduce(place, down_grads, True), Reduce(place, up_grads)
    kept, mixed_grads = prog.feed_forward_back(
        after_b, totals[0], totals[1], grad, mixed, wout_b, along
    )
    layer_rows, total, sums_c, wout_grad = kept
    wait = reduce_down.cores() + reduce_up.cores()

    mixed_grads = to_groups(mixed_grads)
    qkv_grads = to_groups(prog.spatial_back(qkv, mixed_grads, wait))
    reduce_down.rows()
    wait = reduce_down.columns() + reduce_up.rows()
    layer_out = [(ending[0], [layer_rows])]
    if split:
        layer_out.append((ending[1], [hop(layer_rows, "shard", 1)]))
    layer_out = prog.natural(layer_out)
    kept, sent, sent_pair = prog.spatial_input(
        qkv_grads, win_b, after_a, total, along, fc, leaving, wait
    )
    total, low_fc, sums_b = kept
    pieces, pair_b = prog.spatial_weights(qkv_grads, normed_b, wout_grad, low_fc, temporal)
    reduce_b = Reduce(place, pieces, True)
    wait = reduce_b.cores() + reduce_up.columns()
    sources = [across(rows, step) for rows, step in zip(list(sent) + list(sent_pair), steps)]
    out_grad_a, qkv_grad_a = prog.temporal_back(
        sources, arriving, qkv_a, mixed_a, wout_a, wait
    )
    reduce_down.hops()
    reduce_b.rows()
    reduce_b.columns()
    sent, sums_a, pair_a = prog.temporal_input(qkv_grad_a, win_a, start_a, along)
    back = [across(sent[k], (pair, k)) for pair, k in steps]

    sums = jnp.concatenate([sums_a, sums_b, sums_c])
    sums = jnp.stack([sums[k] for k in (0, 2, 6, 1, 3, 7, 4, 5, 8, 9)])
    pair_a = jnp.swapaxes(pair_a.reshape(3, ranks, group), 0, 1)
    pair_b = ordered([pair_b.reshape(quarters, 3, group)[j] for j in range(quarters)], context)
    inner = jnp.stack([pair_a, pair_b], 1)[:, :, ::2]
    inner = inner.reshape(ranks, 4 * heads, shards, HEAD_DIM // shards)
    inner = jnp.swapaxes(inner, 1, 2).reshape(ranks, 1, width)
    outer = ordered([item.reshape(ranks, -1) for item in up_bias_grads], context, 1)
    outer = outer.reshape(ranks, -1, shards, hidden_bias.shape[1])
    outer = jnp.swapaxes(outer, 1, 2).reshape(ranks, 1, width)
    vectors = [jnp.broadcast_to(sums, (ranks,) + sums.shape), inner, outer]
    vectors = jnp.concatenate(vectors, 1)
    if place.paired:
        flipped = jnp.concatenate([vectors[..., columns:], vectors[..., :columns]], -1)
        vectors = jnp.where(shard == 0, vectors, flipped)
    vectors = jnp.pad(vectors, ((0, 0), (0, 16 - vectors.shape[1]), (0, 0))).astype(LOW)
    pieces = prog.temporal_weights(qkv_grad_a, normed_a, mixed_a, out_grad_a, vectors)
    reduce_a = Reduce(place, pieces)
    reduce_up.hops()
    reduce_b.hops()
    for stage in ("cores", "rows", "columns", "hops"):
        getattr(reduce_a, stage)()
    total_up, total_down, total_b, total_a = (
        item.finish() for item in (reduce_up, reduce_down, reduce_b, reduce_a)
    )
    low_total = total.astype(LOW)
    input_grad = [(ending[0], [low_total])]
    if split:
        input_grad.append((ending[1], [hop(low_total, "shard", 1)]))
    input_grad.append((homing, back))
    input_grad = prog.natural(input_grad)

    def in_grad(total):
        part = total[:, : 3 * piece].reshape(quarters, 3, piece, columns)
        return jnp.transpose(part, (3, 1, 0, 2)).reshape(columns, 3, group)

    def out_grad(total):
        return total[:, 3 * piece : 4 * piece].reshape(group, columns)

    in_total = jnp.stack([in_grad(total_a), in_grad(total_b)])
    out_total = jnp.stack([out_grad(total_a), out_grad(total_b)])
    fc_total = total_b[:, 4 * piece :].reshape(group, columns).astype(LOW)
    fc_total = [fc_total] + [hop(fc_total, "tensor", k) for k in range(1, ranks)]
    fc_total = ordered(fc_total, tensor).reshape(width, columns).T.astype(F32)

    vectors = total_a[0, 4 * piece :]
    along, inner, outer = vectors[:10], vectors[10], vectors[11]
    rows_shape = clip_input.shape
    return (
        layer_out.reshape(rows_shape),
        input_grad.reshape(rows_shape),
        along[:3],
        along[3:6],
        in_total,
        inner.reshape(attention_bias.shape),
        out_total,
        along[6:],
        fc_total,
        total_up.reshape(hidden, columns).T,
        outer.reshape(hidden_bias.shape),
        total_down.reshape(hidden, columns),
    )


def solution(mesh):
    rows = P(None, "shard", "tensor", "context", None)
    weights = (
        P(None, "shard"),
        P(None, "shard"),
        P(None, "shard", None, "tensor"),
        P(None, None, "tensor", "shard"),
        P(None, "tensor", "shard"),
        P(None, "shard"),
        P("shard", None),
        P("shard", "tensor"),
        P("tensor", "shard"),
        P("tensor", "shard"),
    )
    return jax.shard_map(
        body,
        mesh=mesh,
        in_specs=(rows, P(None, "shard")) + weights + (rows,),
        out_specs=(rows, rows) + weights,
        check_vma=False,
    )
```

```python
import jax
import jax.numpy as jnp
import numpy as np
from jax import lax
from jax.experimental import pallas as pl
from jax.experimental.pallas import tpu as pltpu
from jax.sharding import PartitionSpec as P

HEAD_DIM = 64
WINDOW = 64
CHUNK = 32
EPS = 1e-06
SQRT_HALF = 0.7071067811865476
INV_ROOT_TAU = 0.3989422804014327
SCALE = HEAD_DIM**-0.5
HIDE = -1e30
LOW = jnp.bfloat16
F32 = jnp.float32
VMEM_BYTES = 60 * 2**20
PEAK = 1.15e9
COSTS = {
    "natural_last": 60,
    "send_rows": 6,
    "temporal_start": 10,
    "temporal": 30,
    "temporal_out": 6,
    "spatial_in": 8,
    "spatial": 20,
    "spatial_out": 8,
    "feed_forward": 26,
    "feed_forward_back": 10,
    "spatial_back": 28,
    "spatial_input": 20,
    "temporal_grad": 20,
    "temporal_back": 70,
    "temporal_input": 70,
    "group_weights": 0.2,
    "natural": 0.2,
    "out_weights": 0.2,
    "frames_of": 0.2,
}


def hop(values, axis, step):
    count = lax.axis_size(axis)
    return lax.ppermute(values, axis, [(i, i ^ step) for i in range(count)])


def hop_group(values):
    quarters, ranks = lax.axis_size("context"), lax.axis_size("tensor")
    pairs = [
        (c * ranks + i, c * ranks + (i ^ group_of(c))) for c in range(quarters) for i in range(ranks)
    ]
    return lax.ppermute(values, ("context", "tensor"), pairs)


def group_of(context):
    return 2 * (context % 2) + context // 2


def pick(values, index, axis=0):
    return lax.dynamic_index_in_dim(values, index, axis, keepdims=False)


def ordered(parts, me, axis=0):
    shape = list(parts[0].shape)
    shape.insert(axis, len(parts))
    out = jnp.zeros(shape, parts[0].dtype)
    for j, part in enumerate(parts):
        out = lax.dynamic_update_index_in_dim(out, part, me ^ j, axis)
    return out


def round_up(value, step):
    return -(-value // step) * step


class Place:
    def __init__(self):
        self.shard = lax.axis_index("shard")
        self.context = lax.axis_index("context")
        self.tensor = lax.axis_index("tensor")
        self.shards = lax.axis_size("shard")
        self.ranks = lax.axis_size("tensor")
        self.quarters = lax.axis_size("context")
        self.paired = self.shards == 2


def tie(values, *others):
    return lax.optimization_barrier((values,) + others)[0] if others else values


def add(*terms):
    total = terms[0].astype(F32)
    for term in terms[1:]:
        total = total + term.astype(F32)
    return total.astype(LOW)


class Gather:
    def __init__(self, place, mine):
        self.place = place
        self.parts = [mine] + [hop(mine, "tensor", k) for k in range(1, place.ranks)]

    def columns(self, *later):
        blocks = jnp.stack([tie(part, *later) for part in self.parts])
        if self.place.paired:
            self.parts = [blocks, hop(blocks, "shard", 1)]
        else:
            self.parts = [lax.all_gather(blocks, "shard", axis=2, tiled=True)]
        self.far = [hop(blocks, "context", 2)] if self.place.paired else []

    def rows(self, *later):
        self.far.append(hop(tie(self.parts[-1], *later), "context", 2))

    def cores(self, *later):
        join = lambda parts: jnp.concatenate([tie(part, *later) for part in parts], -1)
        self.first, second = join(self.parts), join(self.far)
        return [self.first, hop(self.first, "context", 1), second, hop(second, "context", 1)]


class ReduceHidden:
    def __init__(self, place, pieces):
        self.place = place
        self.kept = [pieces[0], pieces[2]]
        self.come = [hop(pieces[1], "context", 1), hop(pieces[3], "context", 1)]
        self.middle = pieces[0].shape[1] // 2
        self.half = pieces[0].shape[2] // (2 if place.paired else 1)

    def part(self, index, rows, columns):
        return add(self.kept[index][:, rows, columns], self.come[index][:, rows, columns])

    def cores(self, *later):
        self.come = [tie(item, *later) for item in self.come]
        top, low = slice(self.middle), slice(self.middle, None)
        left, right = slice(self.half), slice(self.half, None)
        out = []
        if self.place.paired:
            sent = jnp.stack([self.part(index, top, right) for index in range(2)])
            out.append(sent)
            self.come_top = hop(sent, "shard", 1)
        sent = self.part(1, low, slice(None))
        self.come_low = hop(sent, "context", 2)
        self.kept_top = lambda: jnp.stack([self.part(index, top, left) for index in range(2)])
        self.kept_low = lambda at: self.part(0, low, at)
        return out + [sent]

    def scatter(self, total):
        axis = total.ndim - 1
        return lax.psum_scatter(total, "shard", scatter_dimension=axis, tiled=True)

    def legs(self, *later):
        come = tie(self.come_low, *later)
        left, right = slice(self.half), slice(self.half, None)
        if self.place.paired:
            top = add(self.kept_top(), tie(self.come_top, *later))
            low = add(self.kept_low(left), come[..., left])
            sent = add(self.kept_low(right), come[..., right])
            self.come_low = hop(sent, "shard", 1)
        else:
            top = self.scatter(self.kept_top())
            low, sent, self.come_low = self.scatter(add(self.kept_low(left), come)), top, None
        self.top, self.low = top[0], low
        self.come_top = hop(top[1], "context", 2)
        return [top, low, sent]

    def both(self, *later):
        top = add(self.top, tie(self.come_top, *later))
        low = self.low if self.come_low is None else add(self.low, tie(self.come_low, *later))
        mine = jnp.concatenate([top, low], 1)
        self.kept = mine[0]
        self.come = [hop(mine[k], "tensor", k) for k in range(1, self.place.ranks)]
        return [mine]

    def hops(self, *later):
        self.sum = add(self.kept, *[tie(come, *later) for come in self.come])
        return [self.sum]

    def finish(self):
        return gather_context(self.place, self.sum)


def gather_context(place, mine):
    second = hop(mine, "context", 2)
    both = jnp.stack([mine, second])
    far = hop(both, "context", 1)
    return ordered([both[0], far[0], both[1], far[1]], place.context).astype(F32)


class ReduceShared:
    def __init__(self, place, pieces, each):
        self.place, self.each = place, each
        self.kept = [pieces[0], pieces[2]]
        self.come = [hop(pieces[1], "context", 1), hop(pieces[3], "context", 1)]

    def cores(self, *later):
        first, second = [add(a, tie(b, *later)) for a, b in zip(self.kept, self.come)]
        self.kept, self.come = first, hop(second, "context", 2)
        return [first, second]

    def rows(self, *later):
        come = tie(self.come, *later)
        if self.place.paired:
            half = come.shape[-1] // 2
            sent = add(self.kept[:, half:], come[:, half:])
            self.kept, self.come = add(self.kept[:, :half], come[:, :half]), hop(sent, "shard", 1)
            return [sent]
        self.kept = lax.psum_scatter(
            add(self.kept, come), "shard", scatter_dimension=1, tiled=True
        )
        self.come = None
        return [self.kept]

    def columns(self, *later):
        mine = self.kept if self.come is None else add(self.kept, tie(self.come, *later))
        ranks, each = self.place.ranks, self.each
        common = mine[ranks * each :]
        block = lambda k: jnp.concatenate([mine[k * each : (k + 1) * each], common])
        self.kept = block(0)
        self.come = [hop(block(k), "tensor", k) for k in range(1, ranks)]
        return [mine]

    def hops(self, *later):
        self.sum = add(self.kept, *[tie(come, *later) for come in self.come])
        return [self.sum]

    def finish(self):
        return gather_context(self.place, self.sum)


def sum_columns(place, kept, sent, *later):
    if place.paired:
        return add(kept, tie(hop(sent, "shard", 1), *later))
    return lax.psum_scatter(kept, "shard", scatter_dimension=1, tiled=True)


class SumContext:
    def __init__(self, place, total):
        self.core, self.shape = place.context % 2, total.shape
        halves = total.reshape(2, -1, total.shape[-1])
        self.kept, self.come = pick(halves, self.core), hop(pick(halves, 1 - self.core), "context", 1)

    def cores(self, *later):
        self.kept = add(self.kept, tie(self.come, *later))
        self.come = hop(self.kept, "context", 2)
        return [self.kept]

    def finish(self):
        half = add(self.kept, self.come)
        whole = ordered([half, hop(half, "context", 1)], self.core)
        return whole.reshape(self.shape).astype(F32)


class Layout:
    def __init__(self, place, clips):
        self.place = place
        self.batches, self.frames, self.places = clips.shape[:3]
        self.whole = 1 if place.paired else self.batches
        self.split = self.batches - self.whole
        self.first = self.whole * self.places
        self.later = -(-self.split * self.places // 2)
        self.slots = round_up(self.first + self.later, CHUNK)
        self.temporal_rows = self.frames * self.slots
        self.units = self.whole * self.frames + self.split
        self.frame_rows = round_up(self.units * self.places, 16)
        self.natural_blocks = self.batches * self.frames
        self.own = self.whole * self.frames * self.places // 16 * 16

    def label(self, batch, frame, spot):
        return (batch * self.frames * self.place.ranks + frame) * self.places + spot

    def split_labels(self, part, frames):
        flat = self.later * part + np.arange(self.later)[None]
        labels = self.label(
            self.whole + flat // self.places, np.asarray(frames)[:, None], flat % self.places
        )
        return np.where(flat < self.split * self.places, labels, -1)

    def frames_at(self, tensor):
        return self.frames * tensor + np.arange(self.frames)

    def temporal_labels(self, shard, tensor):
        frames = self.frames_at(tensor)
        slot = np.arange(self.first)[None]
        parts = [self.label(slot // self.places, frames[:, None], slot % self.places)]
        if self.split:
            parts.append(self.split_labels(shard, frames))
        labels = np.concatenate(parts, 1)
        spare = self.slots - labels.shape[1]
        return np.pad(labels, ((0, 0), (0, spare)), constant_values=-1)

    def frame_labels(self, shard, tensor, far=False):
        row = np.arange(self.frame_rows)
        unit, spot = row // self.places, row % self.places
        batch, frame = unit // self.frames, self.frames * tensor + unit % self.frames
        later = unit - self.whole * self.frames
        batch = np.where(later >= 0, self.whole + later, batch)
        frame = np.where(later >= 0, self.frames * tensor + shard, frame)
        inside = (unit < self.units) & ((later >= 0) | (not far))
        return np.where(inside, self.label(batch, frame, spot), -1)

    def natural_labels(self, tensor):
        batch = np.arange(self.batches)[:, None, None]
        frame = self.frames_at(tensor)[None, :, None]
        spot = np.arange(WINDOW)[None, None]
        return np.where(spot < self.places, self.label(batch, frame, spot), -1)

    def other_labels(self, shard, tensor):
        batch = np.arange(self.whole, self.batches)[:, None]
        spot = np.arange(WINDOW)[None]
        labels = self.label(batch, self.frames * tensor + shard, spot)
        return np.where(spot < self.places, labels, -1)

    def moves(self, shard, tensor):
        natural, frame = self.natural_labels(tensor), self.frame_labels(shard, tensor)
        temporal = self.temporal_labels(shard, tensor)
        moves = {
            "beginning": ([temporal], [natural]),
            "starting": ([frame], [natural]),
            "returning": ([frame], [temporal]),
            "arriving": ([temporal], [frame]),
            "homing": ([natural], [temporal]),
            "ending": ([natural], [frame]),
        }
        if self.split:
            frames, other = self.frames_at(tensor), 1 - shard

            def packed(part, frames):
                labels = self.split_labels(part, frames).reshape(-1)
                spare = round_up(labels.size, 16) - labels.size
                return np.pad(labels, (0, spare), constant_values=-1)

            mine, theirs = packed(shard, frames), packed(other, frames)
            moves["beginning"][1].append(mine)
            moves["starting"][1].append(self.other_labels(shard, tensor))
            moves["returning"][1].append(packed(other, [frames[shard]]))
            moves["arriving"][1].append(packed(shard, [frames[other]]))
            moves["homing"][1].append(theirs)
            moves["begin_far"] = ([theirs], [natural])
            moves["return_far"] = ([packed(shard, [frames[other]])], [temporal])
            moves["arrive_far"] = ([packed(other, [frames[shard]])], [frame])
            moves["home_far"] = ([mine], [temporal])
            moves["end_far"] = ([natural], [self.frame_labels(other, tensor, True)[self.own :]])
        flat = lambda parts: np.concatenate([np.asarray(part).reshape(-1) for part in parts])
        return {key: (flat(targets), flat(sources)) for key, (targets, sources) in moves.items()}

    def matrices(self):
        ranks = self.place.ranks
        shards = 2 if self.split else 1
        table = [self.moves(i // ranks, i % ranks) for i in range(shards * ranks)]
        line = lambda moves: np.concatenate([part for pair in moves.values() for part in pair])
        lines = jnp.asarray(np.stack([line(moves) for moves in table]).astype(np.int32))
        index = self.place.tensor + (ranks * self.place.shard if self.split else 0)
        labels, at, out = pick(lines, index), 0, {}
        for key, (targets, sources) in table[0].items():
            ends = at + targets.size, at + targets.size + sources.size
            target, source = labels[at : ends[0]], labels[ends[0] : ends[1]]
            same = (target[:, None] == source[None]) & (target[:, None] >= 0)
            out[key], at = same.astype(LOW), ends[1]
        return out


def call(body, outs, ins, scalars, cost=1, scratch=(), after=(), name=None, specs=None):
    given, count = body, len(ins)
    if after:
        body = lambda scalars, *refs: given(scalars, *refs[:count], *refs[count + len(after) :])
    moved = sum(item.size * item.dtype.itemsize for item in list(outs) + list(ins))
    spec = pl.BlockSpec(memory_space=pltpu.VMEM)
    return pl.pallas_call(
        body,
        name=name,
        out_shape=tuple(outs),
        in_specs=[pl.BlockSpec(memory_space=pltpu.SMEM)]
        + list(specs or [spec] * len(ins))
        + [pl.BlockSpec(memory_space=pl.ANY)] * len(after),
        out_specs=(spec,) * len(outs),
        scratch_shapes=list(scratch),
        grid=(1,) if specs else (),
        compiler_params=pltpu.CompilerParams(vmem_limit_bytes=VMEM_BYTES),
        cost_estimate=pl.CostEstimate(
            flops=int(PEAK * cost), bytes_accessed=moved, transcendentals=0
        ),
    )(scalars, *ins, *after)


def shape(*dims, dtype=LOW):
    return jax.ShapeDtypeStruct(dims, dtype)


def nn(first, second):
    return lax.dot_general(first, second, (((1,), (0,)), ((), ())), preferred_element_type=F32)


def nt(first, second):
    return lax.dot_general(first, second, (((1,), (1,)), ((), ())), preferred_element_type=F32)


def tn(first, second):
    return lax.dot_general(first, second, (((0,), (0,)), ((), ())), preferred_element_type=F32)


def swapper(scalars, paired):
    def swap(values):
        if not paired:
            return values
        half = values.shape[-1] // 2
        other = jnp.concatenate([values[:, half:], values[:, :half]], -1)
        return jnp.where(scalars[0] == 0, values, other)

    return swap


def unit_of(values):
    centred = values - jnp.mean(values, -1, keepdims=True)
    inverse = lax.rsqrt(jnp.mean(centred * centred, -1, keepdims=True) + EPS)
    return (centred * inverse, inverse)


def norm_back(grad, unit, inverse, gain):
    scaled = grad * gain
    inner = (
        scaled
        - jnp.mean(scaled, -1, keepdims=True)
        - unit * jnp.mean(scaled * unit, -1, keepdims=True)
    )
    return (
        inverse * inner,
        jnp.sum(grad * unit, 0, keepdims=True),
        jnp.sum(grad, 0, keepdims=True),
    )


def softmax(scores):
    weights = jnp.exp(scores - jnp.max(scores, -1, keepdims=True))
    return weights / jnp.sum(weights, -1, keepdims=True)


def score_back(probs, prob_grad):
    inner = jnp.sum(probs * prob_grad, -1, keepdims=True)
    return (probs * (prob_grad - inner)).astype(LOW)


def half_lanes(width):
    lane = lax.broadcasted_iota(jnp.int32, (1, width), 1)
    return [(lane // HEAD_DIM == e).astype(F32) for e in range(2)]


def column_sum(values):
    return jnp.sum(values.astype(F32), 0, keepdims=True)


def rows_at(start, size):
    return pl.ds(pl.multiple_of(start, 16), size)


class Program:
    def __init__(self, place, layout, width, group, scalars):
        self.place, self.layout, self.width, self.group = place, layout, width, group
        self.scalars = scalars
        self.ranks, self.quarters = place.ranks, place.quarters
        self.piece = group // self.quarters
        self.heads = group // HEAD_DIM
        self.all_heads = group * self.ranks
        spot = np.arange(self.ranks * layout.frames * CHUNK) % CHUNK
        self.same_place = jnp.asarray(
            np.where(spot[:, None] == spot[None], 0, HIDE).astype(np.float32)
        )

    def call(self, body, outs, ins, flops=0, scratch=(), after=(), specs=None, cost=None):
        name = body.__qualname__.split(".")[1]
        cost = COSTS[cost or name]
        return call(body, outs, ins, self.scalars, cost, scratch, after, name, specs)

    def lanes(self, c, h):
        at = c * self.group + h * HEAD_DIM
        return slice(at, at + HEAD_DIM)


    def live(self, scalars, batch):
        return scalars[3 + batch] > 0

    def place_natural(self, scalars, rows, source):
        lay = self.layout
        rows[...] = jnp.zeros_like(rows)
        for item in range(lay.natural_blocks):

            @pl.when(self.live(scalars, item // lay.frames))
            def _(item=item):
                rows[item * WINDOW : item * WINDOW + lay.places] = source[item]

    def send_rows(self, clips, cotangents, matrix, wait=()):
        lay, width = self.layout, self.width
        count, split = lay.natural_blocks, lay.split
        first = lay.whole * lay.frames

        def body(scalars, clips_ref, grads_ref, matrix_ref, sent, frames, rows):
            self.place_natural(scalars, rows, clips_ref)
            sent[...] = nn(matrix_ref[...], rows[...]).astype(LOW)
            for index, source in enumerate((clips_ref, grads_ref)):
                for item in range(split):
                    frame = first + lay.frames * item + 1 - scalars[0]
                    frames[index, item] = source[frame]

        outs = [shape(matrix.shape[0], width), shape(2, split, lay.places, width)]
        scratch = [pltpu.VMEM((count * WINDOW, width), LOW)]
        return self.call(body, outs, [clips, cotangents, matrix], scratch=scratch, after=wait)

    def temporal_start(self, clips, come, matrix):
        lay, width = self.layout, self.width
        count, rows_in = lay.natural_blocks, lay.natural_blocks * WINDOW
        more = 0 if come is None else come.shape[0]

        def body(scalars, clips_ref, *refs):
            matrix_ref, start_ref, normed_ref, rows = refs[-4:]
            self.place_natural(scalars, rows, clips_ref)
            if more:
                rows[rows_in:] = refs[0][...]
            start = nn(matrix_ref[...], rows[...])
            start_ref[...] = start.astype(LOW)
            unit, _ = unit_of(start)
            swap = swapper(scalars, self.place.paired)
            normed_ref[...] = swap(unit).astype(LOW)

        outs = [shape(lay.temporal_rows, width)] * 2
        ins = [clips] + ([come] if more else []) + [matrix]
        scratch = [pltpu.VMEM((rows_in + more, width), LOW)]
        return self.call(body, outs, ins, scratch=scratch)

    def frames_of(self, clips, others, index, matrix, wait=()):
        lay, width = self.layout, self.width
        count, split = lay.natural_blocks, lay.split

        def body(scalars, clips_ref, *refs):
            matrix_ref, out_ref, rows = refs[-3:]
            self.place_natural(scalars, rows, clips_ref)
            for item in range(split):

                @pl.when(jnp.logical_not(self.live(scalars, lay.whole + item)))
                def _(item=item):
                    start = (count + item) * WINDOW
                    rows[start : start + lay.places] = refs[0][index, item]

            out_ref[...] = nn(matrix_ref[...], rows[...]).astype(LOW)

        return self.call(
            body,
            [shape(lay.frame_rows, width)],
            [clips] + ([others] if split else []) + [matrix],
            scratch=[pltpu.VMEM(((count + split) * WINDOW, width), LOW)],
            after=wait,
        )[0]


    def chunk(self, refs, n):
        lay = self.layout
        return jnp.concatenate(
            [
                ref[rows_at(frame * lay.slots + n * CHUNK, CHUNK)]
                for ref in refs
                for frame in range(lay.frames)
            ]
        )

    def put_chunk(self, refs, n, values):
        lay = self.layout
        for k, ref in enumerate(refs):
            for frame in range(lay.frames):
                at = (k * lay.frames + frame) * CHUNK
                ref[rows_at(frame * lay.slots + n * CHUNK, CHUNK)] = values[at : at + CHUNK]

    def temporal(self, units, weights, along, shift, wait=()):
        lay, width, group, ranks = self.layout, self.width, self.group, self.ranks
        rows = lay.temporal_rows

        def body(scalars, *refs):
            unit_refs, weight_refs = refs[:ranks], refs[ranks : ranks + len(weights)]
            refs = refs[ranks + len(weights) :]
            along_ref, shift_ref, same, refs = refs[0], refs[1], refs[2], refs[3:]
            qkv_refs, mixed_refs, normed_refs, out_refs = (
                refs[at : at + ranks] for at in range(0, 4 * ranks, ranks)
            )
            swap = swapper(scalars, self.place.paired)
            gain, move = swap(along_ref[0:1]), swap(along_ref[3:4])
            weight = jnp.concatenate([ref[: 3 * group] for ref in weight_refs], -1)
            for k in range(ranks):
                normed_refs[k][...] = (unit_refs[k][...].astype(F32) * gain + move).astype(LOW)
                qkv_refs[k][...] = (nt(normed_refs[k][...], weight) + shift_ref[...]).astype(LOW)

            @pl.loop(0, lay.slots // CHUNK)
            def _(n):
                values = self.chunk(qkv_refs, n)
                parts = []
                for h in range(self.heads):
                    query, key, value = (values[:, self.lanes(c, h)] for c in range(3))
                    probs = softmax(nt(query, key) * SCALE + same[...])
                    parts.append(nn(probs.astype(LOW), value))
                self.put_chunk(mixed_refs, n, jnp.concatenate(parts, -1).astype(LOW))

            weight = jnp.concatenate([ref[3 * group : 4 * group] for ref in weight_refs], -1)
            for k in range(ranks):
                out_refs[k][...] = nn(mixed_refs[k][...], weight).astype(LOW)

        outs = [shape(rows, 3 * group)] * ranks + [shape(rows, group)] * ranks
        outs += [shape(rows, width)] * (2 * ranks)
        ins = list(units) + list(weights) + [along, shift, self.same_place]
        flops = 8 * ranks * rows * width * group
        flops += 4 * ranks * rows * self.same_place.shape[0] * group
        outs = self.call(body, outs, ins, flops, after=wait)
        return [outs[at : at + ranks] for at in range(0, 4 * ranks, ranks)]

    def temporal_out(self, parts, along, matrix, wait=()):
        lay, width = self.layout, self.width
        far = [] if matrix is None else [matrix]

        def body(scalars, *refs):
            part_refs, along_ref, refs = refs[: self.ranks], refs[self.ranks], refs[self.ranks + 1 :]
            swap = swapper(scalars, self.place.paired)
            total = swap(sum(ref[...].astype(F32) for ref in part_refs)) + along_ref[6:7]
            out_ref = refs[len(far)]
            out_ref[...] = total.astype(LOW)
            if far:
                refs[2][...] = nn(refs[0][...], out_ref[...]).astype(LOW)

        outs = [shape(lay.temporal_rows, width)] + [shape(item.shape[0], width) for item in far]
        return self.call(body, outs, list(parts) + [along] + far, after=wait)

    def temporal_grad(self, parts, matrix, wait=()):
        lay, width = self.layout, self.width

        def body(scalars, *refs):
            matrix_ref, out_ref = refs[len(parts) :]
            swap = swapper(scalars, self.place.paired)
            source = jnp.concatenate([ref[...] for ref in refs[: len(parts)]])
            out_ref[...] = swap(nn(matrix_ref[...], source)).astype(LOW)

        outs = [shape(lay.temporal_rows, width)]
        return self.call(body, outs, list(parts) + [matrix], after=wait)[0]

    def temporal_back(self, qkv, grads, units, weights, wait=()):
        lay, width, group, ranks = self.layout, self.width, self.group, self.ranks
        rows = lay.temporal_rows

        def body(scalars, *refs):
            qkv_refs, grad_refs, unit_refs = (
                refs[at : at + ranks] for at in range(0, 3 * ranks, ranks)
            )
            refs = refs[3 * ranks :]
            weight_refs, same, refs = refs[: len(weights)], refs[len(weights)], refs[len(weights) + 1 :]
            out_refs, back_refs, sums = refs[:ranks], refs[ranks : 2 * ranks], refs[2 * ranks]
            mixed = refs[2 * ranks + 1 :]
            weight = jnp.concatenate([ref[3 * group : 4 * group] for ref in weight_refs], -1)
            for k in range(ranks):
                mixed[k][...] = nt(grad_refs[k][...], weight).astype(LOW)

            @pl.loop(0, lay.slots // CHUNK)
            def _(n):
                values, grads = self.chunk(qkv_refs, n), self.chunk(mixed, n)
                parts = [[], [], []]
                for h in range(self.heads):
                    query, key, value = (values[:, self.lanes(c, h)] for c in range(3))
                    grad = grads[:, self.lanes(0, h)]
                    probs = softmax(nt(query, key) * SCALE + same[...])
                    scored = score_back(probs, nt(grad, value))
                    parts[0].append(nn(scored, key) * SCALE)
                    parts[1].append(tn(scored, query) * SCALE)
                    parts[2].append(tn(probs.astype(LOW), grad))
                total = jnp.concatenate(parts[0] + parts[1] + parts[2], -1)
                self.put_chunk(out_refs, n, total.astype(LOW))

            weight = jnp.concatenate([ref[: 3 * group] for ref in weight_refs], -1)
            sums[...] = jnp.zeros_like(sums)
            for k in range(ranks):
                back = nn(out_refs[k][...], weight)
                back_refs[k][...] = back.astype(LOW)
                sums[0:1] += column_sum(back * unit_refs[k][...].astype(F32))
                sums[1:2] += column_sum(back)

        outs = [shape(rows, 3 * group)] * ranks + [shape(rows, width)] * ranks
        outs += [shape(8, width, dtype=F32)]
        ins = list(qkv) + list(grads) + list(units) + list(weights) + [self.same_place]
        flops = 8 * ranks * rows * width * group
        flops += 10 * ranks * rows * self.same_place.shape[0] * group
        scratch = [pltpu.VMEM((rows, group), LOW)] * ranks
        outs = self.call(body, outs, ins, flops, scratch, wait)
        return outs[:ranks], outs[ranks : 2 * ranks], outs[-1]

    def group_weights(self, qkv_grads, normed, mixed=(), out_grads=(), more=(), wait=()):
        width, group, count = self.width, self.group, len(qkv_grads)
        parts = 2 if self.place.paired else 1
        size = 3 * group + (group if mixed else 0)

        def body(scalars, *refs):
            refs = list(refs)
            take = lambda n: [refs.pop(0) for _ in range(n)]
            grad_refs, normed_refs = take(count), take(count)
            mixed_refs, out_grad_refs = take(len(mixed)), take(len(mixed))
            more_refs, (spread,), out_refs = take(len(more)), take(1), refs
            columns = width // parts

            def put(start, total):
                for part in range(parts):
                    values = total[:, part * columns : (part + 1) * columns]
                    out_refs[part][start : start + total.shape[0]] = values.astype(LOW)

            total = jnp.zeros((3 * group, width), F32)
            sums = jnp.zeros((1, 3 * group), F32)
            for j in range(count):
                total = total + tn(grad_refs[j][...], normed_refs[j][...])
                sums = sums + column_sum(grad_refs[j][...])
            put(0, total)
            if mixed:
                total = jnp.zeros((group, width), F32)
                for j in range(count):
                    total = total + tn(mixed_refs[j][...], out_grad_refs[j][...])
                put(3 * group, total)
            line = jnp.concatenate([sums[:, :group], sums[:, 2 * group :]], -1)
            top = lax.broadcasted_iota(jnp.int32, (16, 2 * group), 0) == 0
            line = jnp.where(top, line, 0.0).astype(LOW)
            for part in range(parts):
                out_refs[part][size : size + 16] = line if parts == 2 else nn(line, spread[...]).astype(LOW)
                for ref in more_refs:
                    rows = ref[:, part * columns : (part + 1) * columns]
                    rows = jnp.concatenate([rows, jnp.zeros_like(rows)])
                    out_refs[part][size + 16 :] = rows.astype(LOW)
                if not more:
                    out_refs[part][size + 16 :] = jnp.zeros((16, columns), LOW)

        outs = [shape(size + 32, width // parts)] * parts
        rows = qkv_grads[0].shape[0]
        ins = list(qkv_grads) + list(normed) + list(mixed) + list(out_grads) + list(more)
        ins += [self.spread()]
        return self.call(body, outs, ins, 2 * count * rows * width * size, after=wait)

    def spread(self):
        shards = self.place.shards
        columns, part = self.width // shards, HEAD_DIM // shards
        out = np.zeros((2 * self.group, self.width), np.float32)
        for item in range(2 * self.group):
            head, feature = divmod(item, HEAD_DIM)
            out[item, feature // part * columns + head * part + feature % part] = 1
        return jnp.asarray(out, LOW)

    def temporal_input(self, backs, start, along, matrix, wait=()):
        lay, width = self.layout, self.width
        far = [] if matrix is None else [matrix]

        def body(scalars, *refs):
            back_refs, refs = refs[: self.ranks], refs[self.ranks :]
            start_ref, along_ref, refs = refs[0], refs[1], refs[2:]
            out_ref = refs[len(far)]
            swap = swapper(scalars, self.place.paired)
            unit, inverse = unit_of(start_ref[...].astype(F32))
            grad = swap(sum(ref[...].astype(F32) for ref in back_refs))
            back, _, _ = norm_back(grad, unit, inverse, along_ref[0:1])
            out_ref[...] = back.astype(LOW)
            if far:
                refs[2][...] = nn(refs[0][...], out_ref[...]).astype(LOW)

        outs = [shape(lay.temporal_rows, width)] + [shape(item.shape[0], width) for item in far]
        return self.call(body, outs, list(backs) + [start, along] + far, after=wait)


    def spatial_in(self, sources, matrix, start, fc, along, wait=()):
        lay, width = self.layout, self.width
        rows = lay.frame_rows

        def body(scalars, *refs):
            source_refs, refs = refs[: len(sources)], refs[len(sources) :]
            matrix_ref, start_ref, fc_refs, refs = refs[0], refs[1], refs[2 : 2 + len(fc)], refs[2 + len(fc) :]
            along_ref, after_ref, temporal_ref, normed_ref = refs
            swap = swapper(scalars, self.place.paired)
            source = jnp.concatenate([ref[...] for ref in source_refs])
            temporal = nn(matrix_ref[...], source)
            temporal_ref[...] = temporal.astype(LOW)
            weight = jnp.concatenate([ref[...] for ref in fc_refs])
            after = start_ref[...].astype(F32) + nn(swap(temporal).astype(LOW), weight)
            after = after + along_ref[7:8]
            after_ref[...] = after
            unit, _ = unit_of(after)
            normed_ref[...] = swap(unit * along_ref[1:2] + along_ref[4:5]).astype(LOW)

        outs = [shape(rows, width, dtype=F32), shape(rows, width), shape(rows, width)]
        ins = list(sources) + [matrix, start] + list(fc) + [along]
        return self.call(body, outs, ins, 2 * rows * width * width, after=wait)

    def windows(self, refs, n):
        at = rows_at(n * (WINDOW - 16), WINDOW)
        return jnp.concatenate([ref[at] for ref in refs])

    def window_mask(self, n, axis):
        size = self.quarters * WINDOW
        dims = (size, 1) if axis == 0 else (1, size)
        index = lax.broadcasted_iota(jnp.int32, dims, axis) & (WINDOW - 1)
        start = n * (self.layout.places - WINDOW + 16)
        return (index >= start) & (index < start + self.layout.places)

    def put_windows(self, refs, n, values, mask):
        for j, ref in enumerate(refs):
            at = rows_at(n * (WINDOW - 16), WINDOW)
            part = slice(j * WINDOW, (j + 1) * WINDOW)
            old = ref[at].astype(F32)
            ref[at] = jnp.where(mask[part], values[part], old).astype(LOW)

    def spatial(self, normed, win, shift, wait=()):
        lay, width, quarters, group = self.layout, self.width, self.quarters, self.group

        def body(scalars, *refs):
            normed_refs, refs = refs[:quarters], refs[quarters:]
            win_refs, shift_ref, refs = refs[: len(win)], refs[len(win)], refs[len(win) + 1 :]
            qkv_refs, out_refs = refs[:quarters], refs[quarters:]
            weight = jnp.concatenate([ref[: 3 * group] for ref in win_refs], -1)
            for j in range(quarters):
                qkv_refs[j][...] = (nt(normed_refs[j][...], weight) + shift_ref[...]).astype(LOW)
                out_refs[j][...] = jnp.zeros_like(out_refs[j])

            @pl.loop(0, lay.units)
            def _(n):
                rows = self.windows(qkv_refs, n)
                hide = jnp.where(self.window_mask(n, 1), 0.0, HIDE)
                parts = []
                for h in range(self.heads):
                    query, key, value = (rows[:, self.lanes(c, h)] for c in range(3))
                    probs = softmax(nt(query, key) * SCALE + hide)
                    parts.append(nn(probs.astype(LOW), value))
                mask = self.window_mask(n, 0)
                self.put_windows(out_refs, n, jnp.concatenate(parts, -1), mask)

        outs = [shape(lay.frame_rows, 3 * group)] * quarters
        outs += [shape(lay.frame_rows, group)] * quarters
        size = quarters * WINDOW
        flops = 6 * quarters * lay.frame_rows * width * group + 4 * lay.units * size * size * group
        outs = self.call(body, outs, list(normed) + list(win) + [shift], flops, after=wait)
        return outs[:quarters], outs[quarters:]

    def spatial_back(self, qkv, grads, win, wait=()):
        lay, width, quarters, group = self.layout, self.width, self.quarters, self.group

        def body(scalars, *refs):
            qkv_refs, grad_refs = refs[:quarters], refs[quarters : 2 * quarters]
            win_refs = refs[2 * quarters : 2 * quarters + len(win)]
            refs = refs[2 * quarters + len(win) :]
            out_refs, back_refs = refs[:quarters], refs[quarters:]
            for ref in out_refs:
                ref[...] = jnp.zeros_like(ref)

            @pl.loop(0, lay.units)
            def _(n):
                rows = self.windows(qkv_refs, n)
                mask = self.window_mask(n, 0)
                grads = self.windows(grad_refs, n) * mask.astype(F32).astype(LOW)
                hide = jnp.where(self.window_mask(n, 1), 0.0, HIDE)
                parts = [[], [], []]
                for h in range(self.heads):
                    query, key, value = (rows[:, self.lanes(c, h)] for c in range(3))
                    grad = grads[:, self.lanes(0, h)]
                    probs = softmax(nt(query, key) * SCALE + hide)
                    scored = score_back(probs, nt(grad, value))
                    parts[0].append(nn(scored, key) * SCALE)
                    parts[1].append(tn(scored, query) * SCALE)
                    parts[2].append(tn(probs.astype(LOW), grad))
                values = jnp.concatenate(parts[0] + parts[1] + parts[2], -1)
                self.put_windows(out_refs, n, values, mask)

            weight = jnp.concatenate([ref[: 3 * group] for ref in win_refs], -1)
            for j in range(quarters):
                back_refs[j][...] = nn(out_refs[j][...], weight).astype(LOW)

        outs = [shape(lay.frame_rows, 3 * group)] * quarters
        outs += [shape(lay.frame_rows, width)] * quarters
        size = quarters * WINDOW
        flops = 10 * lay.units * size * size * group
        flops += 6 * quarters * lay.frame_rows * width * group
        outs = self.call(body, outs, list(qkv) + list(grads) + list(win), flops, after=wait)
        return outs[:quarters], outs[quarters:]

    def put_groups(self, scalars, out, pieces, first):
        for i in range(self.quarters):
            spot = (scalars[1] ^ i) * self.piece
            for j in range(self.quarters):
                k = group_of(scalars[1]) ^ group_of(j)
                out[rows_at(j * self.group + spot, self.piece)] = pieces[i][
                    k, first : first + self.piece
                ]

    def spatial_out(self, mixed, pieces, first, after, grad, along, wait=()):
        lay, width, group = self.layout, self.width, self.group
        rows, quarters = lay.frame_rows, self.quarters
        size = WINDOW

        def body(scalars, *refs):
            mixed_refs, piece_refs, refs = refs[:quarters], refs[quarters : 2 * quarters], refs[2 * quarters :]
            after_ref, grad_ref, along_ref, out_ref, normed_ref, low_ref, wout = refs
            swap = swapper(scalars, self.place.paired)
            self.put_groups(scalars, wout, piece_refs, 0)
            total = jnp.zeros((rows, width), F32)
            for j in range(quarters):
                total = total + nn(mixed_refs[j][...], wout[j * group : (j + 1) * group])
            after = after_ref[...] + swap(total) + along_ref[8:9]
            out_ref[...] = after
            unit, _ = unit_of(after)
            normed_ref[...] = swap(unit * along_ref[2:3] + along_ref[5:6]).astype(LOW)
            low_ref[...] = swap(grad_ref[...].astype(F32)).astype(LOW)

        outs = [
            shape(rows, width, dtype=F32),
            shape(rows, width),
            shape(rows, width),
            shape(self.all_heads, width),
        ]
        ins = list(mixed) + list(pieces) + [after, grad, along]
        whole = pl.BlockSpec(memory_space=pltpu.VMEM)
        part = pl.BlockSpec((self.ranks, size, width), lambda *_: (0, first // size, 0))
        specs = [whole] * quarters + [part] * quarters + [whole] * 3
        flops = 2 * rows * width * self.all_heads
        return self.call(body, outs, ins, flops, after=wait, specs=specs)

    def feed_forward(self, normed, grad, pieces, shifts, totals):
        lay, width = self.layout, self.width
        rows, count, ranks = lay.frame_rows, len(pieces), self.ranks
        hidden = shifts[0].shape[1]
        unit = hidden // ranks
        tile = 256

        def body(scalars, normed_ref, grad_ref, *refs):
            refs = list(refs)
            take = lambda n: [refs.pop(0) for _ in range(n)]
            piece_refs, shift_refs = take(count), take(count)
            before = take(2 if totals else 0)
            out_ref, back_ref = take(2)
            grad_refs, sum_refs = take(count), take(count)
            ups, downs, up_grad, down_grad = take(4)
            out_ref[...] = before[0][...] if totals else jnp.zeros_like(out_ref)
            back_ref[...] = before[1][...] if totals else jnp.zeros_like(back_ref)
            for item in range(count):
                for k in range(ranks):
                    at = slice(k * unit, (k + 1) * unit)
                    ups[at] = piece_refs[item][k, :unit]
                    downs[at] = piece_refs[item][k, unit : 2 * unit]

                @pl.loop(0, hidden // tile)
                def _(m, item=item):
                    at = pl.ds(pl.multiple_of(m * tile, tile), tile)
                    up, down = ups[at], downs[at]
                    values = nt(normed_ref[...], up) + shift_refs[item][:, at]
                    half = 0.5 * (1.0 + lax.erf(values * SQRT_HALF))
                    active = (values * half).astype(LOW)
                    slope = half + values * jnp.exp(-0.5 * values * values) * INV_ROOT_TAU
                    out_ref[...] += nn(active, down)
                    down_grad[at] = tn(active, grad_ref[...]).astype(LOW)
                    hidden_grad = (nt(grad_ref[...], down) * slope).astype(LOW)
                    up_grad[at] = tn(hidden_grad, normed_ref[...]).astype(LOW)
                    back_ref[...] += nn(hidden_grad, up)
                    sum_refs[item][:, at] = column_sum(hidden_grad)

                for k in range(ranks):
                    at = slice(k * unit, (k + 1) * unit)
                    grad_refs[item][k, :unit] = up_grad[at]
                    grad_refs[item][k, unit:] = down_grad[at]

        outs = [shape(rows, width, dtype=F32)] * 2
        outs += [shape(ranks, 2 * unit, width)] * count + [shape(1, hidden, dtype=F32)] * count
        ins = [normed, grad] + list(pieces) + list(shifts) + list(totals or ())
        flops = 12 * rows * width * hidden * count
        scratch = [pltpu.VMEM((hidden, width), LOW)] * 4
        outs = self.call(body, outs, ins, flops, scratch)
        return outs[:2], outs[2 : 2 + count], outs[2 + count :]

    def feed_forward_back(self, after, out, back, grad, mixed, wout, along):
        lay, width, group = self.layout, self.width, self.group
        rows, quarters = lay.frame_rows, self.quarters

        def body(scalars, after_ref, out_ref, back_ref, grad_ref, wout_ref, along_ref, *refs):
            mixed_refs, refs = refs[:quarters], refs[quarters:]
            layer_ref, total_ref, sums, wout_grad = refs[:4]
            mixed_grads = refs[4:]
            swap = swapper(scalars, self.place.paired)
            after = after_ref[...]
            layer_ref[...] = (after + swap(out_ref[...]) + along_ref[9:10]).astype(LOW)
            unit, inverse = unit_of(after)
            back, gain, shift = norm_back(swap(back_ref[...]), unit, inverse, along_ref[2:3])
            grad = grad_ref[...].astype(F32)
            total = grad + back
            total_ref[...] = total
            low = total.astype(LOW)
            sums[0:1] = gain
            sums[1:2] = shift
            sums[2:3] = column_sum(low)
            sums[3:4] = column_sum(grad)
            turned = swap(low.astype(F32)).astype(LOW)
            for j in range(quarters):
                at = slice(j * group, (j + 1) * group)
                mixed_grads[j][...] = nt(turned, wout_ref[at]).astype(LOW)
                wout_grad[at] = tn(mixed_refs[j][...], turned).astype(LOW)

        outs = [
            shape(rows, width),
            shape(rows, width, dtype=F32),
            shape(4, width, dtype=F32),
            shape(self.all_heads, width),
        ] + [shape(rows, group)] * quarters
        ins = [after, out, back, grad, wout, along] + list(mixed)
        outs = self.call(body, outs, ins, 4 * rows * width * self.all_heads)
        return outs[:4], outs[4:]

    def spatial_input(self, backs, after, total, along, fc, matrix, wait=()):
        lay, width = self.layout, self.width
        rows, quarters = lay.frame_rows, self.quarters
        far = [] if matrix is None else [matrix]

        def body(scalars, *refs):
            back_refs, refs = refs[:quarters], refs[quarters:]
            after_ref, total_ref, along_ref, refs = refs[0], refs[1], refs[2], refs[3:]
            fc_refs, refs = refs[: len(fc)], refs[len(fc) :]
            low_ref, out_ref, sums = refs[len(far) : len(far) + 3]
            swap = swapper(scalars, self.place.paired)
            grad = swap(sum(ref[...].astype(F32) for ref in back_refs))
            unit, inverse = unit_of(after_ref[...])
            back, gain, shift = norm_back(grad, unit, inverse, along_ref[1:2])
            low = (total_ref[...] + back).astype(LOW)
            low_ref[...] = low
            weight = jnp.concatenate([ref[...] for ref in fc_refs])
            temporal = swap(nt(low, weight)).astype(LOW)
            out_ref[...] = temporal
            sums[0:1] = gain
            sums[1:2] = shift
            sums[2:3] = column_sum(temporal)
            sums[3:4] = column_sum(low)
            if far:
                refs[4][...] = nn(refs[0][...], temporal).astype(LOW)

        outs = [shape(rows, width), shape(rows, width), shape(4, width, dtype=F32)]
        outs += [shape(item.shape[0], width) for item in far]
        ins = list(backs) + [after, total, along] + list(fc) + far
        return self.call(body, outs, ins, 2 * rows * width * width, after=wait)

    def out_weights(self, wout_grad, low, temporal, vectors, wait=()):
        width, group, piece = self.width, self.group, self.piece
        quarters, ranks = self.quarters, self.ranks
        extra, quarter = vectors.shape[1], width // quarters
        each = piece + extra

        def body(scalars, wout_ref, low_ref, temporal_ref, vectors_ref, *refs):
            pieces, fc = refs[:quarters], refs[quarters]
            swap = swapper(scalars, self.place.paired)
            turned = swap(temporal_ref[...].astype(F32)).astype(LOW)
            fc[...] = tn(low_ref[...], turned).astype(LOW)
            for i in range(quarters):
                spot = (scalars[1] ^ i) * piece
                for j in range(quarters):
                    k = group_of(scalars[1]) ^ group_of(j)
                    pieces[i][rows_at(k * each, piece)] = wout_ref[rows_at(j * group + spot, piece)]
                for k in range(ranks):
                    pieces[i][k * each + piece : (k + 1) * each] = vectors_ref[k]
                pieces[i][ranks * each :] = fc[rows_at((scalars[1] ^ i) * quarter, quarter)]

        outs = [shape(ranks * each + quarter, width)] * quarters
        ins = [wout_grad, low, temporal, vectors]
        flops = 2 * low.shape[0] * width * width
        return self.call(body, outs, ins, flops, [pltpu.VMEM((width, width), LOW)], wait)

    def natural(self, parts, wait=(), last=False):
        lay, width = self.layout, self.width
        count = lay.natural_blocks
        counts = [len(rows) for _, rows in parts]

        def body(scalars, *refs):
            refs = list(refs)
            out_ref = refs.pop()
            total = jnp.zeros((count * WINDOW, width), F32)
            for size in counts:
                matrix = refs.pop(0)
                source = jnp.concatenate([refs.pop(0)[...] for _ in range(size)])
                total = total + nn(matrix[...], source)
            total = total.astype(LOW)
            for item in range(count):
                part = total[item * WINDOW : item * WINDOW + lay.places]
                out_ref[item] = part

                @pl.when(jnp.logical_not(self.live(scalars, item // lay.frames)))
                def _(item=item):
                    out_ref[item] = jnp.zeros((lay.places, width), LOW)


        ins = []
        for matrix, rows in parts:
            ins += [matrix] + list(rows)
        cost = "natural_last" if last else None
        return self.call(body, [shape(count, lay.places, width)], ins, after=wait, cost=cost)[0]


def body(
    clip_input,
    clip_slot,
    norm_gain,
    norm_shift,
    attention_in,
    attention_bias,
    attention_out,
    branch_bias,
    temporal_fc,
    hidden_in,
    hidden_bias,
    hidden_out,
    output_grad,
):
    place = Place()
    shards, quarters, ranks = place.shards, place.quarters, place.ranks
    shard, context, tensor = place.shard, place.context, place.tensor
    clips, cotangents = clip_input[:, 0], output_grad[:, 0]
    lay = Layout(place, clips)
    columns = attention_in.shape[1]
    width = columns * shards
    group = attention_in.shape[3]
    heads = group // HEAD_DIM
    hidden = hidden_in.shape[1]
    piece = group // quarters
    scalars = jnp.concatenate([jnp.stack([shard, context, tensor]), clip_slot[:, 0]])
    prog = Program(place, lay, width, group, scalars.astype(jnp.int32))
    moves = lay.matrices()
    split = lay.split > 0

    def beside(rows):
        return [rows, hop(rows, "shard", 1)] if split else [rows]

    def swapped(rows, axis):
        return [rows[0]] + [hop(rows[k], axis, k) for k in range(1, len(rows))]

    def to_all(rows, axis):
        if axis == "context":
            far = hop(rows, axis, 2)
            return [rows, hop(rows, axis, 1), far, hop(far, axis, 1)]
        return [rows] + [hop(rows, axis, k) for k in range(1, ranks)]

    def shard_parts(block, axis=1):
        if place.paired:
            return [block, hop(block, "shard", 1)]
        return [lax.all_gather(block, "shard", axis=axis, tiled=True)]

    def bias_rows(index):
        rows = attention_bias[index].reshape(-1)
        return jnp.pad(rows, (0, columns - rows.size))[None]

    def in_rows(index):
        return jnp.transpose(attention_in[index], (1, 2, 0)).reshape(3 * group, columns)

    def bias_of(parts, row):
        kinds = 2 * heads * (HEAD_DIM // shards)
        if place.paired:
            lines = [part[row, :kinds] for part in parts]
            lines = jnp.where(shard == 0, jnp.stack(lines), jnp.stack(lines[::-1]))
        else:
            lines = parts[0][row].reshape(shards, columns)[:, :kinds]
        lines = lines.reshape(shards, 2, heads, HEAD_DIM // shards)
        lines = jnp.transpose(lines, (1, 2, 0, 3)).reshape(2, group).astype(F32)
        return jnp.concatenate([lines[0], jnp.zeros(group, F32), lines[1]])[None]

    flat = lambda rows: rows.reshape((-1,) + rows.shape[2:])
    clips, cotangents = flat(clips), flat(cotangents)
    quarter = lambda rows: pick(rows.reshape(quarters, -1, columns), context)
    up_part = pick(hidden_in.reshape(columns, quarters, -1), context, 1).T
    unit = up_part.shape[0]
    block = [up_part, quarter(hidden_out), quarter(attention_out[1])]
    block.append(jnp.pad(hidden_bias.reshape(1, -1), ((0, 15), (0, 0))))
    gather_c = Gather(place, jnp.concatenate(block))

    along = jnp.concatenate([norm_gain, norm_shift, branch_bias, bias_rows(0)])
    along = shard_parts(jnp.pad(along, ((0, 16 - along.shape[0]), (0, 0))))
    shift_a = bias_of(along, 10)
    if place.paired:
        along = jnp.where(shard == 0, *[jnp.concatenate(pair, -1) for pair in (along, along[::-1])])
    else:
        along = along[0]
    along = along[:10].astype(F32)

    come, others = None, None
    if split:
        sent, others = prog.send_rows(clips, cotangents, moves["begin_far"])
        come = hop(sent, "shard", 1)
    weights_a = jnp.concatenate([in_rows(0), attention_out[0]])
    weights_a = shard_parts(tie(weights_a, come) if split else weights_a)
    start_t, unit_a = prog.temporal_start(clips, come, moves["beginning"])
    units_a = to_all(unit_a, "tensor")
    gather_c.columns(unit_a)
    gather_c.rows()

    qkv_a, mixed_a, normed_a, parts = prog.temporal(
        units_a, weights_a, along, shift_a, gather_c.far[:1]
    )
    fc = shard_parts(tie(temporal_fc, parts[0]), 0)
    if split:
        others = hop(tie(others, parts[0]), "shard", 1)
    temporal_t = prog.temporal_out(
        swapped(parts, "tensor"), along, moves.get("return_far"), gather_c.far[-1:]
    )
    in_b = jnp.concatenate([in_rows(1), jnp.pad(bias_rows(1), ((0, 15), (0, 0)))])
    in_b = hop_group(tie(in_b, temporal_t[0]))
    weights_b = shard_parts(in_b)
    shift_b = bias_of(weights_b, 3 * group)
    sources = [temporal_t[0]] + [hop(rows, "shard", 1) for rows in temporal_t[1:]]

    start = prog.frames_of(clips, others, 0, moves["starting"])
    after_a, temporal, normed_b = prog.spatial_in(
        sources, moves["returning"], start, fc, along
    )
    normed_b = to_all(normed_b, "context")
    qkv_b, mixed = prog.spatial(normed_b, weights_b, shift_b)
    mixed = swapped(mixed, "context")
    grad = prog.frames_of(cotangents, others, 1, moves["starting"], [after_a])
    pieces_c = gather_c.cores(after_a)
    line = gather_c.first[:, 2 * unit + piece].astype(F32)
    up_shift = line.reshape((ranks, shards) + hidden_bias.shape)
    if place.paired:
        up_shift = jnp.where(shard == 0, up_shift, up_shift[:, ::-1])
    up_shift = jnp.swapaxes(up_shift, 1, 2).reshape(ranks, quarters, unit)
    up_shift = [pick(up_shift, context ^ j, 1).reshape(1, -1) for j in range(quarters)]
    after_b, normed_c, low, wout_b = prog.spatial_out(
        mixed, pieces_c, 2 * unit, after_a, grad, along
    )

    totals = None
    piece_grads, up_bias_grads = [None] * quarters, [None] * quarters
    for pair in ((1, 3), (0, 2)):
        totals, grads, sums = prog.feed_forward(
            normed_c, low, [pieces_c[j] for j in pair], [up_shift[j] for j in pair], totals
        )
        for index, j in enumerate(pair):
            piece_grads[j] = grads[index]
            up_bias_grads[j] = sums[index]
    reduce_c = ReduceHidden(place, piece_grads)
    kept, mixed_grads = prog.feed_forward_back(
        after_b, totals[0], totals[1], grad, mixed, wout_b, along
    )
    layer_rows, total, sums_c, wout_grad = kept
    wait = reduce_c.cores(layer_rows)

    mixed_grads = swapped(mixed_grads, "context")
    qkv_grads, backs = prog.spatial_back(qkv_b, mixed_grads, weights_b, wait)
    done = backs[0]
    backs = swapped(backs, "context")
    group_grads = prog.group_weights(qkv_grads, normed_b)
    low_total, temporal_grad, sums_b, *sent = prog.spatial_input(
        backs, after_a, total, along, fc, moves.get("arrive_far"), [group_grads[0]] + reduce_c.legs(done)
    )

    sources = [temporal_grad] + [hop(rows, "shard", 1) for rows in sent]
    out_grad = prog.temporal_grad(sources, moves["arriving"], reduce_c.both(low_total))
    out_grads = to_all(out_grad, "tensor")
    layer_out, home = [(moves["ending"], [layer_rows])], [(moves["ending"], [low_total])]
    if split:
        far = hop(tie(jnp.concatenate([layer_rows[lay.own :], low_total[lay.own :]]), out_grad), "shard", 1)
        layer_out.append((moves["end_far"], [far[: far.shape[0] // 2]]))
        home.append((moves["end_far"], [far[far.shape[0] // 2 :]]))
    layer_out = prog.natural(layer_out, [out_grad])
    part_in_b = sum_columns(place, group_grads[0], group_grads[-1], out_grads[1])
    sums = [sums_b[0], sums_c[0], sums_b[1], sums_c[1], sums_b[2], sums_b[3], sums_c[2], sums_c[3]]
    outer = ordered([item.reshape(ranks, -1) for item in up_bias_grads], context, 1)
    outer = outer.reshape(ranks, -1, shards, hidden_bias.shape[1])
    outer = jnp.swapaxes(outer, 1, 2).reshape(ranks, 1, width)
    sums = jnp.stack(sums)
    vectors = jnp.concatenate([jnp.broadcast_to(sums, (ranks,) + sums.shape), outer], 1)
    if place.paired:
        flipped = jnp.concatenate([vectors[..., columns:], vectors[..., :columns]], -1)
        vectors = jnp.where(shard == 0, vectors, flipped)
    vectors = jnp.pad(vectors, ((0, 0), (0, 16 - vectors.shape[1]), (0, 0))).astype(LOW)
    pieces = prog.out_weights(wout_grad, low_total, temporal, vectors, [out_grad])
    reduce_out = ReduceShared(place, pieces, piece + vectors.shape[1])
    wait = reduce_out.cores(out_grads[1]) + [part_in_b, layer_out]
    total_in_b = hop_group(part_in_b)
    qkv_grads, backs, sums_a = prog.temporal_back(qkv_a, out_grads, units_a, weights_a, wait)
    done = backs[0]
    backs = swapped(backs, "tensor")
    for step in (1, 2):
        sums_a = sums_a + hop(sums_a, "tensor", step)
    group_grads = prog.group_weights(qkv_grads, normed_a, mixed_a, out_grads, [sums_a])
    total_in_a = sum_columns(place, group_grads[0], group_grads[-1])
    sum_in = SumContext(place, jnp.concatenate([total_in_a, tie(total_in_b, done)]))
    wait = reduce_out.rows(backs[1]) + reduce_c.hops(done) + reduce_out.columns(backs[1])
    total_c = reduce_c.finish()
    wait += sum_in.cores(backs[1]) + [total_c]
    back, *sent = prog.temporal_input(
        backs, start_t, along, moves.get("home_far"), wait
    )
    home.append((moves["homing"], [back] + [hop(rows, "shard", 1) for rows in sent]))
    input_grad = prog.natural(home, last=True)

    total_in = sum_in.finish()
    total_in_a, total_in_b = total_in[: total_in_a.shape[0]], total_in[total_in_a.shape[0] :]
    reduce_out.hops()
    total_out = reduce_out.finish()

    def in_grad(total):
        part = total[: 3 * group].reshape(3, group, columns)
        return jnp.transpose(part, (2, 0, 1))

    def bias_grad(line):
        part = HEAD_DIM // shards
        if place.paired:
            return pick(line.reshape(2, heads, shards, part), shard, 2)
        return line[: 2 * heads * part].reshape(2, heads, part)

    in_total = jnp.stack([in_grad(total_in_a), in_grad(total_in_b)])
    inner = jnp.stack([bias_grad(total_in_a[4 * group]), bias_grad(total_in_b[3 * group])])
    out_b = total_out[:, :piece].reshape(group, columns)
    out_total = jnp.stack([total_in_a[3 * group : 4 * group], out_b])
    fc_total = total_out[:, -(width // quarters) :].reshape(width, columns).T
    vectors = total_out[0, piece:]
    sums_a = total_in_a[4 * group + 16 : 4 * group + 18]
    gains = jnp.concatenate([sums_a[:1], vectors[0:2]])
    shifts = jnp.concatenate([sums_a[1:], vectors[2:4]])
    rows_shape = clip_input.shape
    return (
        layer_out.reshape(rows_shape),
        input_grad.reshape(rows_shape),
        gains,
        shifts,
        in_total,
        inner,
        out_total,
        vectors[4:8],
        fc_total,
        total_c[:, :unit].reshape(hidden, columns).T,
        vectors[8].reshape(hidden_bias.shape),
        total_c[:, unit:].reshape(hidden, columns),
    )


def solution(mesh):
    rows = P(None, "shard", "tensor", "context", None)
    weights = (
        P(None, "shard"),
        P(None, "shard"),
        P(None, "shard", None, "tensor"),
        P(None, None, "tensor", "shard"),
        P(None, "tensor", "shard"),
        P(None, "shard"),
        P("shard", None),
        P("shard", "tensor"),
        P("tensor", "shard"),
        P("tensor", "shard"),
    )
    return jax.shard_map(
        body,
        mesh=mesh,
        in_specs=(rows, P(None, "shard")) + weights + (rows,),
        out_specs=(rows, rows) + weights,
        check_vma=False,
    )
```

```python
import jax
import jax.numpy as jnp
import numpy as np
from jax import lax
from jax.experimental import pallas as pl
from jax.experimental.pallas import tpu as pltpu
from jax.sharding import PartitionSpec as P

HEAD_DIM = 64
WINDOW = 64
CHUNK = 32
EPS = 1e-06
SQRT_HALF = 0.7071067811865476
INV_ROOT_TAU = 0.3989422804014327
SCALE = HEAD_DIM**-0.5
HIDE = -1e30
LOW = jnp.bfloat16
F32 = jnp.float32
VMEM_BYTES = 60 * 2**20
PEAK = 1.15e9
COSTS = {
    "group_weights_last": 0.2,
    "natural_first": 40,
    "frames_start": 40,
    "frames_grad": 40,
    "natural_last": 60,
    "send_rows": 6,
    "temporal_start": 10,
    "temporal": 30,
    "temporal_out": 6,
    "spatial_in": 8,
    "spatial": 20,
    "spatial_out": 8,
    "feed_forward": 26,
    "feed_forward_back": 10,
    "spatial_back": 28,
    "spatial_input": 20,
    "temporal_grad": 20,
    "temporal_back": 70,
    "temporal_input": 70,
    "group_weights": 0.2,
    "natural": 0.2,
    "out_weights": 0.2,
    "frames_of": 0.2,
}


def hop(values, axis, step):
    count = lax.axis_size(axis)
    return lax.ppermute(values, axis, [(i, i ^ step) for i in range(count)])


def hop_group(values):
    quarters, ranks = lax.axis_size("context"), lax.axis_size("tensor")
    pairs = [
        (c * ranks + i, c * ranks + (i ^ group_of(c))) for c in range(quarters) for i in range(ranks)
    ]
    return lax.ppermute(values, ("context", "tensor"), pairs)


def group_of(context):
    return 2 * (context % 2) + context // 2


def pick(values, index, axis=0):
    return lax.dynamic_index_in_dim(values, index, axis, keepdims=False)


def ordered(parts, me, axis=0):
    shape = list(parts[0].shape)
    shape.insert(axis, len(parts))
    out = jnp.zeros(shape, parts[0].dtype)
    for j, part in enumerate(parts):
        out = lax.dynamic_update_index_in_dim(out, part, me ^ j, axis)
    return out


def round_up(value, step):
    return -(-value // step) * step


class Place:
    def __init__(self):
        self.shard = lax.axis_index("shard")
        self.context = lax.axis_index("context")
        self.tensor = lax.axis_index("tensor")
        self.shards = lax.axis_size("shard")
        self.ranks = lax.axis_size("tensor")
        self.quarters = lax.axis_size("context")
        self.paired = self.shards == 2


def tie(values, *others):
    return lax.optimization_barrier((values,) + others)[0] if others else values


def add(*terms):
    total = terms[0].astype(F32)
    for term in terms[1:]:
        total = total + term.astype(F32)
    return total.astype(LOW)


class Gather:
    def __init__(self, place, mine):
        self.place = place
        self.parts = [mine] + [hop(mine, "tensor", k) for k in range(1, place.ranks)]

    def columns(self, *later):
        blocks = jnp.stack([tie(part, *later) for part in self.parts])
        if self.place.paired:
            self.parts = [blocks, hop(blocks, "shard", 1)]
        else:
            self.parts = [lax.all_gather(blocks, "shard", axis=2, tiled=True)]
        self.far = [hop(blocks, "context", 2)] if self.place.paired else []

    def rows(self, *later):
        self.far.append(hop(tie(self.parts[-1], *later), "context", 2))

    def cores(self, *later):
        join = lambda parts: jnp.concatenate([tie(part, *later) for part in parts], -1)
        self.first, second = join(self.parts), join(self.far)
        return [self.first, hop(self.first, "context", 1), second, hop(second, "context", 1)]


class ReduceHidden:
    def __init__(self, place, pieces):
        self.place = place
        self.kept = [pieces[0], pieces[2]]
        self.come = [hop(pieces[1], "context", 1), hop(pieces[3], "context", 1)]
        self.middle = pieces[0].shape[1] // 2
        self.half = pieces[0].shape[2] // (2 if place.paired else 1)

    def part(self, index, rows, columns):
        return add(self.kept[index][:, rows, columns], self.come[index][:, rows, columns])

    def cores(self, *later):
        self.come = [tie(item, *later) for item in self.come]
        top, low = slice(self.middle), slice(self.middle, None)
        left, right = slice(self.half), slice(self.half, None)
        out = []
        if self.place.paired:
            sent = jnp.stack([self.part(index, top, right) for index in range(2)])
            out.append(sent)
            self.come_top = hop(sent, "shard", 1)
        self.sent_low = self.part(1, low, slice(None))
        self.kept_top = lambda: jnp.stack([self.part(index, top, left) for index in range(2)])
        self.kept_low = lambda at: self.part(0, low, at)
        return out + [self.sent_low]

    def start_low(self, *later):
        self.come_low = hop(tie(self.sent_low, *later), "context", 2)

    def scatter(self, total):
        axis = total.ndim - 1
        return lax.psum_scatter(total, "shard", scatter_dimension=axis, tiled=True)

    def top_leg(self, *later):
        top = self.kept_top()
        top = add(top, tie(self.come_top, *later)) if self.place.paired else self.scatter(top)
        self.top, self.come_top = top[0], hop(top[1], "context", 2)
        return [top]

    def low_leg(self, *later):
        come = tie(self.come_low, *later)
        left, right = slice(self.half), slice(self.half, None)
        low = add(self.kept_low(left), come[..., left])
        if self.place.paired:
            sent = add(self.kept_low(right), come[..., right])
            self.come_low = hop(sent, "shard", 1)
        else:
            low, sent, self.come_low = self.scatter(low), low, None
        self.low = low
        return [low, sent]

    def both(self, *later):
        top = add(self.top, tie(self.come_top, *later))
        low = self.low if self.come_low is None else add(self.low, tie(self.come_low, *later))
        mine = jnp.concatenate([top, low], 1)
        self.kept = mine[0]
        self.come = [hop(mine[k], "tensor", k) for k in range(1, self.place.ranks)]
        return [mine]

    def hops(self, *later):
        self.sum = add(self.kept, *[tie(come, *later) for come in self.come])
        return [self.sum]

    def finish(self):
        return gather_context(self.place, self.sum)


def gather_context(place, mine):
    second = hop(mine, "context", 2)
    both = jnp.stack([mine, second])
    far = hop(both, "context", 1)
    return ordered([both[0], far[0], both[1], far[1]], place.context).astype(F32)


class ReduceShared:
    def __init__(self, place, pieces, each):
        self.place, self.each = place, each
        self.kept = [pieces[0], pieces[2]]
        self.come = [hop(pieces[1], "context", 1), hop(pieces[3], "context", 1)]

    def cores(self, *later):
        first, second = [add(a, tie(b, *later)) for a, b in zip(self.kept, self.come)]
        self.kept, self.come = first, hop(second, "context", 2)
        return [first, second]

    def rows(self, *later):
        come = tie(self.come, *later)
        if self.place.paired:
            half = come.shape[-1] // 2
            sent = add(self.kept[:, half:], come[:, half:])
            self.kept, self.come = add(self.kept[:, :half], come[:, :half]), hop(sent, "shard", 1)
            return [sent]
        self.kept = lax.psum_scatter(
            add(self.kept, come), "shard", scatter_dimension=1, tiled=True
        )
        self.come = None
        return [self.kept]

    def columns(self, more):
        mine = self.kept if self.come is None else add(self.kept, self.come)
        ranks, each = self.place.ranks, self.each
        common = jnp.concatenate([mine[ranks * each :], more])
        block = lambda k: jnp.concatenate([mine[k * each : (k + 1) * each], common])
        self.kept = block(0)
        self.come = [hop(block(k), "tensor", k) for k in range(1, ranks)]
        return [mine]

    def hops(self, *later):
        self.sum = add(self.kept, *[tie(come, *later) for come in self.come])
        return [self.sum]

    def finish(self):
        return gather_context(self.place, self.sum)


def sum_columns(place, kept, sent, *later):
    if place.paired:
        return add(kept, tie(hop(sent, "shard", 1), *later))
    return lax.psum_scatter(kept, "shard", scatter_dimension=1, tiled=True)


class SumContext:
    def __init__(self, place, total):
        self.core, self.shape = place.context % 2, total.shape
        halves = total.reshape(2, -1, total.shape[-1])
        self.kept, self.come = pick(halves, self.core), hop(pick(halves, 1 - self.core), "context", 1)

    def cores(self, *later):
        self.kept = add(self.kept, tie(self.come, *later))
        self.come = hop(self.kept, "context", 2)
        return [self.kept]

    def finish(self):
        half = add(self.kept, self.come)
        whole = ordered([half, hop(half, "context", 1)], self.core)
        return whole.reshape(self.shape).astype(F32)


class Layout:
    def __init__(self, place, clips):
        self.place = place
        self.batches, self.frames, self.places = clips.shape[:3]
        self.whole = 1 if place.paired else self.batches
        self.split = self.batches - self.whole
        self.first = self.whole * self.places
        self.later = -(-self.split * self.places // 2)
        self.slots = round_up(self.first + self.later, CHUNK)
        self.temporal_rows = self.frames * self.slots
        self.units = self.whole * self.frames + self.split
        self.frame_rows = round_up(self.units * self.places, 16)
        self.natural_blocks = self.batches * self.frames
        self.own = self.whole * self.frames * self.places // 16 * 16

    def label(self, batch, frame, spot):
        return (batch * self.frames * self.place.ranks + frame) * self.places + spot

    def split_labels(self, part, frames):
        flat = self.later * part + np.arange(self.later)[None]
        labels = self.label(
            self.whole + flat // self.places, np.asarray(frames)[:, None], flat % self.places
        )
        return np.where(flat < self.split * self.places, labels, -1)

    def frames_at(self, tensor):
        return self.frames * tensor + np.arange(self.frames)

    def temporal_labels(self, shard, tensor):
        frames = self.frames_at(tensor)
        slot = np.arange(self.first)[None]
        parts = [self.label(slot // self.places, frames[:, None], slot % self.places)]
        if self.split:
            parts.append(self.split_labels(shard, frames))
        labels = np.concatenate(parts, 1)
        spare = self.slots - labels.shape[1]
        return np.pad(labels, ((0, 0), (0, spare)), constant_values=-1)

    def frame_labels(self, shard, tensor, far=False):
        row = np.arange(self.frame_rows)
        unit, spot = row // self.places, row % self.places
        batch, frame = unit // self.frames, self.frames * tensor + unit % self.frames
        later = unit - self.whole * self.frames
        batch = np.where(later >= 0, self.whole + later, batch)
        frame = np.where(later >= 0, self.frames * tensor + shard, frame)
        inside = (unit < self.units) & ((later >= 0) | (not far))
        return np.where(inside, self.label(batch, frame, spot), -1)

    def natural_labels(self, tensor):
        batch = np.arange(self.batches)[:, None, None]
        frame = self.frames_at(tensor)[None, :, None]
        spot = np.arange(WINDOW)[None, None]
        return np.where(spot < self.places, self.label(batch, frame, spot), -1)

    def other_labels(self, shard, tensor):
        batch = np.arange(self.whole, self.batches)[:, None]
        spot = np.arange(WINDOW)[None]
        labels = self.label(batch, self.frames * tensor + shard, spot)
        return np.where(spot < self.places, labels, -1)

    def moves(self, shard, tensor):
        natural, frame = self.natural_labels(tensor), self.frame_labels(shard, tensor)
        temporal = self.temporal_labels(shard, tensor)
        moves = {
            "beginning": ([temporal], [natural]),
            "starting": ([frame], [natural]),
            "returning": ([frame], [temporal]),
            "arriving": ([temporal], [frame]),
            "homing": ([natural], [temporal]),
            "ending": ([natural], [frame]),
        }
        if self.split:
            frames, other = self.frames_at(tensor), 1 - shard

            def packed(part, frames):
                labels = self.split_labels(part, frames).reshape(-1)
                spare = round_up(labels.size, 16) - labels.size
                return np.pad(labels, (0, spare), constant_values=-1)

            mine, theirs = packed(shard, frames), packed(other, frames)
            moves["beginning"][1].append(mine)
            moves["starting"][1].append(self.other_labels(shard, tensor))
            moves["returning"][1].append(packed(other, [frames[shard]]))
            moves["arriving"][1].append(packed(shard, [frames[other]]))
            moves["homing"][1].append(theirs)
            moves["begin_far"] = ([theirs], [natural])
            moves["return_far"] = ([packed(shard, [frames[other]])], [temporal])
            moves["arrive_far"] = ([packed(other, [frames[shard]])], [frame])
            moves["home_far"] = ([mine], [temporal])
            moves["end_far"] = ([natural], [self.frame_labels(other, tensor, True)[self.own :]])
        flat = lambda parts: np.concatenate([np.asarray(part).reshape(-1) for part in parts])
        return {key: (flat(targets), flat(sources)) for key, (targets, sources) in moves.items()}

    def matrices(self):
        ranks = self.place.ranks
        shards = 2 if self.split else 1
        table = [self.moves(i // ranks, i % ranks) for i in range(shards * ranks)]
        line = lambda moves: np.concatenate([part for pair in moves.values() for part in pair])
        lines = jnp.asarray(np.stack([line(moves) for moves in table]).astype(np.int32))
        index = self.place.tensor + (ranks * self.place.shard if self.split else 0)
        labels, at, out = pick(lines, index), 0, {}
        for key, (targets, sources) in table[0].items():
            ends = at + targets.size, at + targets.size + sources.size
            target, source = labels[at : ends[0]], labels[ends[0] : ends[1]]
            same = (target[:, None] == source[None]) & (target[:, None] >= 0)
            out[key], at = same.astype(LOW), ends[1]
        return out


def call(body, outs, ins, scalars, cost=1, scratch=(), after=(), name=None, specs=None):
    given, count = body, len(ins)
    if after:
        body = lambda scalars, *refs: given(scalars, *refs[:count], *refs[count + len(after) :])
    moved = sum(item.size * item.dtype.itemsize for item in list(outs) + list(ins))
    spec = pl.BlockSpec(memory_space=pltpu.VMEM)
    return pl.pallas_call(
        body,
        name=name,
        out_shape=tuple(outs),
        in_specs=[pl.BlockSpec(memory_space=pltpu.SMEM)]
        + list(specs or [spec] * len(ins))
        + [pl.BlockSpec(memory_space=pl.ANY)] * len(after),
        out_specs=(spec,) * len(outs),
        scratch_shapes=list(scratch),
        grid=(1,) if specs else (),
        compiler_params=pltpu.CompilerParams(vmem_limit_bytes=VMEM_BYTES),
        cost_estimate=pl.CostEstimate(
            flops=int(PEAK * cost), bytes_accessed=moved if cost >= 1 else 0, transcendentals=0
        ),
    )(scalars, *ins, *after)


def shape(*dims, dtype=LOW):
    return jax.ShapeDtypeStruct(dims, dtype)


def nn(first, second):
    return lax.dot_general(first, second, (((1,), (0,)), ((), ())), preferred_element_type=F32)


def nt(first, second):
    return lax.dot_general(first, second, (((1,), (1,)), ((), ())), preferred_element_type=F32)


def tn(first, second):
    return lax.dot_general(first, second, (((0,), (0,)), ((), ())), preferred_element_type=F32)


def swapper(scalars, paired):
    def swap(values):
        if not paired:
            return values
        half = values.shape[-1] // 2
        other = jnp.concatenate([values[:, half:], values[:, :half]], -1)
        return jnp.where(scalars[0] == 0, values, other)

    return swap


def unit_of(values):
    centred = values - jnp.mean(values, -1, keepdims=True)
    inverse = lax.rsqrt(jnp.mean(centred * centred, -1, keepdims=True) + EPS)
    return (centred * inverse, inverse)


def norm_back(grad, unit, inverse, gain):
    scaled = grad * gain
    inner = (
        scaled
        - jnp.mean(scaled, -1, keepdims=True)
        - unit * jnp.mean(scaled * unit, -1, keepdims=True)
    )
    return (
        inverse * inner,
        jnp.sum(grad * unit, 0, keepdims=True),
        jnp.sum(grad, 0, keepdims=True),
    )


def attention(query, key, value, hide):
    probs = softmax(nt(key, query) + hide)
    return tn(probs.astype(LOW), value)


def softmax(scores):
    weights = jnp.exp(scores - jnp.max(scores, 0, keepdims=True))
    return weights * (1.0 / jnp.sum(weights, 0, keepdims=True))


def attention_back(query, key, value, grad, hide):
    probs = softmax(nt(key, query) + hide)
    prob_grad = nt(value, grad)
    inner = jnp.sum(probs * prob_grad, 0, keepdims=True)
    scored = (probs * (prob_grad - inner)).astype(LOW)
    return (tn(scored, key) * SCALE, nn(scored, query), nn(probs.astype(LOW), grad))


def column_sum(values):
    return jnp.sum(values.astype(F32), 0, keepdims=True)


def rows_at(start, size):
    return pl.ds(pl.multiple_of(start, 16), size)


class Program:
    def __init__(self, place, layout, width, group, scalars):
        self.place, self.layout, self.width, self.group = place, layout, width, group
        self.scalars = scalars
        self.ranks, self.quarters = place.ranks, place.quarters
        self.piece = group // self.quarters
        self.heads = group // HEAD_DIM
        self.all_heads = group * self.ranks
        spot = np.arange(self.ranks * layout.frames * CHUNK) % CHUNK
        self.same_place = jnp.asarray(
            np.where(spot[:, None] == spot[None], 0, HIDE).astype(np.float32)
        )

    def call(self, body, outs, ins, flops=0, scratch=(), after=(), specs=None, cost=None):
        name = body.__qualname__.split(".")[1]
        cost = COSTS[cost or name]
        return call(body, outs, ins, self.scalars, cost, scratch, after, name, specs)

    def lanes(self, c, h):
        at = c * self.group + h * HEAD_DIM
        return slice(at, at + HEAD_DIM)


    def live(self, scalars, batch):
        return scalars[3 + batch] > 0

    def place_natural(self, scalars, rows, source):
        lay = self.layout
        rows[...] = jnp.zeros_like(rows)
        for item in range(lay.natural_blocks):

            @pl.when(self.live(scalars, item // lay.frames))
            def _(item=item):
                rows[item * WINDOW : item * WINDOW + lay.places] = source[item]

    def send_rows(self, clips, cotangents, matrix, wait=()):
        lay, width = self.layout, self.width
        count, split = lay.natural_blocks, lay.split
        first = lay.whole * lay.frames

        def body(scalars, clips_ref, grads_ref, matrix_ref, sent, frames, rows):
            self.place_natural(scalars, rows, clips_ref)
            sent[...] = nn(matrix_ref[...], rows[...]).astype(LOW)
            for index, source in enumerate((clips_ref, grads_ref)):
                for item in range(split):
                    frame = first + lay.frames * item + 1 - scalars[0]
                    frames[index, item] = source[frame]

        outs = [shape(matrix.shape[0], width), shape(2, split, lay.places, width)]
        scratch = [pltpu.VMEM((count * WINDOW, width), LOW)]
        return self.call(body, outs, [clips, cotangents, matrix], scratch=scratch, after=wait)

    def temporal_start(self, clips, come, matrix):
        lay, width = self.layout, self.width
        count, rows_in = lay.natural_blocks, lay.natural_blocks * WINDOW
        more = 0 if come is None else come.shape[0]

        def body(scalars, clips_ref, *refs):
            matrix_ref, start_ref, normed_ref, rows = refs[-4:]
            self.place_natural(scalars, rows, clips_ref)
            if more:
                rows[rows_in:] = refs[0][...]
            start = nn(matrix_ref[...], rows[...])
            start_ref[...] = start.astype(LOW)
            unit, _ = unit_of(start)
            swap = swapper(scalars, self.place.paired)
            normed_ref[...] = swap(unit).astype(LOW)

        outs = [shape(lay.temporal_rows, width)] * 2
        ins = [clips] + ([come] if more else []) + [matrix]
        scratch = [pltpu.VMEM((rows_in + more, width), LOW)]
        return self.call(body, outs, ins, scratch=scratch)

    def frames_of(self, clips, others, index, matrix, cost, wait=()):
        lay, width = self.layout, self.width
        count, split = lay.natural_blocks, lay.split

        def body(scalars, clips_ref, *refs):
            matrix_ref, out_ref, rows = refs[-3:]
            self.place_natural(scalars, rows, clips_ref)
            for item in range(split):

                @pl.when(jnp.logical_not(self.live(scalars, lay.whole + item)))
                def _(item=item):
                    start = (count + item) * WINDOW
                    rows[start : start + lay.places] = refs[0][index, item]

            out_ref[...] = nn(matrix_ref[...], rows[...]).astype(LOW)

        return self.call(
            body,
            [shape(lay.frame_rows, width)],
            [clips] + ([others] if split else []) + [matrix],
            scratch=[pltpu.VMEM(((count + split) * WINDOW, width), LOW)],
            after=wait,
            cost=cost,
        )[0]


    def chunk(self, refs, n):
        lay = self.layout
        return jnp.concatenate(
            [
                ref[rows_at(frame * lay.slots + n * CHUNK, CHUNK)]
                for ref in refs
                for frame in range(lay.frames)
            ]
        )

    def put_chunk(self, refs, n, values):
        lay = self.layout
        for k, ref in enumerate(refs):
            for frame in range(lay.frames):
                at = (k * lay.frames + frame) * CHUNK
                ref[rows_at(frame * lay.slots + n * CHUNK, CHUNK)] = values[at : at + CHUNK]

    def temporal(self, units, weights, along, shift, wait=()):
        lay, width, group, ranks = self.layout, self.width, self.group, self.ranks
        rows = lay.temporal_rows

        def body(scalars, *refs):
            unit_refs, weight_refs = refs[:ranks], refs[ranks : ranks + len(weights)]
            refs = refs[ranks + len(weights) :]
            along_ref, shift_ref, same, refs = refs[0], refs[1], refs[2], refs[3:]
            qkv_refs, mixed_refs, normed_refs, out_refs = (
                refs[at : at + ranks] for at in range(0, 4 * ranks, ranks)
            )
            swap = swapper(scalars, self.place.paired)
            gain, move = swap(along_ref[0:1]), swap(along_ref[3:4])
            weight = jnp.concatenate([ref[: 3 * group] for ref in weight_refs], -1)
            for k in range(ranks):
                normed_refs[k][...] = (unit_refs[k][...].astype(F32) * gain + move).astype(LOW)
                qkv_refs[k][...] = (nt(normed_refs[k][...], weight) + shift_ref[...]).astype(LOW)

            @pl.loop(0, lay.slots // CHUNK, unroll=True)
            def _(n):
                values = self.chunk(qkv_refs, n)
                parts = []
                for h in range(self.heads):
                    query, key, value = (values[:, self.lanes(c, h)] for c in range(3))
                    parts.append(attention(query * LOW(SCALE), key, value, same[...]))
                self.put_chunk(mixed_refs, n, jnp.concatenate(parts, -1).astype(LOW))

            weight = jnp.concatenate([ref[3 * group : 4 * group] for ref in weight_refs], -1)
            for k in range(ranks):
                out_refs[k][...] = nn(mixed_refs[k][...], weight).astype(LOW)

        outs = [shape(rows, 3 * group)] * ranks + [shape(rows, group)] * ranks
        outs += [shape(rows, width)] * (2 * ranks)
        ins = list(units) + list(weights) + [along, shift, self.same_place]
        flops = 8 * ranks * rows * width * group
        flops += 4 * ranks * rows * self.same_place.shape[0] * group
        outs = self.call(body, outs, ins, flops, after=wait)
        return [outs[at : at + ranks] for at in range(0, 4 * ranks, ranks)]

    def temporal_out(self, parts, along, matrix, wait=()):
        lay, width = self.layout, self.width
        far = [] if matrix is None else [matrix]

        def body(scalars, *refs):
            part_refs, along_ref, refs = refs[: self.ranks], refs[self.ranks], refs[self.ranks + 1 :]
            swap = swapper(scalars, self.place.paired)
            total = swap(sum(ref[...].astype(F32) for ref in part_refs)) + along_ref[6:7]
            out_ref = refs[len(far)]
            out_ref[...] = total.astype(LOW)
            if far:
                refs[2][...] = nn(refs[0][...], out_ref[...]).astype(LOW)

        outs = [shape(lay.temporal_rows, width)] + [shape(item.shape[0], width) for item in far]
        return self.call(body, outs, list(parts) + [along] + far, after=wait)

    def temporal_grad(self, parts, matrix, wait=()):
        lay, width = self.layout, self.width

        def body(scalars, *refs):
            matrix_ref, out_ref = refs[len(parts) :]
            swap = swapper(scalars, self.place.paired)
            source = jnp.concatenate([ref[...] for ref in refs[: len(parts)]])
            out_ref[...] = swap(nn(matrix_ref[...], source)).astype(LOW)

        outs = [shape(lay.temporal_rows, width)]
        return self.call(body, outs, list(parts) + [matrix], after=wait)[0]

    def temporal_back(self, qkv, grads, units, weights, wait=()):
        lay, width, group, ranks = self.layout, self.width, self.group, self.ranks
        rows = lay.temporal_rows

        def body(scalars, *refs):
            qkv_refs, grad_refs, unit_refs = (
                refs[at : at + ranks] for at in range(0, 3 * ranks, ranks)
            )
            refs = refs[3 * ranks :]
            weight_refs, same, refs = refs[: len(weights)], refs[len(weights)], refs[len(weights) + 1 :]
            out_refs, back_refs, sums = refs[:ranks], refs[ranks : 2 * ranks], refs[2 * ranks]
            mixed = refs[2 * ranks + 1 :]
            weight = jnp.concatenate([ref[3 * group : 4 * group] for ref in weight_refs], -1)
            for k in range(ranks):
                mixed[k][...] = nt(grad_refs[k][...], weight).astype(LOW)

            @pl.loop(0, lay.slots // CHUNK, unroll=True)
            def _(n):
                values, grads = self.chunk(qkv_refs, n), self.chunk(mixed, n)
                parts = [[], [], []]
                for h in range(self.heads):
                    query, key, value = (values[:, self.lanes(c, h)] for c in range(3))
                    grad = grads[:, self.lanes(0, h)]
                    got = attention_back(query * LOW(SCALE), key, value, grad, same[...])
                    for part, item in zip(parts, got):
                        part.append(item)
                total = jnp.concatenate(parts[0] + parts[1] + parts[2], -1)
                self.put_chunk(out_refs, n, total.astype(LOW))

            weight = jnp.concatenate([ref[: 3 * group] for ref in weight_refs], -1)
            sums[...] = jnp.zeros_like(sums)
            for k in range(ranks):
                back = nn(out_refs[k][...], weight)
                back_refs[k][...] = back.astype(LOW)
                sums[0:1] += column_sum(back * unit_refs[k][...].astype(F32))
                sums[1:2] += column_sum(back)

        outs = [shape(rows, 3 * group)] * ranks + [shape(rows, width)] * ranks
        outs += [shape(8, width, dtype=F32)]
        ins = list(qkv) + list(grads) + list(units) + list(weights) + [self.same_place]
        flops = 8 * ranks * rows * width * group
        flops += 10 * ranks * rows * self.same_place.shape[0] * group
        scratch = [pltpu.VMEM((rows, group), LOW)] * ranks
        outs = self.call(body, outs, ins, flops, scratch, wait)
        return outs[:ranks], outs[ranks : 2 * ranks], outs[-1]

    def group_weights(self, qkv_grads, normed, mixed=(), out_grads=(), more=(), wait=(), cost=None):
        width, group, count = self.width, self.group, len(qkv_grads)
        parts = 2 if self.place.paired else 1
        size = 3 * group + (group if mixed else 0)

        def body(scalars, *refs):
            refs = list(refs)
            take = lambda n: [refs.pop(0) for _ in range(n)]
            grad_refs, normed_refs = take(count), take(count)
            mixed_refs, out_grad_refs = take(len(mixed)), take(len(mixed))
            more_refs, (spread,), out_refs = take(len(more)), take(1), refs
            columns = width // parts

            def put(start, total):
                for part in range(parts):
                    values = total[:, part * columns : (part + 1) * columns]
                    out_refs[part][start : start + total.shape[0]] = values.astype(LOW)

            total = jnp.zeros((3 * group, width), F32)
            sums = jnp.zeros((1, 3 * group), F32)
            for j in range(count):
                total = total + tn(grad_refs[j][...], normed_refs[j][...])
                sums = sums + column_sum(grad_refs[j][...])
            put(0, total)
            if mixed:
                total = jnp.zeros((group, width), F32)
                for j in range(count):
                    total = total + tn(mixed_refs[j][...], out_grad_refs[j][...])
                put(3 * group, total)
            line = jnp.concatenate([sums[:, :group], sums[:, 2 * group :]], -1)
            top = lax.broadcasted_iota(jnp.int32, (16, 2 * group), 0) == 0
            line = jnp.where(top, line, 0.0).astype(LOW)
            for part in range(parts):
                out_refs[part][size : size + 16] = line if parts == 2 else nn(line, spread[...]).astype(LOW)
                for ref in more_refs:
                    rows = ref[:, part * columns : (part + 1) * columns]
                    rows = jnp.concatenate([rows, jnp.zeros_like(rows)])
                    out_refs[part][size + 16 :] = rows.astype(LOW)
                if not more:
                    out_refs[part][size + 16 :] = jnp.zeros((16, columns), LOW)

        outs = [shape(size + 32, width // parts)] * parts
        rows = qkv_grads[0].shape[0]
        ins = list(qkv_grads) + list(normed) + list(mixed) + list(out_grads) + list(more)
        ins += [self.spread()]
        flops = 2 * count * rows * width * size
        return self.call(body, outs, ins, flops, after=wait, cost=cost)

    def spread(self):
        shards = self.place.shards
        columns, part = self.width // shards, HEAD_DIM // shards
        out = np.zeros((2 * self.group, self.width), np.float32)
        for item in range(2 * self.group):
            head, feature = divmod(item, HEAD_DIM)
            out[item, feature // part * columns + head * part + feature % part] = 1
        return jnp.asarray(out, LOW)

    def temporal_input(self, backs, start, along, matrix, wait=()):
        lay, width = self.layout, self.width
        far = [] if matrix is None else [matrix]

        def body(scalars, *refs):
            back_refs, refs = refs[: self.ranks], refs[self.ranks :]
            start_ref, along_ref, refs = refs[0], refs[1], refs[2:]
            out_ref = refs[len(far)]
            swap = swapper(scalars, self.place.paired)
            unit, inverse = unit_of(start_ref[...].astype(F32))
            grad = swap(sum(ref[...].astype(F32) for ref in back_refs))
            back, _, _ = norm_back(grad, unit, inverse, along_ref[0:1])
            out_ref[...] = back.astype(LOW)
            if far:
                refs[2][...] = nn(refs[0][...], out_ref[...]).astype(LOW)

        outs = [shape(lay.temporal_rows, width)] + [shape(item.shape[0], width) for item in far]
        return self.call(body, outs, list(backs) + [start, along] + far, after=wait)


    def spatial_in(self, sources, matrix, start, fc, along, wait=()):
        lay, width = self.layout, self.width
        rows = lay.frame_rows

        def body(scalars, *refs):
            source_refs, refs = refs[: len(sources)], refs[len(sources) :]
            matrix_ref, start_ref, fc_refs, refs = refs[0], refs[1], refs[2 : 2 + len(fc)], refs[2 + len(fc) :]
            along_ref, after_ref, temporal_ref, normed_ref = refs
            swap = swapper(scalars, self.place.paired)
            source = jnp.concatenate([ref[...] for ref in source_refs])
            temporal = nn(matrix_ref[...], source)
            temporal_ref[...] = temporal.astype(LOW)
            weight = jnp.concatenate([ref[...] for ref in fc_refs])
            after = start_ref[...].astype(F32) + nn(swap(temporal).astype(LOW), weight)
            after = after + along_ref[7:8]
            after_ref[...] = after
            unit, _ = unit_of(after)
            normed_ref[...] = swap(unit * along_ref[1:2] + along_ref[4:5]).astype(LOW)

        outs = [shape(rows, width, dtype=F32), shape(rows, width), shape(rows, width)]
        ins = list(sources) + [matrix, start] + list(fc) + [along]
        return self.call(body, outs, ins, 2 * rows * width * width, after=wait)

    def windows(self, refs, n):
        at = rows_at(n * (WINDOW - 16), WINDOW)
        return jnp.concatenate([ref[at] for ref in refs])

    def window_mask(self, n, axis):
        size = self.quarters * WINDOW
        dims = (size, 1) if axis == 0 else (1, size)
        index = lax.broadcasted_iota(jnp.int32, dims, axis) & (WINDOW - 1)
        start = n * (self.layout.places - WINDOW + 16)
        return (index >= start) & (index < start + self.layout.places)

    def put_windows(self, refs, n, values, mask):
        for j, ref in enumerate(refs):
            at = rows_at(n * (WINDOW - 16), WINDOW)
            part = slice(j * WINDOW, (j + 1) * WINDOW)
            old = ref[at].astype(F32)
            ref[at] = jnp.where(mask[part], values[part], old).astype(LOW)

    def spatial(self, normed, win, shift, wait=()):
        lay, width, quarters, group = self.layout, self.width, self.quarters, self.group

        def body(scalars, *refs):
            normed_refs, refs = refs[:quarters], refs[quarters:]
            win_refs, shift_ref, refs = refs[: len(win)], refs[len(win)], refs[len(win) + 1 :]
            qkv_refs, out_refs = refs[:quarters], refs[quarters:]
            weight = jnp.concatenate([ref[: 3 * group] for ref in win_refs], -1)
            for j in range(quarters):
                qkv_refs[j][...] = (nt(normed_refs[j][...], weight) + shift_ref[...]).astype(LOW)
                out_refs[j][...] = jnp.zeros_like(out_refs[j])

            @pl.loop(0, lay.units, unroll=True)
            def _(n):
                rows = self.windows(qkv_refs, n)
                hide = jnp.where(self.window_mask(n, 0), 0.0, HIDE)
                parts = []
                for h in range(self.heads):
                    query, key, value = (rows[:, self.lanes(c, h)] for c in range(3))
                    parts.append(attention(query * LOW(SCALE), key, value, hide))
                mask = self.window_mask(n, 0)
                self.put_windows(out_refs, n, jnp.concatenate(parts, -1), mask)

        outs = [shape(lay.frame_rows, 3 * group)] * quarters
        outs += [shape(lay.frame_rows, group)] * quarters
        size = quarters * WINDOW
        flops = 6 * quarters * lay.frame_rows * width * group + 4 * lay.units * size * size * group
        outs = self.call(body, outs, list(normed) + list(win) + [shift], flops, after=wait)
        return outs[:quarters], outs[quarters:]

    def spatial_back(self, qkv, grads, win, wait=()):
        lay, width, quarters, group = self.layout, self.width, self.quarters, self.group

        def body(scalars, *refs):
            qkv_refs, grad_refs = refs[:quarters], refs[quarters : 2 * quarters]
            win_refs = refs[2 * quarters : 2 * quarters + len(win)]
            refs = refs[2 * quarters + len(win) :]
            out_refs, back_refs = refs[:quarters], refs[quarters:]
            for ref in out_refs:
                ref[...] = jnp.zeros_like(ref)

            @pl.loop(0, lay.units, unroll=True)
            def _(n):
                rows = self.windows(qkv_refs, n)
                mask = self.window_mask(n, 0)
                grads = self.windows(grad_refs, n) * mask.astype(F32).astype(LOW)
                hide = jnp.where(self.window_mask(n, 0), 0.0, HIDE)
                parts = [[], [], []]
                for h in range(self.heads):
                    query, key, value = (rows[:, self.lanes(c, h)] for c in range(3))
                    grad = grads[:, self.lanes(0, h)]
                    got = attention_back(query * LOW(SCALE), key, value, grad, hide)
                    for part, item in zip(parts, got):
                        part.append(item)
                values = jnp.concatenate(parts[0] + parts[1] + parts[2], -1)
                self.put_windows(out_refs, n, values, mask)

            weight = jnp.concatenate([ref[: 3 * group] for ref in win_refs], -1)
            for j in range(quarters):
                back_refs[j][...] = nn(out_refs[j][...], weight).astype(LOW)

        outs = [shape(lay.frame_rows, 3 * group)] * quarters
        outs += [shape(lay.frame_rows, width)] * quarters
        size = quarters * WINDOW
        flops = 10 * lay.units * size * size * group
        flops += 6 * quarters * lay.frame_rows * width * group
        outs = self.call(body, outs, list(qkv) + list(grads) + list(win), flops, after=wait)
        return outs[:quarters], outs[quarters:]

    def put_groups(self, scalars, out, pieces, first):
        for i in range(self.quarters):
            spot = (scalars[1] ^ i) * self.piece
            for j in range(self.quarters):
                k = group_of(scalars[1]) ^ group_of(j)
                out[rows_at(j * self.group + spot, self.piece)] = pieces[i][
                    k, first : first + self.piece
                ]

    def spatial_out(self, mixed, pieces, first, after, grad, along, wait=()):
        lay, width, group = self.layout, self.width, self.group
        rows, quarters = lay.frame_rows, self.quarters
        size = WINDOW

        def body(scalars, *refs):
            mixed_refs, piece_refs, refs = refs[:quarters], refs[quarters : 2 * quarters], refs[2 * quarters :]
            after_ref, grad_ref, along_ref, out_ref, normed_ref, low_ref, wout = refs
            swap = swapper(scalars, self.place.paired)
            self.put_groups(scalars, wout, piece_refs, 0)
            total = jnp.zeros((rows, width), F32)
            for j in range(quarters):
                total = total + nn(mixed_refs[j][...], wout[j * group : (j + 1) * group])
            after = after_ref[...] + swap(total) + along_ref[8:9]
            out_ref[...] = after
            unit, _ = unit_of(after)
            normed_ref[...] = swap(unit * along_ref[2:3] + along_ref[5:6]).astype(LOW)
            low_ref[...] = swap(grad_ref[...].astype(F32)).astype(LOW)

        outs = [
            shape(rows, width, dtype=F32),
            shape(rows, width),
            shape(rows, width),
            shape(self.all_heads, width),
        ]
        ins = list(mixed) + list(pieces) + [after, grad, along]
        whole = pl.BlockSpec(memory_space=pltpu.VMEM)
        part = pl.BlockSpec((self.ranks, size, width), lambda *_: (0, first // size, 0))
        specs = [whole] * quarters + [part] * quarters + [whole] * 3
        flops = 2 * rows * width * self.all_heads
        return self.call(body, outs, ins, flops, after=wait, specs=specs)

    def feed_forward(self, normed, grad, pieces, shifts, totals):
        lay, width = self.layout, self.width
        rows, count, ranks = lay.frame_rows, len(pieces), self.ranks
        hidden = shifts[0].shape[1]
        unit = hidden // ranks
        tile = hidden

        def body(scalars, normed_ref, grad_ref, *refs):
            refs = list(refs)
            take = lambda n: [refs.pop(0) for _ in range(n)]
            piece_refs, shift_refs = take(count), take(count)
            before = take(2 if totals else 0)
            out_ref, back_ref = take(2)
            grad_refs, sum_refs = take(count), take(count)
            ups, downs, up_grad, down_grad = take(4)
            out_ref[...] = before[0][...] if totals else jnp.zeros_like(out_ref)
            back_ref[...] = before[1][...] if totals else jnp.zeros_like(back_ref)
            for item in range(count):
                for k in range(ranks):
                    at = slice(k * unit, (k + 1) * unit)
                    ups[at] = piece_refs[item][k, :unit]
                    downs[at] = piece_refs[item][k, unit : 2 * unit]

                @pl.loop(0, hidden // tile)
                def _(m, item=item):
                    at = pl.ds(pl.multiple_of(m * tile, tile), tile)
                    up, down = ups[at], downs[at]
                    values = nt(normed_ref[...], up) + shift_refs[item][:, at]
                    half = 0.5 * (1.0 + lax.erf(values * SQRT_HALF))
                    active = (values * half).astype(LOW)
                    slope = half + values * jnp.exp(-0.5 * values * values) * INV_ROOT_TAU
                    out_ref[...] += nn(active, down)
                    down_grad[at] = tn(active, grad_ref[...]).astype(LOW)
                    hidden_grad = (nt(grad_ref[...], down) * slope).astype(LOW)
                    up_grad[at] = tn(hidden_grad, normed_ref[...]).astype(LOW)
                    back_ref[...] += nn(hidden_grad, up)
                    sum_refs[item][:, at] = column_sum(hidden_grad)

                for k in range(ranks):
                    at = slice(k * unit, (k + 1) * unit)
                    grad_refs[item][k, :unit] = up_grad[at]
                    grad_refs[item][k, unit:] = down_grad[at]

        outs = [shape(rows, width, dtype=F32)] * 2
        outs += [shape(ranks, 2 * unit, width)] * count + [shape(1, hidden, dtype=F32)] * count
        ins = [normed, grad] + list(pieces) + list(shifts) + list(totals or ())
        flops = 12 * rows * width * hidden * count
        scratch = [pltpu.VMEM((hidden, width), LOW)] * 4
        outs = self.call(body, outs, ins, flops, scratch)
        return outs[:2], outs[2 : 2 + count], outs[2 + count :]

    def feed_forward_back(self, after, out, back, grad, mixed, wout, along):
        lay, width, group = self.layout, self.width, self.group
        rows, quarters = lay.frame_rows, self.quarters

        def body(scalars, after_ref, out_ref, back_ref, grad_ref, wout_ref, along_ref, *refs):
            mixed_refs, refs = refs[:quarters], refs[quarters:]
            layer_ref, total_ref, sums, wout_grad = refs[:4]
            mixed_grads = refs[4:]
            swap = swapper(scalars, self.place.paired)
            after = after_ref[...]
            layer_ref[...] = (after + swap(out_ref[...]) + along_ref[9:10]).astype(LOW)
            unit, inverse = unit_of(after)
            back, gain, shift = norm_back(swap(back_ref[...]), unit, inverse, along_ref[2:3])
            grad = grad_ref[...].astype(F32)
            total = grad + back
            total_ref[...] = total
            low = total.astype(LOW)
            sums[0:1] = gain
            sums[1:2] = shift
            sums[2:3] = column_sum(low)
            sums[3:4] = column_sum(grad)
            turned = swap(low.astype(F32)).astype(LOW)
            for j in range(quarters):
                at = slice(j * group, (j + 1) * group)
                mixed_grads[j][...] = nt(turned, wout_ref[at]).astype(LOW)
                wout_grad[at] = tn(mixed_refs[j][...], turned).astype(LOW)

        outs = [
            shape(rows, width),
            shape(rows, width, dtype=F32),
            shape(4, width, dtype=F32),
            shape(self.all_heads, width),
        ] + [shape(rows, group)] * quarters
        ins = [after, out, back, grad, wout, along] + list(mixed)
        outs = self.call(body, outs, ins, 4 * rows * width * self.all_heads)
        return outs[:4], outs[4:]

    def spatial_input(self, backs, after, total, along, fc, matrix, wait=()):
        lay, width = self.layout, self.width
        rows, quarters = lay.frame_rows, self.quarters
        far = [] if matrix is None else [matrix]

        def body(scalars, *refs):
            back_refs, refs = refs[:quarters], refs[quarters:]
            after_ref, total_ref, along_ref, refs = refs[0], refs[1], refs[2], refs[3:]
            fc_refs, refs = refs[: len(fc)], refs[len(fc) :]
            low_ref, out_ref, sums = refs[len(far) : len(far) + 3]
            swap = swapper(scalars, self.place.paired)
            grad = swap(sum(ref[...].astype(F32) for ref in back_refs))
            unit, inverse = unit_of(after_ref[...])
            back, gain, shift = norm_back(grad, unit, inverse, along_ref[1:2])
            low = (total_ref[...] + back).astype(LOW)
            low_ref[...] = low
            weight = jnp.concatenate([ref[...] for ref in fc_refs])
            temporal = swap(nt(low, weight)).astype(LOW)
            out_ref[...] = temporal
            sums[0:1] = gain
            sums[1:2] = shift
            sums[2:3] = column_sum(temporal)
            sums[3:4] = column_sum(low)
            if far:
                refs[4][...] = nn(refs[0][...], temporal).astype(LOW)

        outs = [shape(rows, width), shape(rows, width), shape(4, width, dtype=F32)]
        outs += [shape(item.shape[0], width) for item in far]
        ins = list(backs) + [after, total, along] + list(fc) + far
        return self.call(body, outs, ins, 2 * rows * width * width, after=wait)

    def out_weights(self, wout_grad, low, temporal, vectors, wait=()):
        width, group, piece = self.width, self.group, self.piece
        quarters, ranks = self.quarters, self.ranks
        extra, quarter = vectors.shape[1], width // quarters
        each = piece + extra

        def body(scalars, wout_ref, low_ref, temporal_ref, vectors_ref, *refs):
            pieces, fc = refs[:quarters], refs[quarters]
            swap = swapper(scalars, self.place.paired)
            turned = swap(temporal_ref[...].astype(F32)).astype(LOW)
            fc[...] = tn(low_ref[...], turned).astype(LOW)
            for i in range(quarters):
                spot = (scalars[1] ^ i) * piece
                for j in range(quarters):
                    k = group_of(scalars[1]) ^ group_of(j)
                    pieces[i][rows_at(k * each, piece)] = wout_ref[rows_at(j * group + spot, piece)]
                for k in range(ranks):
                    pieces[i][k * each + piece : (k + 1) * each] = vectors_ref[k]
                pieces[i][ranks * each :] = fc[rows_at((scalars[1] ^ i) * quarter, quarter)]

        outs = [shape(ranks * each + quarter, width)] * quarters
        ins = [wout_grad, low, temporal, vectors]
        flops = 2 * low.shape[0] * width * width
        return self.call(body, outs, ins, flops, [pltpu.VMEM((width, width), LOW)], wait)

    def natural(self, parts, cost, wait=()):
        lay, width = self.layout, self.width
        count = lay.natural_blocks
        counts = [len(rows) for _, rows in parts]

        def body(scalars, *refs):
            refs = list(refs)
            out_ref = refs.pop()
            total = jnp.zeros((count * WINDOW, width), F32)
            for size in counts:
                matrix = refs.pop(0)
                source = jnp.concatenate([refs.pop(0)[...] for _ in range(size)])
                total = total + nn(matrix[...], source)
            total = total.astype(LOW)
            for item in range(count):
                part = total[item * WINDOW : item * WINDOW + lay.places]
                out_ref[item] = part

                @pl.when(jnp.logical_not(self.live(scalars, item // lay.frames)))
                def _(item=item):
                    out_ref[item] = jnp.zeros((lay.places, width), LOW)


        ins = []
        for matrix, rows in parts:
            ins += [matrix] + list(rows)
        return self.call(body, [shape(count, lay.places, width)], ins, after=wait, cost=cost)[0]


def body(
    clip_input,
    clip_slot,
    norm_gain,
    norm_shift,
    attention_in,
    attention_bias,
    attention_out,
    branch_bias,
    temporal_fc,
    hidden_in,
    hidden_bias,
    hidden_out,
    output_grad,
):
    place = Place()
    shards, quarters, ranks = place.shards, place.quarters, place.ranks
    shard, context, tensor = place.shard, place.context, place.tensor
    clips, cotangents = clip_input[:, 0], output_grad[:, 0]
    lay = Layout(place, clips)
    columns = attention_in.shape[1]
    width = columns * shards
    group = attention_in.shape[3]
    heads = group // HEAD_DIM
    hidden = hidden_in.shape[1]
    piece = group // quarters
    scalars = jnp.concatenate([jnp.stack([shard, context, tensor]), clip_slot[:, 0]])
    prog = Program(place, lay, width, group, scalars.astype(jnp.int32))
    moves = lay.matrices()
    split = lay.split > 0

    def beside(rows):
        return [rows, hop(rows, "shard", 1)] if split else [rows]

    def swapped(rows, axis):
        return [rows[0]] + [hop(rows[k], axis, k) for k in range(1, len(rows))]

    def to_all(rows, axis):
        if axis == "context":
            far = hop(rows, axis, 2)
            return [rows, hop(rows, axis, 1), far, hop(far, axis, 1)]
        return [rows] + [hop(rows, axis, k) for k in range(1, ranks)]

    def shard_parts(block, axis=1):
        if place.paired:
            return [block, hop(block, "shard", 1)]
        return [lax.all_gather(block, "shard", axis=axis, tiled=True)]

    def bias_rows(index):
        rows = attention_bias[index].reshape(-1)
        return jnp.pad(rows, (0, columns - rows.size))[None]

    def in_rows(index):
        return jnp.transpose(attention_in[index], (1, 2, 0)).reshape(3 * group, columns)

    def bias_of(parts, row):
        kinds = 2 * heads * (HEAD_DIM // shards)
        if place.paired:
            lines = [part[row, :kinds] for part in parts]
            lines = jnp.where(shard == 0, jnp.stack(lines), jnp.stack(lines[::-1]))
        else:
            lines = parts[0][row].reshape(shards, columns)[:, :kinds]
        lines = lines.reshape(shards, 2, heads, HEAD_DIM // shards)
        lines = jnp.transpose(lines, (1, 2, 0, 3)).reshape(2, group).astype(F32)
        return jnp.concatenate([lines[0], jnp.zeros(group, F32), lines[1]])[None]

    flat = lambda rows: rows.reshape((-1,) + rows.shape[2:])
    clips, cotangents = flat(clips), flat(cotangents)
    quarter = lambda rows: pick(rows.reshape(quarters, -1, columns), context)
    up_part = pick(hidden_in.reshape(columns, quarters, -1), context, 1).T
    unit = up_part.shape[0]
    block = [up_part, quarter(hidden_out), quarter(attention_out[1])]
    block.append(jnp.pad(hidden_bias.reshape(1, -1), ((0, 15), (0, 0))))
    gather_c = Gather(place, jnp.concatenate(block))

    along = jnp.concatenate([norm_gain, norm_shift, branch_bias, bias_rows(0)])
    along = shard_parts(jnp.pad(along, ((0, 16 - along.shape[0]), (0, 0))))
    shift_a = bias_of(along, 10)
    if place.paired:
        along = jnp.where(shard == 0, *[jnp.concatenate(pair, -1) for pair in (along, along[::-1])])
    else:
        along = along[0]
    along = along[:10].astype(F32)

    come, others = None, None
    if split:
        sent, others = prog.send_rows(clips, cotangents, moves["begin_far"])
        come = hop(sent, "shard", 1)
    weights_a = jnp.concatenate([in_rows(0), attention_out[0]])
    weights_a = shard_parts(tie(weights_a, come) if split else weights_a)
    start_t, unit_a = prog.temporal_start(clips, come, moves["beginning"])
    units_a = to_all(unit_a, "tensor")
    gather_c.columns(unit_a)
    gather_c.rows()

    qkv_a, mixed_a, normed_a, parts = prog.temporal(
        units_a, weights_a, along, shift_a
    )
    fc = shard_parts(tie(temporal_fc, parts[0]), 0)
    if split:
        others = hop(tie(others, units_a[1]), "shard", 1)
    temporal_t = prog.temporal_out(
        swapped(parts, "tensor"), along, moves.get("return_far"), gather_c.far
    )
    sources = [temporal_t[0]] + [hop(rows, "shard", 1) for rows in temporal_t[1:]]
    in_b = jnp.concatenate([in_rows(1), jnp.pad(bias_rows(1), ((0, 15), (0, 0)))])
    in_b = hop_group(tie(in_b, sources[-1]))
    weights_b = shard_parts(in_b)
    shift_b = bias_of(weights_b, 3 * group)

    start = prog.frames_of(clips, others, 0, moves["starting"], "frames_start", [units_a[1]])
    after_a, temporal, normed_b = prog.spatial_in(
        sources, moves["returning"], start, fc, along
    )
    normed_b = to_all(normed_b, "context")
    qkv_b, mixed = prog.spatial(normed_b, weights_b, shift_b)
    mixed = swapped(mixed, "context")
    grad = prog.frames_of(
        cotangents, others, 1, moves["starting"], "frames_grad", [parts[0]]
    )
    pieces_c = gather_c.cores(after_a)
    line = gather_c.first[:, 2 * unit + piece].astype(F32)
    up_shift = line.reshape((ranks, shards) + hidden_bias.shape)
    if place.paired:
        up_shift = jnp.where(shard == 0, up_shift, up_shift[:, ::-1])
    up_shift = jnp.swapaxes(up_shift, 1, 2).reshape(ranks, quarters, unit)
    up_shift = [pick(up_shift, context ^ j, 1).reshape(1, -1) for j in range(quarters)]
    after_b, normed_c, low, wout_b = prog.spatial_out(
        mixed, pieces_c, 2 * unit, after_a, grad, along
    )

    totals = None
    piece_grads, up_bias_grads = [None] * quarters, [None] * quarters
    for pair in ((1, 3), (0, 2)):
        totals, grads, sums = prog.feed_forward(
            normed_c, low, [pieces_c[j] for j in pair], [up_shift[j] for j in pair], totals
        )
        for index, j in enumerate(pair):
            piece_grads[j] = grads[index]
            up_bias_grads[j] = sums[index]
    reduce_c = ReduceHidden(place, piece_grads)
    kept, mixed_grads = prog.feed_forward_back(
        after_b, totals[0], totals[1], grad, mixed, wout_b, along
    )
    layer_rows, total, sums_c, wout_grad = kept
    wait = reduce_c.cores(layer_rows)

    mixed_grads = swapped(mixed_grads, "context")
    qkv_grads, backs = prog.spatial_back(qkv_b, mixed_grads, weights_b, wait)
    done = backs[0]
    reduce_c.start_low(done)
    backs = swapped(backs, "context")
    group_grads = prog.group_weights(qkv_grads, normed_b, wait=[reduce_c.come_top] if split else ())
    low_total, temporal_grad, sums_b, *sent = prog.spatial_input(
        backs, after_a, total, along, fc, moves.get("arrive_far"), [group_grads[0]]
    )

    sources = [temporal_grad] + [hop(rows, "shard", 1) for rows in sent]
    out_grad = prog.temporal_grad(sources, moves["arriving"])
    out_grads = to_all(out_grad, "tensor")
    layer_out, home = [(moves["ending"], [layer_rows])], [(moves["ending"], [low_total])]
    if split:
        far = hop(tie(jnp.concatenate([layer_rows[lay.own :], low_total[lay.own :]]), out_grad), "shard", 1)
        layer_out.append((moves["end_far"], [far[: far.shape[0] // 2]]))
        home.append((moves["end_far"], [far[far.shape[0] // 2 :]]))
    layer_out = prog.natural(layer_out, "natural_first", [out_grad])
    grads_b = group_grads
    sums = [sums_b[0], sums_c[0], sums_b[1], sums_c[1], sums_b[2], sums_b[3], sums_c[2], sums_c[3]]
    outer = ordered([item.reshape(ranks, -1) for item in up_bias_grads], context, 1)
    outer = outer.reshape(ranks, -1, shards, hidden_bias.shape[1])
    outer = jnp.swapaxes(outer, 1, 2).reshape(ranks, 1, width)
    sums = jnp.stack(sums)
    vectors = jnp.concatenate([jnp.broadcast_to(sums, (ranks,) + sums.shape), outer], 1)
    if place.paired:
        flipped = jnp.concatenate([vectors[..., columns:], vectors[..., :columns]], -1)
        vectors = jnp.where(shard == 0, vectors, flipped)
    vectors = jnp.pad(vectors, ((0, 0), (0, 16 - vectors.shape[1]), (0, 0))).astype(LOW)
    pieces = prog.out_weights(wout_grad, low_total, temporal, vectors, [out_grad, reduce_c.come_low])
    reduce_out = ReduceShared(place, pieces, piece + vectors.shape[1])
    reduce_out.cores(out_grads[1])
    wait = [layer_out, pieces[0]] + reduce_c.low_leg(out_grad) + reduce_c.top_leg(out_grad)
    qkv_grads, backs, sums_a = prog.temporal_back(qkv_a, out_grads, units_a, weights_a, wait)
    done = backs[0]
    backs = swapped(backs, "tensor")
    group_grads = prog.group_weights(
        qkv_grads, normed_a, mixed_a, out_grads, [sums_a], cost="group_weights_last"
    )
    back, *sent = prog.temporal_input(
        backs, start_t, along, moves.get("home_far"), reduce_out.rows(done) + [group_grads[0]]
    )
    reduce_c.both(back)
    total_in_b = hop_group(sum_columns(place, grads_b[0], grads_b[-1], back))
    total_in_a = sum_columns(place, group_grads[0], group_grads[-1])
    home.append((moves["homing"], [back] + [hop(rows, "shard", 1) for rows in sent]))
    input_grad = prog.natural(home, "natural_last")

    reduce_out.columns(total_in_a[4 * group + 16 :])
    sum_in = SumContext(place, jnp.concatenate([total_in_a, tie(total_in_b, back)]))
    sum_in.cores()
    reduce_c.hops()
    reduce_out.hops()
    total_c, total_out, total_in = reduce_c.finish(), reduce_out.finish(), sum_in.finish()
    total_in_a, total_in_b = total_in[: total_in_a.shape[0]], total_in[total_in_a.shape[0] :]
    sums_a = jnp.sum(total_out[:, -16:], 0)
    total_out = total_out[:, :-16]

    def in_grad(total):
        part = total[: 3 * group].reshape(3, group, columns)
        return jnp.transpose(part, (2, 0, 1))

    def bias_grad(line):
        part = HEAD_DIM // shards
        if place.paired:
            return pick(line.reshape(2, heads, shards, part), shard, 2)
        return line[: 2 * heads * part].reshape(2, heads, part)

    in_total = jnp.stack([in_grad(total_in_a), in_grad(total_in_b)])
    inner = jnp.stack([bias_grad(total_in_a[4 * group]), bias_grad(total_in_b[3 * group])])
    out_b = total_out[:, :piece].reshape(group, columns)
    out_total = jnp.stack([total_in_a[3 * group : 4 * group], out_b])
    fc_total = total_out[:, -(width // quarters) :].reshape(width, columns).T
    vectors = total_out[0, piece:]
    gains = jnp.concatenate([sums_a[:1], vectors[0:2]])
    shifts = jnp.concatenate([sums_a[1:2], vectors[2:4]])
    rows_shape = clip_input.shape
    return (
        layer_out.reshape(rows_shape),
        input_grad.reshape(rows_shape),
        gains,
        shifts,
        in_total,
        inner,
        out_total,
        vectors[4:8],
        fc_total,
        total_c[:, :unit].reshape(hidden, columns).T,
        vectors[8].reshape(hidden_bias.shape),
        total_c[:, unit:].reshape(hidden, columns),
    )


def solution(mesh):
    rows = P(None, "shard", "tensor", "context", None)
    weights = (
        P(None, "shard"),
        P(None, "shard"),
        P(None, "shard", None, "tensor"),
        P(None, None, "tensor", "shard"),
        P(None, "tensor", "shard"),
        P(None, "shard"),
        P("shard", None),
        P("shard", "tensor"),
        P("tensor", "shard"),
        P("tensor", "shard"),
    )
    return jax.shard_map(
        body,
        mesh=mesh,
        in_specs=(rows, P(None, "shard")) + weights + (rows,),
        out_specs=(rows, rows) + weights,
        check_vma=False,
    )
```

```python
import jax
import jax.numpy as jnp
import numpy as np
from jax import lax
from jax.experimental import pallas as pl
from jax.experimental.pallas import tpu as pltpu
from jax.sharding import PartitionSpec as P

HEAD_DIM = 64
WINDOW = 64
CHUNK = 32
EPS = 1e-06
SQRT_HALF = 0.7071067811865476
INV_ROOT_TAU = 0.3989422804014327
SCALE = HEAD_DIM**-0.5
HIDE = -1e30
LOW = jnp.bfloat16
F32 = jnp.float32
VMEM_BYTES = 60 * 2**20
PEAK = 1.15e9
SHARD, CONTEXT, TENSOR = "shard", "context", "tensor"


class Cost:
    group_weights_last = 0.2
    natural_first = 40
    frames_start = 40
    frames_grad = 40
    natural_last = 60
    send_rows = 6
    temporal_start = 10
    temporal = 30
    temporal_out = 6
    spatial_in = 8
    spatial = 20
    spatial_out = 8
    feed_forward = 26
    feed_forward_back = 10
    spatial_back = 28
    spatial_input = 20
    temporal_grad = 20
    temporal_back = 70
    temporal_input = 70
    group_weights = 0.2
    natural = 0.2
    out_weights = 0.2
    frames_of = 0.2


class Move:
    beginning, starting, returning, arriving, homing, ending = range(6)
    begin_far, return_far, arrive_far, home_far, end_far = range(6, 11)


def hop(values, axis, step):
    count = lax.axis_size(axis)
    return lax.ppermute(values, axis, [(i, i ^ step) for i in range(count)])


def hop_group(values):
    quarters, ranks = lax.axis_size(CONTEXT), lax.axis_size(TENSOR)
    pairs = [
        (c * ranks + i, c * ranks + (i ^ group_of(c))) for c in range(quarters) for i in range(ranks)
    ]
    return lax.ppermute(values, (CONTEXT, TENSOR), pairs)


def group_of(context):
    return 2 * (context % 2) + context // 2


def pick(values, index, axis=0):
    return lax.dynamic_index_in_dim(values, index, axis, keepdims=False)


def ordered(parts, me, axis=0):
    shape = list(parts[0].shape)
    shape.insert(axis, len(parts))
    out = jnp.zeros(shape, parts[0].dtype)
    for j, part in enumerate(parts):
        out = lax.dynamic_update_index_in_dim(out, part, me ^ j, axis)
    return out


def round_up(value, step):
    return -(-value // step) * step


class Place:
    def __init__(self):
        self.shard = lax.axis_index(SHARD)
        self.context = lax.axis_index(CONTEXT)
        self.tensor = lax.axis_index(TENSOR)
        self.shards = lax.axis_size(SHARD)
        self.ranks = lax.axis_size(TENSOR)
        self.quarters = lax.axis_size(CONTEXT)
        self.paired = self.shards == 2


def tie(values, *others):
    return lax.optimization_barrier((values,) + others)[0] if others else values


def add(*terms):
    total = terms[0].astype(F32)
    for term in terms[1:]:
        total = total + term.astype(F32)
    return total.astype(LOW)


class Gather:
    def __init__(self, place, mine):
        self.place = place
        self.parts = [mine] + [hop(mine, TENSOR, k) for k in range(1, place.ranks)]

    def columns(self, *later):
        blocks = jnp.stack([tie(part, *later) for part in self.parts])
        if self.place.paired:
            self.parts = [blocks, hop(blocks, SHARD, 1)]
        else:
            self.parts = [lax.all_gather(blocks, SHARD, axis=2, tiled=True)]
        self.far = [hop(blocks, CONTEXT, 2)] if self.place.paired else []

    def rows(self, *later):
        self.far.append(hop(tie(self.parts[-1], *later), CONTEXT, 2))

    def cores(self, *later):
        join = lambda parts: jnp.concatenate([tie(part, *later) for part in parts], -1)
        self.first, second = join(self.parts), join(self.far)
        return [self.first, hop(self.first, CONTEXT, 1), second, hop(second, CONTEXT, 1)]


class ReduceHidden:
    def __init__(self, place, pieces):
        self.place = place
        self.kept = [pieces[0], pieces[2]]
        self.come = [hop(pieces[1], CONTEXT, 1), hop(pieces[3], CONTEXT, 1)]
        self.middle = pieces[0].shape[1] // 2
        self.half = pieces[0].shape[2] // (2 if place.paired else 1)

    def part(self, index, rows, columns):
        return add(self.kept[index][:, rows, columns], self.come[index][:, rows, columns])

    def cores(self, *later):
        self.come = [tie(item, *later) for item in self.come]
        top, low = slice(self.middle), slice(self.middle, None)
        left, right = slice(self.half), slice(self.half, None)
        out = []
        if self.place.paired:
            sent = jnp.stack([self.part(index, top, right) for index in range(2)])
            out.append(sent)
            self.come_top = hop(sent, SHARD, 1)
        self.sent_low = self.part(1, low, slice(None))
        self.kept_top = lambda: jnp.stack([self.part(index, top, left) for index in range(2)])
        self.kept_low = lambda at: self.part(0, low, at)
        return out + [self.sent_low]

    def start_low(self, *later):
        self.come_low = hop(tie(self.sent_low, *later), CONTEXT, 2)

    def scatter(self, total):
        axis = total.ndim - 1
        return lax.psum_scatter(total, SHARD, scatter_dimension=axis, tiled=True)

    def top_leg(self, *later):
        top = self.kept_top()
        top = add(top, tie(self.come_top, *later)) if self.place.paired else self.scatter(top)
        self.top, self.come_top = top[0], hop(top[1], CONTEXT, 2)
        return [top]

    def low_leg(self, *later):
        come = tie(self.come_low, *later)
        left, right = slice(self.half), slice(self.half, None)
        low = add(self.kept_low(left), come[..., left])
        if self.place.paired:
            sent = add(self.kept_low(right), come[..., right])
            self.come_low = hop(sent, SHARD, 1)
        else:
            low, sent, self.come_low = self.scatter(low), low, None
        self.low = low
        return [low, sent]

    def both(self, *later):
        top = add(self.top, tie(self.come_top, *later))
        low = self.low if self.come_low is None else add(self.low, tie(self.come_low, *later))
        mine = jnp.concatenate([top, low], 1)
        self.kept = mine[0]
        self.come = [hop(mine[k], TENSOR, k) for k in range(1, self.place.ranks)]
        return [mine]

    def hops(self, *later):
        self.sum = add(self.kept, *[tie(come, *later) for come in self.come])
        return [self.sum]

    def finish(self):
        return gather_context(self.place, self.sum)


def gather_context(place, mine):
    second = hop(mine, CONTEXT, 2)
    both = jnp.stack([mine, second])
    far = hop(both, CONTEXT, 1)
    return ordered([both[0], far[0], both[1], far[1]], place.context).astype(F32)


class ReduceShared:
    def __init__(self, place, pieces, each):
        self.place, self.each = place, each
        self.kept = [pieces[0], pieces[2]]
        self.come = [hop(pieces[1], CONTEXT, 1), hop(pieces[3], CONTEXT, 1)]

    def cores(self, *later):
        first, second = [add(a, tie(b, *later)) for a, b in zip(self.kept, self.come)]
        self.kept, self.come = first, hop(second, CONTEXT, 2)
        return [first, second]

    def rows(self, *later):
        come = tie(self.come, *later)
        if self.place.paired:
            half = come.shape[-1] // 2
            sent = add(self.kept[:, half:], come[:, half:])
            self.kept, self.come = add(self.kept[:, :half], come[:, :half]), hop(sent, SHARD, 1)
            return [sent]
        self.kept = lax.psum_scatter(
            add(self.kept, come), SHARD, scatter_dimension=1, tiled=True
        )
        self.come = None
        return [self.kept]

    def columns(self, more):
        mine = self.kept if self.come is None else add(self.kept, self.come)
        ranks, each = self.place.ranks, self.each
        common = jnp.concatenate([mine[ranks * each :], more])
        block = lambda k: jnp.concatenate([mine[k * each : (k + 1) * each], common])
        self.kept = block(0)
        self.come = [hop(block(k), TENSOR, k) for k in range(1, ranks)]
        return [mine]

    def hops(self, *later):
        self.sum = add(self.kept, *[tie(come, *later) for come in self.come])
        return [self.sum]

    def finish(self):
        return gather_context(self.place, self.sum)


def sum_columns(place, kept, sent, *later):
    if place.paired:
        return add(kept, tie(hop(sent, SHARD, 1), *later))
    return lax.psum_scatter(kept, SHARD, scatter_dimension=1, tiled=True)


class SumContext:
    def __init__(self, place, total):
        self.core, self.shape = place.context % 2, total.shape
        halves = total.reshape(2, -1, total.shape[-1])
        self.kept, self.come = pick(halves, self.core), hop(pick(halves, 1 - self.core), CONTEXT, 1)

    def cores(self, *later):
        self.kept = add(self.kept, tie(self.come, *later))
        self.come = hop(self.kept, CONTEXT, 2)
        return [self.kept]

    def finish(self):
        half = add(self.kept, self.come)
        whole = ordered([half, hop(half, CONTEXT, 1)], self.core)
        return whole.reshape(self.shape).astype(F32)


class Layout:
    def __init__(self, place, clips):
        self.place = place
        self.batches, self.frames, self.places = clips.shape[:3]
        self.whole = 1 if place.paired else self.batches
        self.split = self.batches - self.whole
        self.first = self.whole * self.places
        self.later = -(-self.split * self.places // 2)
        self.slots = round_up(self.first + self.later, CHUNK)
        self.temporal_rows = self.frames * self.slots
        self.units = self.whole * self.frames + self.split
        self.frame_rows = round_up(self.units * self.places, 16)
        self.natural_blocks = self.batches * self.frames
        self.own = self.whole * self.frames * self.places // 16 * 16

    def label(self, batch, frame, spot):
        return (batch * self.frames * self.place.ranks + frame) * self.places + spot

    def split_labels(self, part, frames):
        flat = self.later * part + np.arange(self.later)[None]
        labels = self.label(
            self.whole + flat // self.places, np.asarray(frames)[:, None], flat % self.places
        )
        return np.where(flat < self.split * self.places, labels, -1)

    def frames_at(self, tensor):
        return self.frames * tensor + np.arange(self.frames)

    def temporal_labels(self, shard, tensor):
        frames = self.frames_at(tensor)
        slot = np.arange(self.first)[None]
        parts = [self.label(slot // self.places, frames[:, None], slot % self.places)]
        if self.split:
            parts.append(self.split_labels(shard, frames))
        labels = np.concatenate(parts, 1)
        spare = self.slots - labels.shape[1]
        return np.pad(labels, ((0, 0), (0, spare)), constant_values=-1)

    def frame_labels(self, shard, tensor, far=False):
        row = np.arange(self.frame_rows)
        unit, spot = row // self.places, row % self.places
        batch, frame = unit // self.frames, self.frames * tensor + unit % self.frames
        later = unit - self.whole * self.frames
        batch = np.where(later >= 0, self.whole + later, batch)
        frame = np.where(later >= 0, self.frames * tensor + shard, frame)
        inside = (unit < self.units) & ((later >= 0) | (not far))
        return np.where(inside, self.label(batch, frame, spot), -1)

    def natural_labels(self, tensor):
        batch = np.arange(self.batches)[:, None, None]
        frame = self.frames_at(tensor)[None, :, None]
        spot = np.arange(WINDOW)[None, None]
        return np.where(spot < self.places, self.label(batch, frame, spot), -1)

    def other_labels(self, shard, tensor):
        batch = np.arange(self.whole, self.batches)[:, None]
        spot = np.arange(WINDOW)[None]
        labels = self.label(batch, self.frames * tensor + shard, spot)
        return np.where(spot < self.places, labels, -1)

    def moves(self, shard, tensor):
        natural, frame = self.natural_labels(tensor), self.frame_labels(shard, tensor)
        temporal = self.temporal_labels(shard, tensor)
        moves = {
            Move.beginning: ([temporal], [natural]),
            Move.starting: ([frame], [natural]),
            Move.returning: ([frame], [temporal]),
            Move.arriving: ([temporal], [frame]),
            Move.homing: ([natural], [temporal]),
            Move.ending: ([natural], [frame]),
        }
        if self.split:
            frames, other = self.frames_at(tensor), 1 - shard

            def packed(part, frames):
                labels = self.split_labels(part, frames).reshape(-1)
                spare = round_up(labels.size, 16) - labels.size
                return np.pad(labels, (0, spare), constant_values=-1)

            mine, theirs = packed(shard, frames), packed(other, frames)
            moves[Move.beginning][1].append(mine)
            moves[Move.starting][1].append(self.other_labels(shard, tensor))
            moves[Move.returning][1].append(packed(other, [frames[shard]]))
            moves[Move.arriving][1].append(packed(shard, [frames[other]]))
            moves[Move.homing][1].append(theirs)
            moves[Move.begin_far] = ([theirs], [natural])
            moves[Move.return_far] = ([packed(shard, [frames[other]])], [temporal])
            moves[Move.arrive_far] = ([packed(other, [frames[shard]])], [frame])
            moves[Move.home_far] = ([mine], [temporal])
            moves[Move.end_far] = ([natural], [self.frame_labels(other, tensor, True)[self.own :]])
        flat = lambda parts: np.concatenate([np.asarray(part).reshape(-1) for part in parts])
        return {key: (flat(targets), flat(sources)) for key, (targets, sources) in moves.items()}

    def matrices(self):
        ranks = self.place.ranks
        shards = 2 if self.split else 1
        table = [self.moves(i // ranks, i % ranks) for i in range(shards * ranks)]
        line = lambda moves: np.concatenate([part for pair in moves.values() for part in pair])
        lines = jnp.asarray(np.stack([line(moves) for moves in table]).astype(np.int32))
        index = self.place.tensor + (ranks * self.place.shard if self.split else 0)
        labels, at, out = pick(lines, index), 0, {}
        for key, (targets, sources) in table[0].items():
            ends = at + targets.size, at + targets.size + sources.size
            target, source = labels[at : ends[0]], labels[ends[0] : ends[1]]
            same = (target[:, None] == source[None]) & (target[:, None] >= 0)
            out[key], at = same.astype(LOW), ends[1]
        return out


def call(body, outs, ins, scalars, cost=1, scratch=(), after=(), name=None, specs=None):
    given, count = body, len(ins)
    if after:
        body = lambda scalars, *refs: given(scalars, *refs[:count], *refs[count + len(after) :])
    moved = sum(item.size * item.dtype.itemsize for item in list(outs) + list(ins))
    spec = pl.BlockSpec(memory_space=pltpu.VMEM)
    return pl.pallas_call(
        body,
        name=name,
        out_shape=tuple(outs),
        in_specs=[pl.BlockSpec(memory_space=pltpu.SMEM)]
        + list(specs or [spec] * len(ins))
        + [pl.BlockSpec(memory_space=pl.ANY)] * len(after),
        out_specs=(spec,) * len(outs),
        scratch_shapes=list(scratch),
        grid=(1,) if specs else (),
        compiler_params=pltpu.CompilerParams(vmem_limit_bytes=VMEM_BYTES),
        cost_estimate=pl.CostEstimate(
            flops=int(PEAK * cost), bytes_accessed=moved if cost >= 1 else 0, transcendentals=0
        ),
    )(scalars, *ins, *after)


def shape(*dims, dtype=LOW):
    return jax.ShapeDtypeStruct(dims, dtype)


def nn(first, second):
    return lax.dot_general(first, second, (((1,), (0,)), ((), ())), preferred_element_type=F32)


def nt(first, second):
    return lax.dot_general(first, second, (((1,), (1,)), ((), ())), preferred_element_type=F32)


def tn(first, second):
    return lax.dot_general(first, second, (((0,), (0,)), ((), ())), preferred_element_type=F32)


def swapper(scalars, paired):
    def swap(values):
        if not paired:
            return values
        half = values.shape[-1] // 2
        other = jnp.concatenate([values[:, half:], values[:, :half]], -1)
        return jnp.where(scalars[0] == 0, values, other)

    return swap


def unit_of(values):
    centred = values - jnp.mean(values, -1, keepdims=True)
    inverse = lax.rsqrt(jnp.mean(centred * centred, -1, keepdims=True) + EPS)
    return (centred * inverse, inverse)


def norm_back(grad, unit, inverse, gain):
    scaled = grad * gain
    inner = (
        scaled
        - jnp.mean(scaled, -1, keepdims=True)
        - unit * jnp.mean(scaled * unit, -1, keepdims=True)
    )
    return (
        inverse * inner,
        jnp.sum(grad * unit, 0, keepdims=True),
        jnp.sum(grad, 0, keepdims=True),
    )


def attention(query, key, value, hide):
    probs = softmax(nt(key, query) + hide)
    return tn(probs.astype(LOW), value)


def softmax(scores):
    weights = jnp.exp(scores - jnp.max(scores, 0, keepdims=True))
    return weights * (1.0 / jnp.sum(weights, 0, keepdims=True))


def attention_back(query, key, value, grad, hide):
    probs = softmax(nt(key, query) + hide)
    prob_grad = nt(value, grad)
    inner = jnp.sum(probs * prob_grad, 0, keepdims=True)
    scored = (probs * (prob_grad - inner)).astype(LOW)
    return (tn(scored, key) * SCALE, nn(scored, query), nn(probs.astype(LOW), grad))


def column_sum(values):
    return jnp.sum(values.astype(F32), 0, keepdims=True)


def rows_at(start, size):
    return pl.ds(pl.multiple_of(start, 16), size)


class Program:
    def __init__(self, place, layout, width, group, scalars):
        self.place, self.layout, self.width, self.group = place, layout, width, group
        self.scalars = scalars
        self.ranks, self.quarters = place.ranks, place.quarters
        self.piece = group // self.quarters
        self.heads = group // HEAD_DIM
        self.all_heads = group * self.ranks
        spot = np.arange(self.ranks * layout.frames * CHUNK) % CHUNK
        self.same_place = jnp.asarray(
            np.where(spot[:, None] == spot[None], 0, HIDE).astype(np.float32)
        )

    def call(self, body, outs, ins, flops=0, scratch=(), after=(), specs=None, cost=None):
        name = body.__qualname__.split(".")[1]
        cost = cost or getattr(Cost, name)
        return call(body, outs, ins, self.scalars, cost, scratch, after, name, specs)

    def lanes(self, c, h):
        at = c * self.group + h * HEAD_DIM
        return slice(at, at + HEAD_DIM)


    def live(self, scalars, batch):
        return scalars[3 + batch] > 0

    def place_natural(self, scalars, rows, source):
        lay = self.layout
        rows[...] = jnp.zeros_like(rows)
        for item in range(lay.natural_blocks):

            @pl.when(self.live(scalars, item // lay.frames))
            def _(item=item):
                rows[item * WINDOW : item * WINDOW + lay.places] = source[item]

    def send_rows(self, clips, cotangents, matrix, wait=()):
        lay, width = self.layout, self.width
        count, split = lay.natural_blocks, lay.split
        first = lay.whole * lay.frames

        def body(scalars, clips_ref, grads_ref, matrix_ref, sent, frames, rows):
            self.place_natural(scalars, rows, clips_ref)
            sent[...] = nn(matrix_ref[...], rows[...]).astype(LOW)
            for index, source in enumerate((clips_ref, grads_ref)):
                for item in range(split):
                    frame = first + lay.frames * item + 1 - scalars[0]
                    frames[index, item] = source[frame]

        outs = [shape(matrix.shape[0], width), shape(2, split, lay.places, width)]
        scratch = [pltpu.VMEM((count * WINDOW, width), LOW)]
        return self.call(body, outs, [clips, cotangents, matrix], scratch=scratch, after=wait)

    def temporal_start(self, clips, come, matrix):
        lay, width = self.layout, self.width
        count, rows_in = lay.natural_blocks, lay.natural_blocks * WINDOW
        more = 0 if come is None else come.shape[0]

        def body(scalars, clips_ref, *refs):
            matrix_ref, start_ref, normed_ref, rows = refs[-4:]
            self.place_natural(scalars, rows, clips_ref)
            if more:
                rows[rows_in:] = refs[0][...]
            start = nn(matrix_ref[...], rows[...])
            start_ref[...] = start.astype(LOW)
            unit, _ = unit_of(start)
            swap = swapper(scalars, self.place.paired)
            normed_ref[...] = swap(unit).astype(LOW)

        outs = [shape(lay.temporal_rows, width)] * 2
        ins = [clips] + ([come] if more else []) + [matrix]
        scratch = [pltpu.VMEM((rows_in + more, width), LOW)]
        return self.call(body, outs, ins, scratch=scratch)

    def frames_of(self, clips, others, index, matrix, cost, wait=()):
        lay, width = self.layout, self.width
        count, split = lay.natural_blocks, lay.split

        def body(scalars, clips_ref, *refs):
            matrix_ref, out_ref, rows = refs[-3:]
            self.place_natural(scalars, rows, clips_ref)
            for item in range(split):

                @pl.when(jnp.logical_not(self.live(scalars, lay.whole + item)))
                def _(item=item):
                    start = (count + item) * WINDOW
                    rows[start : start + lay.places] = refs[0][index, item]

            out_ref[...] = nn(matrix_ref[...], rows[...]).astype(LOW)

        return self.call(
            body,
            [shape(lay.frame_rows, width)],
            [clips] + ([others] if split else []) + [matrix],
            scratch=[pltpu.VMEM(((count + split) * WINDOW, width), LOW)],
            after=wait,
            cost=cost,
        )[0]


    def chunk(self, refs, n):
        lay = self.layout
        return jnp.concatenate(
            [
                ref[rows_at(frame * lay.slots + n * CHUNK, CHUNK)]
                for ref in refs
                for frame in range(lay.frames)
            ]
        )

    def put_chunk(self, refs, n, values):
        lay = self.layout
        for k, ref in enumerate(refs):
            for frame in range(lay.frames):
                at = (k * lay.frames + frame) * CHUNK
                ref[rows_at(frame * lay.slots + n * CHUNK, CHUNK)] = values[at : at + CHUNK]

    def temporal(self, units, weights, along, shift, wait=()):
        lay, width, group, ranks = self.layout, self.width, self.group, self.ranks
        rows = lay.temporal_rows

        def body(scalars, *refs):
            unit_refs, weight_refs = refs[:ranks], refs[ranks : ranks + len(weights)]
            refs = refs[ranks + len(weights) :]
            along_ref, shift_ref, same, refs = refs[0], refs[1], refs[2], refs[3:]
            qkv_refs, mixed_refs, normed_refs, out_refs = (
                refs[at : at + ranks] for at in range(0, 4 * ranks, ranks)
            )
            swap = swapper(scalars, self.place.paired)
            gain, move = swap(along_ref[0:1]), swap(along_ref[3:4])
            weight = jnp.concatenate([ref[: 3 * group] for ref in weight_refs], -1)
            for k in range(ranks):
                normed_refs[k][...] = (unit_refs[k][...].astype(F32) * gain + move).astype(LOW)
                qkv_refs[k][...] = (nt(normed_refs[k][...], weight) + shift_ref[...]).astype(LOW)

            @pl.loop(0, lay.slots // CHUNK, unroll=True)
            def _(n):
                values = self.chunk(qkv_refs, n)
                parts = []
                for h in range(self.heads):
                    query, key, value = (values[:, self.lanes(c, h)] for c in range(3))
                    parts.append(attention(query * LOW(SCALE), key, value, same[...]))
                self.put_chunk(mixed_refs, n, jnp.concatenate(parts, -1).astype(LOW))

            weight = jnp.concatenate([ref[3 * group : 4 * group] for ref in weight_refs], -1)
            for k in range(ranks):
                out_refs[k][...] = nn(mixed_refs[k][...], weight).astype(LOW)

        outs = [shape(rows, 3 * group)] * ranks + [shape(rows, group)] * ranks
        outs += [shape(rows, width)] * (2 * ranks)
        ins = list(units) + list(weights) + [along, shift, self.same_place]
        flops = 8 * ranks * rows * width * group
        flops += 4 * ranks * rows * self.same_place.shape[0] * group
        outs = self.call(body, outs, ins, flops, after=wait)
        return [outs[at : at + ranks] for at in range(0, 4 * ranks, ranks)]

    def temporal_out(self, parts, along, matrix, wait=()):
        lay, width = self.layout, self.width
        far = [] if matrix is None else [matrix]

        def body(scalars, *refs):
            part_refs, along_ref, refs = refs[: self.ranks], refs[self.ranks], refs[self.ranks + 1 :]
            swap = swapper(scalars, self.place.paired)
            total = swap(sum(ref[...].astype(F32) for ref in part_refs)) + along_ref[6:7]
            out_ref = refs[len(far)]
            out_ref[...] = total.astype(LOW)
            if far:
                refs[2][...] = nn(refs[0][...], out_ref[...]).astype(LOW)

        outs = [shape(lay.temporal_rows, width)] + [shape(item.shape[0], width) for item in far]
        return self.call(body, outs, list(parts) + [along] + far, after=wait)

    def temporal_grad(self, parts, matrix, wait=()):
        lay, width = self.layout, self.width

        def body(scalars, *refs):
            matrix_ref, out_ref = refs[len(parts) :]
            swap = swapper(scalars, self.place.paired)
            source = jnp.concatenate([ref[...] for ref in refs[: len(parts)]])
            out_ref[...] = swap(nn(matrix_ref[...], source)).astype(LOW)

        outs = [shape(lay.temporal_rows, width)]
        return self.call(body, outs, list(parts) + [matrix], after=wait)[0]

    def temporal_back(self, qkv, grads, units, weights, wait=()):
        lay, width, group, ranks = self.layout, self.width, self.group, self.ranks
        rows = lay.temporal_rows

        def body(scalars, *refs):
            qkv_refs, grad_refs, unit_refs = (
                refs[at : at + ranks] for at in range(0, 3 * ranks, ranks)
            )
            refs = refs[3 * ranks :]
            weight_refs, same, refs = refs[: len(weights)], refs[len(weights)], refs[len(weights) + 1 :]
            out_refs, back_refs, sums = refs[:ranks], refs[ranks : 2 * ranks], refs[2 * ranks]
            mixed = refs[2 * ranks + 1 :]
            weight = jnp.concatenate([ref[3 * group : 4 * group] for ref in weight_refs], -1)
            for k in range(ranks):
                mixed[k][...] = nt(grad_refs[k][...], weight).astype(LOW)

            @pl.loop(0, lay.slots // CHUNK, unroll=True)
            def _(n):
                values, grads = self.chunk(qkv_refs, n), self.chunk(mixed, n)
                parts = [[], [], []]
                for h in range(self.heads):
                    query, key, value = (values[:, self.lanes(c, h)] for c in range(3))
                    grad = grads[:, self.lanes(0, h)]
                    got = attention_back(query * LOW(SCALE), key, value, grad, same[...])
                    for part, item in zip(parts, got):
                        part.append(item)
                total = jnp.concatenate(parts[0] + parts[1] + parts[2], -1)
                self.put_chunk(out_refs, n, total.astype(LOW))

            weight = jnp.concatenate([ref[: 3 * group] for ref in weight_refs], -1)
            sums[...] = jnp.zeros_like(sums)
            for k in range(ranks):
                back = nn(out_refs[k][...], weight)
                back_refs[k][...] = back.astype(LOW)
                sums[0:1] += column_sum(back * unit_refs[k][...].astype(F32))
                sums[1:2] += column_sum(back)

        outs = [shape(rows, 3 * group)] * ranks + [shape(rows, width)] * ranks
        outs += [shape(8, width, dtype=F32)]
        ins = list(qkv) + list(grads) + list(units) + list(weights) + [self.same_place]
        flops = 8 * ranks * rows * width * group
        flops += 10 * ranks * rows * self.same_place.shape[0] * group
        scratch = [pltpu.VMEM((rows, group), LOW)] * ranks
        outs = self.call(body, outs, ins, flops, scratch, wait)
        return outs[:ranks], outs[ranks : 2 * ranks], outs[-1]

    def group_weights(self, qkv_grads, normed, mixed=(), out_grads=(), more=(), wait=(), cost=None):
        width, group, count = self.width, self.group, len(qkv_grads)
        parts = 2 if self.place.paired else 1
        size = 3 * group + (group if mixed else 0)

        def body(scalars, *refs):
            refs = list(refs)
            take = lambda n: [refs.pop(0) for _ in range(n)]
            grad_refs, normed_refs = take(count), take(count)
            mixed_refs, out_grad_refs = take(len(mixed)), take(len(mixed))
            more_refs, (spread,), out_refs = take(len(more)), take(1), refs
            columns = width // parts

            def put(start, total):
                for part in range(parts):
                    values = total[:, part * columns : (part + 1) * columns]
                    out_refs[part][start : start + total.shape[0]] = values.astype(LOW)

            total = jnp.zeros((3 * group, width), F32)
            sums = jnp.zeros((1, 3 * group), F32)
            for j in range(count):
                total = total + tn(grad_refs[j][...], normed_refs[j][...])
                sums = sums + column_sum(grad_refs[j][...])
            put(0, total)
            if mixed:
                total = jnp.zeros((group, width), F32)
                for j in range(count):
                    total = total + tn(mixed_refs[j][...], out_grad_refs[j][...])
                put(3 * group, total)
            line = jnp.concatenate([sums[:, :group], sums[:, 2 * group :]], -1)
            top = lax.broadcasted_iota(jnp.int32, (16, 2 * group), 0) == 0
            line = jnp.where(top, line, 0.0).astype(LOW)
            for part in range(parts):
                out_refs[part][size : size + 16] = line if parts == 2 else nn(line, spread[...]).astype(LOW)
                for ref in more_refs:
                    rows = ref[:, part * columns : (part + 1) * columns]
                    rows = jnp.concatenate([rows, jnp.zeros_like(rows)])
                    out_refs[part][size + 16 :] = rows.astype(LOW)
                if not more:
                    out_refs[part][size + 16 :] = jnp.zeros((16, columns), LOW)

        outs = [shape(size + 32, width // parts)] * parts
        rows = qkv_grads[0].shape[0]
        ins = list(qkv_grads) + list(normed) + list(mixed) + list(out_grads) + list(more)
        ins += [self.spread()]
        flops = 2 * count * rows * width * size
        return self.call(body, outs, ins, flops, after=wait, cost=cost)

    def spread(self):
        shards = self.place.shards
        columns, part = self.width // shards, HEAD_DIM // shards
        out = np.zeros((2 * self.group, self.width), np.float32)
        for item in range(2 * self.group):
            head, feature = divmod(item, HEAD_DIM)
            out[item, feature // part * columns + head * part + feature % part] = 1
        return jnp.asarray(out, LOW)

    def temporal_input(self, backs, start, along, matrix, wait=()):
        lay, width = self.layout, self.width
        far = [] if matrix is None else [matrix]

        def body(scalars, *refs):
            back_refs, refs = refs[: self.ranks], refs[self.ranks :]
            start_ref, along_ref, refs = refs[0], refs[1], refs[2:]
            out_ref = refs[len(far)]
            swap = swapper(scalars, self.place.paired)
            unit, inverse = unit_of(start_ref[...].astype(F32))
            grad = swap(sum(ref[...].astype(F32) for ref in back_refs))
            back, _, _ = norm_back(grad, unit, inverse, along_ref[0:1])
            out_ref[...] = back.astype(LOW)
            if far:
                refs[2][...] = nn(refs[0][...], out_ref[...]).astype(LOW)

        outs = [shape(lay.temporal_rows, width)] + [shape(item.shape[0], width) for item in far]
        return self.call(body, outs, list(backs) + [start, along] + far, after=wait)


    def spatial_in(self, sources, matrix, start, fc, along, wait=()):
        lay, width = self.layout, self.width
        rows = lay.frame_rows

        def body(scalars, *refs):
            source_refs, refs = refs[: len(sources)], refs[len(sources) :]
            matrix_ref, start_ref, fc_refs, refs = refs[0], refs[1], refs[2 : 2 + len(fc)], refs[2 + len(fc) :]
            along_ref, after_ref, temporal_ref, normed_ref = refs
            swap = swapper(scalars, self.place.paired)
            source = jnp.concatenate([ref[...] for ref in source_refs])
            temporal = nn(matrix_ref[...], source)
            temporal_ref[...] = temporal.astype(LOW)
            weight = jnp.concatenate([ref[...] for ref in fc_refs])
            after = start_ref[...].astype(F32) + nn(swap(temporal).astype(LOW), weight)
            after = after + along_ref[7:8]
            after_ref[...] = after
            unit, _ = unit_of(after)
            normed_ref[...] = swap(unit * along_ref[1:2] + along_ref[4:5]).astype(LOW)

        outs = [shape(rows, width, dtype=F32), shape(rows, width), shape(rows, width)]
        ins = list(sources) + [matrix, start] + list(fc) + [along]
        return self.call(body, outs, ins, 2 * rows * width * width, after=wait)

    def windows(self, refs, n):
        at = rows_at(n * (WINDOW - 16), WINDOW)
        return jnp.concatenate([ref[at] for ref in refs])

    def window_mask(self, n, axis):
        size = self.quarters * WINDOW
        dims = (size, 1) if axis == 0 else (1, size)
        index = lax.broadcasted_iota(jnp.int32, dims, axis) & (WINDOW - 1)
        start = n * (self.layout.places - WINDOW + 16)
        return (index >= start) & (index < start + self.layout.places)

    def put_windows(self, refs, n, values, mask):
        for j, ref in enumerate(refs):
            at = rows_at(n * (WINDOW - 16), WINDOW)
            part = slice(j * WINDOW, (j + 1) * WINDOW)
            old = ref[at].astype(F32)
            ref[at] = jnp.where(mask[part], values[part], old).astype(LOW)

    def spatial(self, normed, win, shift, wait=()):
        lay, width, quarters, group = self.layout, self.width, self.quarters, self.group

        def body(scalars, *refs):
            normed_refs, refs = refs[:quarters], refs[quarters:]
            win_refs, shift_ref, refs = refs[: len(win)], refs[len(win)], refs[len(win) + 1 :]
            qkv_refs, out_refs = refs[:quarters], refs[quarters:]
            weight = jnp.concatenate([ref[: 3 * group] for ref in win_refs], -1)
            for j in range(quarters):
                qkv_refs[j][...] = (nt(normed_refs[j][...], weight) + shift_ref[...]).astype(LOW)
                out_refs[j][...] = jnp.zeros_like(out_refs[j])

            @pl.loop(0, lay.units, unroll=True)
            def _(n):
                rows = self.windows(qkv_refs, n)
                hide = jnp.where(self.window_mask(n, 0), 0.0, HIDE)
                parts = []
                for h in range(self.heads):
                    query, key, value = (rows[:, self.lanes(c, h)] for c in range(3))
                    parts.append(attention(query * LOW(SCALE), key, value, hide))
                mask = self.window_mask(n, 0)
                self.put_windows(out_refs, n, jnp.concatenate(parts, -1), mask)

        outs = [shape(lay.frame_rows, 3 * group)] * quarters
        outs += [shape(lay.frame_rows, group)] * quarters
        size = quarters * WINDOW
        flops = 6 * quarters * lay.frame_rows * width * group + 4 * lay.units * size * size * group
        outs = self.call(body, outs, list(normed) + list(win) + [shift], flops, after=wait)
        return outs[:quarters], outs[quarters:]

    def spatial_back(self, qkv, grads, win, wait=()):
        lay, width, quarters, group = self.layout, self.width, self.quarters, self.group

        def body(scalars, *refs):
            qkv_refs, grad_refs = refs[:quarters], refs[quarters : 2 * quarters]
            win_refs = refs[2 * quarters : 2 * quarters + len(win)]
            refs = refs[2 * quarters + len(win) :]
            out_refs, back_refs = refs[:quarters], refs[quarters:]
            for ref in out_refs:
                ref[...] = jnp.zeros_like(ref)

            @pl.loop(0, lay.units, unroll=True)
            def _(n):
                rows = self.windows(qkv_refs, n)
                mask = self.window_mask(n, 0)
                grads = self.windows(grad_refs, n) * mask.astype(F32).astype(LOW)
                hide = jnp.where(self.window_mask(n, 0), 0.0, HIDE)
                parts = [[], [], []]
                for h in range(self.heads):
                    query, key, value = (rows[:, self.lanes(c, h)] for c in range(3))
                    grad = grads[:, self.lanes(0, h)]
                    got = attention_back(query * LOW(SCALE), key, value, grad, hide)
                    for part, item in zip(parts, got):
                        part.append(item)
                values = jnp.concatenate(parts[0] + parts[1] + parts[2], -1)
                self.put_windows(out_refs, n, values, mask)

            weight = jnp.concatenate([ref[: 3 * group] for ref in win_refs], -1)
            for j in range(quarters):
                back_refs[j][...] = nn(out_refs[j][...], weight).astype(LOW)

        outs = [shape(lay.frame_rows, 3 * group)] * quarters
        outs += [shape(lay.frame_rows, width)] * quarters
        size = quarters * WINDOW
        flops = 10 * lay.units * size * size * group
        flops += 6 * quarters * lay.frame_rows * width * group
        outs = self.call(body, outs, list(qkv) + list(grads) + list(win), flops, after=wait)
        return outs[:quarters], outs[quarters:]

    def put_groups(self, scalars, out, pieces, first):
        for i in range(self.quarters):
            spot = (scalars[1] ^ i) * self.piece
            for j in range(self.quarters):
                k = group_of(scalars[1]) ^ group_of(j)
                out[rows_at(j * self.group + spot, self.piece)] = pieces[i][
                    k, first : first + self.piece
                ]

    def spatial_out(self, mixed, pieces, first, after, grad, along, wait=()):
        lay, width, group = self.layout, self.width, self.group
        rows, quarters = lay.frame_rows, self.quarters
        size = WINDOW

        def body(scalars, *refs):
            mixed_refs, piece_refs, refs = refs[:quarters], refs[quarters : 2 * quarters], refs[2 * quarters :]
            after_ref, grad_ref, along_ref, out_ref, normed_ref, low_ref, wout = refs
            swap = swapper(scalars, self.place.paired)
            self.put_groups(scalars, wout, piece_refs, 0)
            total = jnp.zeros((rows, width), F32)
            for j in range(quarters):
                total = total + nn(mixed_refs[j][...], wout[j * group : (j + 1) * group])
            after = after_ref[...] + swap(total) + along_ref[8:9]
            out_ref[...] = after
            unit, _ = unit_of(after)
            normed_ref[...] = swap(unit * along_ref[2:3] + along_ref[5:6]).astype(LOW)
            low_ref[...] = swap(grad_ref[...].astype(F32)).astype(LOW)

        outs = [
            shape(rows, width, dtype=F32),
            shape(rows, width),
            shape(rows, width),
            shape(self.all_heads, width),
        ]
        ins = list(mixed) + list(pieces) + [after, grad, along]
        whole = pl.BlockSpec(memory_space=pltpu.VMEM)
        part = pl.BlockSpec((self.ranks, size, width), lambda *_: (0, first // size, 0))
        specs = [whole] * quarters + [part] * quarters + [whole] * 3
        flops = 2 * rows * width * self.all_heads
        return self.call(body, outs, ins, flops, after=wait, specs=specs)

    def feed_forward(self, normed, grad, pieces, shifts, totals):
        lay, width = self.layout, self.width
        rows, count, ranks = lay.frame_rows, len(pieces), self.ranks
        hidden = shifts[0].shape[1]
        unit = hidden // ranks
        tile = hidden

        def body(scalars, normed_ref, grad_ref, *refs):
            refs = list(refs)
            take = lambda n: [refs.pop(0) for _ in range(n)]
            piece_refs, shift_refs = take(count), take(count)
            before = take(2 if totals else 0)
            out_ref, back_ref = take(2)
            grad_refs, sum_refs = take(count), take(count)
            ups, downs, up_grad, down_grad = take(4)
            out_ref[...] = before[0][...] if totals else jnp.zeros_like(out_ref)
            back_ref[...] = before[1][...] if totals else jnp.zeros_like(back_ref)
            for item in range(count):
                for k in range(ranks):
                    at = slice(k * unit, (k + 1) * unit)
                    ups[at] = piece_refs[item][k, :unit]
                    downs[at] = piece_refs[item][k, unit : 2 * unit]

                @pl.loop(0, hidden // tile)
                def _(m, item=item):
                    at = pl.ds(pl.multiple_of(m * tile, tile), tile)
                    up, down = ups[at], downs[at]
                    values = nt(normed_ref[...], up) + shift_refs[item][:, at]
                    half = 0.5 * (1.0 + lax.erf(values * SQRT_HALF))
                    active = (values * half).astype(LOW)
                    slope = half + values * jnp.exp(-0.5 * values * values) * INV_ROOT_TAU
                    out_ref[...] += nn(active, down)
                    down_grad[at] = tn(active, grad_ref[...]).astype(LOW)
                    hidden_grad = (nt(grad_ref[...], down) * slope).astype(LOW)
                    up_grad[at] = tn(hidden_grad, normed_ref[...]).astype(LOW)
                    back_ref[...] += nn(hidden_grad, up)
                    sum_refs[item][:, at] = column_sum(hidden_grad)

                for k in range(ranks):
                    at = slice(k * unit, (k + 1) * unit)
                    grad_refs[item][k, :unit] = up_grad[at]
                    grad_refs[item][k, unit:] = down_grad[at]

        outs = [shape(rows, width, dtype=F32)] * 2
        outs += [shape(ranks, 2 * unit, width)] * count + [shape(1, hidden, dtype=F32)] * count
        ins = [normed, grad] + list(pieces) + list(shifts) + list(totals or ())
        flops = 12 * rows * width * hidden * count
        scratch = [pltpu.VMEM((hidden, width), LOW)] * 4
        outs = self.call(body, outs, ins, flops, scratch)
        return outs[:2], outs[2 : 2 + count], outs[2 + count :]

    def feed_forward_back(self, after, out, back, grad, mixed, wout, along):
        lay, width, group = self.layout, self.width, self.group
        rows, quarters = lay.frame_rows, self.quarters

        def body(scalars, after_ref, out_ref, back_ref, grad_ref, wout_ref, along_ref, *refs):
            mixed_refs, refs = refs[:quarters], refs[quarters:]
            layer_ref, total_ref, sums, wout_grad = refs[:4]
            mixed_grads = refs[4:]
            swap = swapper(scalars, self.place.paired)
            after = after_ref[...]
            layer_ref[...] = (after + swap(out_ref[...]) + along_ref[9:10]).astype(LOW)
            unit, inverse = unit_of(after)
            back, gain, shift = norm_back(swap(back_ref[...]), unit, inverse, along_ref[2:3])
            grad = grad_ref[...].astype(F32)
            total = grad + back
            total_ref[...] = total
            low = total.astype(LOW)
            sums[0:1] = gain
            sums[1:2] = shift
            sums[2:3] = column_sum(low)
            sums[3:4] = column_sum(grad)
            turned = swap(low.astype(F32)).astype(LOW)
            for j in range(quarters):
                at = slice(j * group, (j + 1) * group)
                mixed_grads[j][...] = nt(turned, wout_ref[at]).astype(LOW)
                wout_grad[at] = tn(mixed_refs[j][...], turned).astype(LOW)

        outs = [
            shape(rows, width),
            shape(rows, width, dtype=F32),
            shape(4, width, dtype=F32),
            shape(self.all_heads, width),
        ] + [shape(rows, group)] * quarters
        ins = [after, out, back, grad, wout, along] + list(mixed)
        outs = self.call(body, outs, ins, 4 * rows * width * self.all_heads)
        return outs[:4], outs[4:]

    def spatial_input(self, backs, after, total, along, fc, matrix, wait=()):
        lay, width = self.layout, self.width
        rows, quarters = lay.frame_rows, self.quarters
        far = [] if matrix is None else [matrix]

        def body(scalars, *refs):
            back_refs, refs = refs[:quarters], refs[quarters:]
            after_ref, total_ref, along_ref, refs = refs[0], refs[1], refs[2], refs[3:]
            fc_refs, refs = refs[: len(fc)], refs[len(fc) :]
            low_ref, out_ref, sums = refs[len(far) : len(far) + 3]
            swap = swapper(scalars, self.place.paired)
            grad = swap(sum(ref[...].astype(F32) for ref in back_refs))
            unit, inverse = unit_of(after_ref[...])
            back, gain, shift = norm_back(grad, unit, inverse, along_ref[1:2])
            low = (total_ref[...] + back).astype(LOW)
            low_ref[...] = low
            weight = jnp.concatenate([ref[...] for ref in fc_refs])
            temporal = swap(nt(low, weight)).astype(LOW)
            out_ref[...] = temporal
            sums[0:1] = gain
            sums[1:2] = shift
            sums[2:3] = column_sum(temporal)
            sums[3:4] = column_sum(low)
            if far:
                refs[4][...] = nn(refs[0][...], temporal).astype(LOW)

        outs = [shape(rows, width), shape(rows, width), shape(4, width, dtype=F32)]
        outs += [shape(item.shape[0], width) for item in far]
        ins = list(backs) + [after, total, along] + list(fc) + far
        return self.call(body, outs, ins, 2 * rows * width * width, after=wait)

    def out_weights(self, wout_grad, low, temporal, vectors, wait=()):
        width, group, piece = self.width, self.group, self.piece
        quarters, ranks = self.quarters, self.ranks
        extra, quarter = vectors.shape[1], width // quarters
        each = piece + extra

        def body(scalars, wout_ref, low_ref, temporal_ref, vectors_ref, *refs):
            pieces, fc = refs[:quarters], refs[quarters]
            swap = swapper(scalars, self.place.paired)
            turned = swap(temporal_ref[...].astype(F32)).astype(LOW)
            fc[...] = tn(low_ref[...], turned).astype(LOW)
            for i in range(quarters):
                spot = (scalars[1] ^ i) * piece
                for j in range(quarters):
                    k = group_of(scalars[1]) ^ group_of(j)
                    pieces[i][rows_at(k * each, piece)] = wout_ref[rows_at(j * group + spot, piece)]
                for k in range(ranks):
                    pieces[i][k * each + piece : (k + 1) * each] = vectors_ref[k]
                pieces[i][ranks * each :] = fc[rows_at((scalars[1] ^ i) * quarter, quarter)]

        outs = [shape(ranks * each + quarter, width)] * quarters
        ins = [wout_grad, low, temporal, vectors]
        flops = 2 * low.shape[0] * width * width
        return self.call(body, outs, ins, flops, [pltpu.VMEM((width, width), LOW)], wait)

    def natural(self, parts, cost, wait=()):
        lay, width = self.layout, self.width
        count = lay.natural_blocks
        counts = [len(rows) for _, rows in parts]

        def body(scalars, *refs):
            refs = list(refs)
            out_ref = refs.pop()
            total = jnp.zeros((count * WINDOW, width), F32)
            for size in counts:
                matrix = refs.pop(0)
                source = jnp.concatenate([refs.pop(0)[...] for _ in range(size)])
                total = total + nn(matrix[...], source)
            total = total.astype(LOW)
            for item in range(count):
                part = total[item * WINDOW : item * WINDOW + lay.places]
                out_ref[item] = part

                @pl.when(jnp.logical_not(self.live(scalars, item // lay.frames)))
                def _(item=item):
                    out_ref[item] = jnp.zeros((lay.places, width), LOW)


        ins = []
        for matrix, rows in parts:
            ins += [matrix] + list(rows)
        return self.call(body, [shape(count, lay.places, width)], ins, after=wait, cost=cost)[0]


def body(
    clip_input,
    clip_slot,
    norm_gain,
    norm_shift,
    attention_in,
    attention_bias,
    attention_out,
    branch_bias,
    temporal_fc,
    hidden_in,
    hidden_bias,
    hidden_out,
    output_grad,
):
    place = Place()
    shards, quarters, ranks = place.shards, place.quarters, place.ranks
    shard, context, tensor = place.shard, place.context, place.tensor
    clips, cotangents = clip_input[:, 0], output_grad[:, 0]
    lay = Layout(place, clips)
    columns = attention_in.shape[1]
    width = columns * shards
    group = attention_in.shape[3]
    heads = group // HEAD_DIM
    hidden = hidden_in.shape[1]
    piece = group // quarters
    scalars = jnp.concatenate([jnp.stack([shard, context, tensor]), clip_slot[:, 0]])
    prog = Program(place, lay, width, group, scalars.astype(jnp.int32))
    moves = lay.matrices()
    split = lay.split > 0

    def beside(rows):
        return [rows, hop(rows, SHARD, 1)] if split else [rows]

    def swapped(rows, axis):
        return [rows[0]] + [hop(rows[k], axis, k) for k in range(1, len(rows))]

    def to_all(rows, axis):
        if axis == CONTEXT:
            far = hop(rows, axis, 2)
            return [rows, hop(rows, axis, 1), far, hop(far, axis, 1)]
        return [rows] + [hop(rows, axis, k) for k in range(1, ranks)]

    def shard_parts(block, axis=1):
        if place.paired:
            return [block, hop(block, SHARD, 1)]
        return [lax.all_gather(block, SHARD, axis=axis, tiled=True)]

    def bias_rows(index):
        rows = attention_bias[index].reshape(-1)
        return jnp.pad(rows, (0, columns - rows.size))[None]

    def in_rows(index):
        return jnp.transpose(attention_in[index], (1, 2, 0)).reshape(3 * group, columns)

    def bias_of(parts, row):
        kinds = 2 * heads * (HEAD_DIM // shards)
        if place.paired:
            lines = [part[row, :kinds] for part in parts]
            lines = jnp.where(shard == 0, jnp.stack(lines), jnp.stack(lines[::-1]))
        else:
            lines = parts[0][row].reshape(shards, columns)[:, :kinds]
        lines = lines.reshape(shards, 2, heads, HEAD_DIM // shards)
        lines = jnp.transpose(lines, (1, 2, 0, 3)).reshape(2, group).astype(F32)
        return jnp.concatenate([lines[0], jnp.zeros(group, F32), lines[1]])[None]

    flat = lambda rows: rows.reshape((-1,) + rows.shape[2:])
    clips, cotangents = flat(clips), flat(cotangents)
    quarter = lambda rows: pick(rows.reshape(quarters, -1, columns), context)
    up_part = pick(hidden_in.reshape(columns, quarters, -1), context, 1).T
    unit = up_part.shape[0]
    block = [up_part, quarter(hidden_out), quarter(attention_out[1])]
    block.append(jnp.pad(hidden_bias.reshape(1, -1), ((0, 15), (0, 0))))
    gather_c = Gather(place, jnp.concatenate(block))

    along = jnp.concatenate([norm_gain, norm_shift, branch_bias, bias_rows(0)])
    along = shard_parts(jnp.pad(along, ((0, 16 - along.shape[0]), (0, 0))))
    shift_a = bias_of(along, 10)
    if place.paired:
        along = jnp.where(shard == 0, *[jnp.concatenate(pair, -1) for pair in (along, along[::-1])])
    else:
        along = along[0]
    along = along[:10].astype(F32)

    come, others = None, None
    if split:
        sent, others = prog.send_rows(clips, cotangents, moves[Move.begin_far])
        come = hop(sent, SHARD, 1)
    weights_a = jnp.concatenate([in_rows(0), attention_out[0]])
    weights_a = shard_parts(tie(weights_a, come) if split else weights_a)
    start_t, unit_a = prog.temporal_start(clips, come, moves[Move.beginning])
    units_a = to_all(unit_a, TENSOR)
    gather_c.columns(unit_a)
    gather_c.rows()

    qkv_a, mixed_a, normed_a, parts = prog.temporal(
        units_a, weights_a, along, shift_a
    )
    fc = shard_parts(tie(temporal_fc, parts[0]), 0)
    if split:
        others = hop(tie(others, units_a[1]), SHARD, 1)
    temporal_t = prog.temporal_out(
        swapped(parts, TENSOR), along, moves.get(Move.return_far), gather_c.far
    )
    sources = [temporal_t[0]] + [hop(rows, SHARD, 1) for rows in temporal_t[1:]]
    in_b = jnp.concatenate([in_rows(1), jnp.pad(bias_rows(1), ((0, 15), (0, 0)))])
    in_b = hop_group(tie(in_b, sources[-1]))
    weights_b = shard_parts(in_b)
    shift_b = bias_of(weights_b, 3 * group)

    start = prog.frames_of(clips, others, 0, moves[Move.starting], Cost.frames_start, [units_a[1]])
    after_a, temporal, normed_b = prog.spatial_in(
        sources, moves[Move.returning], start, fc, along
    )
    normed_b = to_all(normed_b, CONTEXT)
    qkv_b, mixed = prog.spatial(normed_b, weights_b, shift_b)
    mixed = swapped(mixed, CONTEXT)
    grad = prog.frames_of(
        cotangents, others, 1, moves[Move.starting], Cost.frames_grad, [parts[0]]
    )
    pieces_c = gather_c.cores(after_a)
    line = gather_c.first[:, 2 * unit + piece].astype(F32)
    up_shift = line.reshape((ranks, shards) + hidden_bias.shape)
    if place.paired:
        up_shift = jnp.where(shard == 0, up_shift, up_shift[:, ::-1])
    up_shift = jnp.swapaxes(up_shift, 1, 2).reshape(ranks, quarters, unit)
    up_shift = [pick(up_shift, context ^ j, 1).reshape(1, -1) for j in range(quarters)]
    after_b, normed_c, low, wout_b = prog.spatial_out(
        mixed, pieces_c, 2 * unit, after_a, grad, along
    )

    totals = None
    piece_grads, up_bias_grads = [None] * quarters, [None] * quarters
    for pair in ((1, 3), (0, 2)):
        totals, grads, sums = prog.feed_forward(
            normed_c, low, [pieces_c[j] for j in pair], [up_shift[j] for j in pair], totals
        )
        for index, j in enumerate(pair):
            piece_grads[j] = grads[index]
            up_bias_grads[j] = sums[index]
    reduce_c = ReduceHidden(place, piece_grads)
    kept, mixed_grads = prog.feed_forward_back(
        after_b, totals[0], totals[1], grad, mixed, wout_b, along
    )
    layer_rows, total, sums_c, wout_grad = kept
    wait = reduce_c.cores(layer_rows)

    mixed_grads = swapped(mixed_grads, CONTEXT)
    qkv_grads, backs = prog.spatial_back(qkv_b, mixed_grads, weights_b, wait)
    done = backs[0]
    reduce_c.start_low(done)
    backs = swapped(backs, CONTEXT)
    group_grads = prog.group_weights(qkv_grads, normed_b, wait=[reduce_c.come_top] if split else ())
    low_total, temporal_grad, sums_b, *sent = prog.spatial_input(
        backs, after_a, total, along, fc, moves.get(Move.arrive_far), [group_grads[0]]
    )

    sources = [temporal_grad] + [hop(rows, SHARD, 1) for rows in sent]
    out_grad = prog.temporal_grad(sources, moves[Move.arriving])
    out_grads = to_all(out_grad, TENSOR)
    layer_out, home = [(moves[Move.ending], [layer_rows])], [(moves[Move.ending], [low_total])]
    if split:
        far = hop(tie(jnp.concatenate([layer_rows[lay.own :], low_total[lay.own :]]), out_grad), SHARD, 1)
        layer_out.append((moves[Move.end_far], [far[: far.shape[0] // 2]]))
        home.append((moves[Move.end_far], [far[far.shape[0] // 2 :]]))
    layer_out = prog.natural(layer_out, Cost.natural_first, [out_grad])
    grads_b = group_grads
    sums = [sums_b[0], sums_c[0], sums_b[1], sums_c[1], sums_b[2], sums_b[3], sums_c[2], sums_c[3]]
    outer = ordered([item.reshape(ranks, -1) for item in up_bias_grads], context, 1)
    outer = outer.reshape(ranks, -1, shards, hidden_bias.shape[1])
    outer = jnp.swapaxes(outer, 1, 2).reshape(ranks, 1, width)
    sums = jnp.stack(sums)
    vectors = jnp.concatenate([jnp.broadcast_to(sums, (ranks,) + sums.shape), outer], 1)
    if place.paired:
        flipped = jnp.concatenate([vectors[..., columns:], vectors[..., :columns]], -1)
        vectors = jnp.where(shard == 0, vectors, flipped)
    vectors = jnp.pad(vectors, ((0, 0), (0, 16 - vectors.shape[1]), (0, 0))).astype(LOW)
    pieces = prog.out_weights(wout_grad, low_total, temporal, vectors, [out_grad, reduce_c.come_low])
    reduce_out = ReduceShared(place, pieces, piece + vectors.shape[1])
    reduce_out.cores(out_grads[1])
    wait = [layer_out, pieces[0]] + reduce_c.low_leg(out_grad) + reduce_c.top_leg(out_grad)
    qkv_grads, backs, sums_a = prog.temporal_back(qkv_a, out_grads, units_a, weights_a, wait)
    done = backs[0]
    backs = swapped(backs, TENSOR)
    group_grads = prog.group_weights(
        qkv_grads, normed_a, mixed_a, out_grads, [sums_a], cost=Cost.group_weights_last
    )
    back, *sent = prog.temporal_input(
        backs, start_t, along, moves.get(Move.home_far), reduce_out.rows(done) + [group_grads[0]]
    )
    reduce_c.both(back)
    total_in_b = hop_group(sum_columns(place, grads_b[0], grads_b[-1], back))
    total_in_a = sum_columns(place, group_grads[0], group_grads[-1])
    home.append((moves[Move.homing], [back] + [hop(rows, SHARD, 1) for rows in sent]))
    input_grad = prog.natural(home, Cost.natural_last)

    reduce_out.columns(total_in_a[4 * group + 16 :])
    sum_in = SumContext(place, jnp.concatenate([total_in_a, tie(total_in_b, back)]))
    sum_in.cores()
    reduce_c.hops()
    reduce_out.hops()
    total_c, total_out, total_in = reduce_c.finish(), reduce_out.finish(), sum_in.finish()
    total_in_a, total_in_b = total_in[: total_in_a.shape[0]], total_in[total_in_a.shape[0] :]
    sums_a = jnp.sum(total_out[:, -16:], 0)
    total_out = total_out[:, :-16]

    def in_grad(total):
        part = total[: 3 * group].reshape(3, group, columns)
        return jnp.transpose(part, (2, 0, 1))

    def bias_grad(line):
        part = HEAD_DIM // shards
        if place.paired:
            return pick(line.reshape(2, heads, shards, part), shard, 2)
        return line[: 2 * heads * part].reshape(2, heads, part)

    in_total = jnp.stack([in_grad(total_in_a), in_grad(total_in_b)])
    inner = jnp.stack([bias_grad(total_in_a[4 * group]), bias_grad(total_in_b[3 * group])])
    out_b = total_out[:, :piece].reshape(group, columns)
    out_total = jnp.stack([total_in_a[3 * group : 4 * group], out_b])
    fc_total = total_out[:, -(width // quarters) :].reshape(width, columns).T
    vectors = total_out[0, piece:]
    gains = jnp.concatenate([sums_a[:1], vectors[0:2]])
    shifts = jnp.concatenate([sums_a[1:2], vectors[2:4]])
    rows_shape = clip_input.shape
    return (
        layer_out.reshape(rows_shape),
        input_grad.reshape(rows_shape),
        gains,
        shifts,
        in_total,
        inner,
        out_total,
        vectors[4:8],
        fc_total,
        total_c[:, :unit].reshape(hidden, columns).T,
        vectors[8].reshape(hidden_bias.shape),
        total_c[:, unit:].reshape(hidden, columns),
    )


def solution(mesh):
    rows = P(None, SHARD, TENSOR, CONTEXT, None)
    weights = (
        P(None, SHARD),
        P(None, SHARD),
        P(None, SHARD, None, TENSOR),
        P(None, None, TENSOR, SHARD),
        P(None, TENSOR, SHARD),
        P(None, SHARD),
        P(SHARD, None),
        P(SHARD, TENSOR),
        P(TENSOR, SHARD),
        P(TENSOR, SHARD),
    )
    return jax.shard_map(
        body,
        mesh=mesh,
        in_specs=(rows, P(None, SHARD)) + weights + (rows,),
        out_specs=(rows, rows) + weights,
        check_vma=False,
    )
```

```python
import jax
import jax.numpy as jnp
import numpy as np
from jax import lax
from jax.experimental import pallas as pl
from jax.experimental.pallas import tpu as pltpu
from jax.sharding import PartitionSpec as P

HEAD_DIM = 64
WINDOW = 64
CHUNK = 32
EPS = 1e-06
SQRT_HALF = 0.7071067811865476
INV_ROOT_TAU = 0.3989422804014327
SCALE = HEAD_DIM**-0.5
HIDE = -1e30
LOW = jnp.bfloat16
F32 = jnp.float32
VMEM_BYTES = 60 * 2**20
PEAK = 1.15e9
SHARD, CONTEXT, TENSOR = "shard", "context", "tensor"


class Cost:
    group_weights_last = 0.2
    natural_first = 40
    frames_start = 40
    frames_grad = 40
    natural_last = 60
    send_rows = 6
    temporal_start = 10
    temporal = 30
    temporal_out = 6
    spatial_in = 8
    spatial = 20
    spatial_out = 8
    feed_forward = 26
    feed_forward_back = 10
    spatial_back = 28
    spatial_input = 20
    temporal_grad = 20
    temporal_back = 70
    temporal_input = 70
    group_weights = 0.2
    natural = 0.2
    out_weights = 0.2
    frames_of = 0.2


class Move:
    beginning, starting, returning, arriving, homing, ending = range(6)
    begin_far, return_far, arrive_far, home_far, end_far = range(6, 11)


def hop(values, axis, step):
    count = lax.axis_size(axis)
    return lax.ppermute(values, axis, [(i, i ^ step) for i in range(count)])


def hop_group(values):
    quarters, ranks = lax.axis_size(CONTEXT), lax.axis_size(TENSOR)
    pairs = [
        (c * ranks + i, c * ranks + (i ^ group_of(c))) for c in range(quarters) for i in range(ranks)
    ]
    return lax.ppermute(values, (CONTEXT, TENSOR), pairs)


def group_of(context):
    return 2 * (context % 2) + context // 2


def pick(values, index, axis=0):
    return lax.dynamic_index_in_dim(values, index, axis, keepdims=False)


def ordered(parts, me, axis=0):
    shape = list(parts[0].shape)
    shape.insert(axis, len(parts))
    out = jnp.zeros(shape, parts[0].dtype)
    for j, part in enumerate(parts):
        out = lax.dynamic_update_index_in_dim(out, part, me ^ j, axis)
    return out


def round_up(value, step):
    return -(-value // step) * step


class Place:
    def __init__(self):
        self.shard = lax.axis_index(SHARD)
        self.context = lax.axis_index(CONTEXT)
        self.tensor = lax.axis_index(TENSOR)
        self.shards = lax.axis_size(SHARD)
        self.ranks = lax.axis_size(TENSOR)
        self.quarters = lax.axis_size(CONTEXT)
        self.paired = self.shards == 2


def tie(values, *others):
    return lax.optimization_barrier((values,) + others)[0] if others else values


def add(*terms):
    total = terms[0].astype(F32)
    for term in terms[1:]:
        total = total + term.astype(F32)
    return total.astype(LOW)


class Gather:
    def __init__(self, place, mine):
        self.place = place
        self.parts = [mine] + [hop(mine, TENSOR, k) for k in range(1, place.ranks)]

    def columns(self, *later):
        blocks = jnp.stack([tie(part, *later) for part in self.parts])
        if self.place.paired:
            self.parts = [blocks, hop(blocks, SHARD, 1)]
        else:
            self.parts = [lax.all_gather(blocks, SHARD, axis=2, tiled=True)]
        self.far = [hop(blocks, CONTEXT, 2)] if self.place.paired else []

    def rows(self, *later):
        self.far.append(hop(tie(self.parts[-1], *later), CONTEXT, 2))

    def cores(self, *later):
        join = lambda parts: jnp.concatenate([tie(part, *later) for part in parts], -1)
        self.first, second = join(self.parts), join(self.far)
        return [self.first, hop(self.first, CONTEXT, 1), second, hop(second, CONTEXT, 1)]


class ReduceHidden:
    def __init__(self, place, pieces):
        self.place = place
        self.kept = [pieces[0], pieces[2]]
        self.come = [hop(pieces[1], CONTEXT, 1), hop(pieces[3], CONTEXT, 1)]
        self.middle = pieces[0].shape[1] // 2
        self.half = pieces[0].shape[2] // (2 if place.paired else 1)

    def part(self, index, rows, columns):
        return add(self.kept[index][:, rows, columns], self.come[index][:, rows, columns])

    def cores(self, *later):
        self.come = [tie(item, *later) for item in self.come]
        top, low = slice(self.middle), slice(self.middle, None)
        left, right = slice(self.half), slice(self.half, None)
        out = []
        if self.place.paired:
            sent = jnp.stack([self.part(index, top, right) for index in range(2)])
            out.append(sent)
            self.come_top = hop(sent, SHARD, 1)
        self.sent_low = self.part(1, low, slice(None))
        self.kept_top = lambda: jnp.stack([self.part(index, top, left) for index in range(2)])
        self.kept_low = lambda at: self.part(0, low, at)
        return out + [self.sent_low]

    def start_low(self, *later):
        self.come_low = hop(tie(self.sent_low, *later), CONTEXT, 2)

    def scatter(self, total):
        axis = total.ndim - 1
        return lax.psum_scatter(total, SHARD, scatter_dimension=axis, tiled=True)

    def top_leg(self, *later):
        top = self.kept_top()
        top = add(top, tie(self.come_top, *later)) if self.place.paired else self.scatter(top)
        self.top, self.come_top = top[0], hop(top[1], CONTEXT, 2)
        return [top]

    def low_leg(self, *later):
        come = tie(self.come_low, *later)
        left, right = slice(self.half), slice(self.half, None)
        low = add(self.kept_low(left), come[..., left])
        if self.place.paired:
            sent = add(self.kept_low(right), come[..., right])
            self.come_low = hop(sent, SHARD, 1)
        else:
            low, sent, self.come_low = self.scatter(low), low, None
        self.low = low
        return [low, sent]

    def both(self, *later):
        top = add(self.top, tie(self.come_top, *later))
        low = self.low if self.come_low is None else add(self.low, tie(self.come_low, *later))
        mine = jnp.concatenate([top, low], 1)
        self.kept = mine[0]
        self.come = [hop(mine[k], TENSOR, k) for k in range(1, self.place.ranks)]
        return [mine]

    def hops(self, *later):
        self.sum = add(self.kept, *[tie(come, *later) for come in self.come])
        return [self.sum]

    def finish(self):
        return gather_context(self.place, self.sum)


def gather_context(place, mine):
    second = hop(mine, CONTEXT, 2)
    both = jnp.stack([mine, second])
    far = hop(both, CONTEXT, 1)
    return [both, far]


class ReduceShared:
    def __init__(self, place, pieces, each):
        self.place, self.each = place, each
        self.kept = [pieces[0], pieces[2]]
        self.come = [hop(pieces[1], CONTEXT, 1), hop(pieces[3], CONTEXT, 1)]

    def cores(self, *later):
        first, second = [add(a, tie(b, *later)) for a, b in zip(self.kept, self.come)]
        self.kept, self.come = first, hop(second, CONTEXT, 2)
        return [first, second]

    def rows(self, *later):
        come = tie(self.come, *later)
        if self.place.paired:
            half = come.shape[-1] // 2
            sent = add(self.kept[:, half:], come[:, half:])
            self.kept, self.come = add(self.kept[:, :half], come[:, :half]), hop(sent, SHARD, 1)
            return [sent]
        self.kept = lax.psum_scatter(
            add(self.kept, come), SHARD, scatter_dimension=1, tiled=True
        )
        self.come = None
        return [self.kept]

    def columns(self, more):
        mine = self.kept if self.come is None else add(self.kept, self.come)
        ranks, each = self.place.ranks, self.each
        common = jnp.concatenate([mine[ranks * each :], more])
        block = lambda k: jnp.concatenate([mine[k * each : (k + 1) * each], common])
        self.kept = block(0)
        self.come = [hop(block(k), TENSOR, k) for k in range(1, ranks)]
        return [mine]

    def hops(self, *later):
        self.sum = add(self.kept, *[tie(come, *later) for come in self.come])
        return [self.sum]

    def finish(self):
        return gather_context(self.place, self.sum)


def sum_columns(place, kept, sent, *later):
    if place.paired:
        return add(kept, tie(hop(sent, SHARD, 1), *later))
    return lax.psum_scatter(kept, SHARD, scatter_dimension=1, tiled=True)


class SumContext:
    def __init__(self, place, total):
        self.core, self.shape = place.context % 2, total.shape
        halves = total.reshape(2, -1, total.shape[-1])
        self.kept, self.come = pick(halves, self.core), hop(pick(halves, 1 - self.core), CONTEXT, 1)

    def cores(self, *later):
        self.kept = add(self.kept, tie(self.come, *later))
        self.come = hop(self.kept, CONTEXT, 2)
        return [self.kept]

    def finish(self):
        half = add(self.kept, self.come)
        whole = ordered([half, hop(half, CONTEXT, 1)], self.core)
        return whole.reshape(self.shape).astype(F32)


class Layout:
    def __init__(self, place, clips):
        self.place = place
        self.batches, self.frames, self.places = clips.shape[:3]
        self.whole = 1 if place.paired else self.batches
        self.split = self.batches - self.whole
        self.first = self.whole * self.places
        self.later = -(-self.split * self.places // 2)
        self.slots = round_up(self.first + self.later, CHUNK)
        self.temporal_rows = self.frames * self.slots
        self.units = self.whole * self.frames + self.split
        self.frame_rows = round_up(self.units * self.places, 16)
        self.natural_blocks = self.batches * self.frames
        self.own = self.whole * self.frames * self.places // 16 * 16

    def label(self, batch, frame, spot):
        return (batch * self.frames * self.place.ranks + frame) * self.places + spot

    def split_labels(self, part, frames):
        flat = self.later * part + np.arange(self.later)[None]
        labels = self.label(
            self.whole + flat // self.places, np.asarray(frames)[:, None], flat % self.places
        )
        return np.where(flat < self.split * self.places, labels, -1)

    def frames_at(self, tensor):
        return self.frames * tensor + np.arange(self.frames)

    def temporal_labels(self, shard, tensor):
        frames = self.frames_at(tensor)
        slot = np.arange(self.first)[None]
        parts = [self.label(slot // self.places, frames[:, None], slot % self.places)]
        if self.split:
            parts.append(self.split_labels(shard, frames))
        labels = np.concatenate(parts, 1)
        spare = self.slots - labels.shape[1]
        return np.pad(labels, ((0, 0), (0, spare)), constant_values=-1)

    def frame_labels(self, shard, tensor, far=False):
        row = np.arange(self.frame_rows)
        unit, spot = row // self.places, row % self.places
        batch, frame = unit // self.frames, self.frames * tensor + unit % self.frames
        later = unit - self.whole * self.frames
        batch = np.where(later >= 0, self.whole + later, batch)
        frame = np.where(later >= 0, self.frames * tensor + shard, frame)
        inside = (unit < self.units) & ((later >= 0) | (not far))
        return np.where(inside, self.label(batch, frame, spot), -1)

    def natural_labels(self, tensor):
        batch = np.arange(self.batches)[:, None, None]
        frame = self.frames_at(tensor)[None, :, None]
        spot = np.arange(WINDOW)[None, None]
        return np.where(spot < self.places, self.label(batch, frame, spot), -1)

    def other_labels(self, shard, tensor):
        batch = np.arange(self.whole, self.batches)[:, None]
        spot = np.arange(WINDOW)[None]
        labels = self.label(batch, self.frames * tensor + shard, spot)
        return np.where(spot < self.places, labels, -1)

    def moves(self, shard, tensor):
        natural, frame = self.natural_labels(tensor), self.frame_labels(shard, tensor)
        temporal = self.temporal_labels(shard, tensor)
        moves = {
            Move.beginning: ([temporal], [natural]),
            Move.starting: ([frame], [natural]),
            Move.returning: ([frame], [temporal]),
            Move.arriving: ([temporal], [frame]),
            Move.homing: ([natural], [temporal]),
            Move.ending: ([natural], [frame]),
        }
        if self.split:
            frames, other = self.frames_at(tensor), 1 - shard

            def packed(part, frames):
                labels = self.split_labels(part, frames).reshape(-1)
                spare = round_up(labels.size, 16) - labels.size
                return np.pad(labels, (0, spare), constant_values=-1)

            mine, theirs = packed(shard, frames), packed(other, frames)
            moves[Move.beginning][1].append(mine)
            moves[Move.starting][1].append(self.other_labels(shard, tensor))
            moves[Move.returning][1].append(packed(other, [frames[shard]]))
            moves[Move.arriving][1].append(packed(shard, [frames[other]]))
            moves[Move.homing][1].append(theirs)
            moves[Move.begin_far] = ([theirs], [natural])
            moves[Move.return_far] = ([packed(shard, [frames[other]])], [temporal])
            moves[Move.arrive_far] = ([packed(other, [frames[shard]])], [frame])
            moves[Move.home_far] = ([mine], [temporal])
            moves[Move.end_far] = ([natural], [self.frame_labels(other, tensor, True)[self.own :]])
        flat = lambda parts: np.concatenate([np.asarray(part).reshape(-1) for part in parts])
        return {key: (flat(targets), flat(sources)) for key, (targets, sources) in moves.items()}

    def matrices(self):
        ranks = self.place.ranks
        shards = 2 if self.split else 1
        table = [self.moves(i // ranks, i % ranks) for i in range(shards * ranks)]
        line = lambda moves: np.concatenate([part for pair in moves.values() for part in pair])
        lines = jnp.asarray(np.stack([line(moves) for moves in table]).astype(np.int32))
        index = self.place.tensor + (ranks * self.place.shard if self.split else 0)
        labels, at, out = pick(lines, index), 0, {}
        for key, (targets, sources) in table[0].items():
            ends = at + targets.size, at + targets.size + sources.size
            target, source = labels[at : ends[0]], labels[ends[0] : ends[1]]
            same = (target[:, None] == source[None]) & (target[:, None] >= 0)
            out[key], at = same.astype(LOW), ends[1]
        return out


def call(body, outs, ins, scalars, cost=1, scratch=(), after=(), name=None, specs=None):
    given, count = body, len(ins)
    if after:
        body = lambda scalars, *refs: given(scalars, *refs[:count], *refs[count + len(after) :])
    moved = sum(item.size * item.dtype.itemsize for item in list(outs) + list(ins))
    spec = pl.BlockSpec(memory_space=pltpu.VMEM)
    return pl.pallas_call(
        body,
        name=name,
        out_shape=tuple(outs),
        in_specs=[pl.BlockSpec(memory_space=pltpu.SMEM)]
        + list(specs or [spec] * len(ins))
        + [pl.BlockSpec(memory_space=pl.ANY)] * len(after),
        out_specs=(spec,) * len(outs),
        scratch_shapes=list(scratch),
        grid=(1,) if specs else (),
        compiler_params=pltpu.CompilerParams(vmem_limit_bytes=VMEM_BYTES),
        cost_estimate=pl.CostEstimate(
            flops=int(PEAK * cost), bytes_accessed=moved if cost >= 1 else 0, transcendentals=0
        ),
    )(scalars, *ins, *after)


def shape(*dims, dtype=LOW):
    return jax.ShapeDtypeStruct(dims, dtype)


def nn(first, second):
    return lax.dot_general(first, second, (((1,), (0,)), ((), ())), preferred_element_type=F32)


def nt(first, second):
    return lax.dot_general(first, second, (((1,), (1,)), ((), ())), preferred_element_type=F32)


def tn(first, second):
    return lax.dot_general(first, second, (((0,), (0,)), ((), ())), preferred_element_type=F32)


def swapper(scalars, paired):
    def swap(values):
        if not paired:
            return values
        half = values.shape[-1] // 2
        other = jnp.concatenate([values[:, half:], values[:, :half]], -1)
        return jnp.where(scalars[0] == 0, values, other)

    return swap


def unit_of(values):
    centred = values - jnp.mean(values, -1, keepdims=True)
    inverse = lax.rsqrt(jnp.mean(centred * centred, -1, keepdims=True) + EPS)
    return (centred * inverse, inverse)


def norm_back(grad, unit, inverse, gain):
    scaled = grad * gain
    inner = (
        scaled
        - jnp.mean(scaled, -1, keepdims=True)
        - unit * jnp.mean(scaled * unit, -1, keepdims=True)
    )
    return (
        inverse * inner,
        jnp.sum(grad * unit, 0, keepdims=True),
        jnp.sum(grad, 0, keepdims=True),
    )


def attention(query, key, value, hide):
    probs = softmax(nt(key, query) + hide)
    return tn(probs.astype(LOW), value)


def softmax(scores):
    weights = jnp.exp(scores - jnp.max(scores, 0, keepdims=True))
    return weights * (1.0 / jnp.sum(weights, 0, keepdims=True))


def attention_back(query, key, value, grad, hide):
    probs = softmax(nt(key, query) + hide)
    prob_grad = nt(value, grad)
    inner = jnp.sum(probs * prob_grad, 0, keepdims=True)
    scored = (probs * (prob_grad - inner)).astype(LOW)
    return (tn(scored, key) * SCALE, nn(scored, query), nn(probs.astype(LOW), grad))


def column_sum(values):
    return jnp.sum(values.astype(F32), 0, keepdims=True)


def rows_at(start, size):
    return pl.ds(pl.multiple_of(start, 16), size)


class Program:
    def __init__(self, place, layout, width, group, scalars):
        self.place, self.layout, self.width, self.group = place, layout, width, group
        self.scalars = scalars
        self.ranks, self.quarters = place.ranks, place.quarters
        self.piece = group // self.quarters
        self.heads = group // HEAD_DIM
        self.all_heads = group * self.ranks
        spot = np.arange(self.ranks * layout.frames * CHUNK) % CHUNK
        self.same_place = jnp.asarray(
            np.where(spot[:, None] == spot[None], 0, HIDE).astype(np.float32)
        )

    def call(self, body, outs, ins, flops=0, scratch=(), after=(), specs=None, cost=None):
        name = body.__qualname__.split(".")[1]
        cost = cost or getattr(Cost, name)
        return call(body, outs, ins, self.scalars, cost, scratch, after, name, specs)

    def lanes(self, c, h):
        at = c * self.group + h * HEAD_DIM
        return slice(at, at + HEAD_DIM)


    def live(self, scalars, batch):
        return scalars[3 + batch] > 0

    def place_natural(self, scalars, rows, source):
        lay = self.layout
        rows[...] = jnp.zeros_like(rows)
        for item in range(lay.natural_blocks):

            @pl.when(self.live(scalars, item // lay.frames))
            def _(item=item):
                rows[item * WINDOW : item * WINDOW + lay.places] = source[item]

    def send_rows(self, clips, cotangents, matrix, wait=()):
        lay, width = self.layout, self.width
        count, split = lay.natural_blocks, lay.split
        first = lay.whole * lay.frames

        def body(scalars, clips_ref, grads_ref, matrix_ref, sent, frames, rows):
            self.place_natural(scalars, rows, clips_ref)
            sent[...] = nn(matrix_ref[...], rows[...]).astype(LOW)
            for index, source in enumerate((clips_ref, grads_ref)):
                for item in range(split):
                    frame = first + lay.frames * item + 1 - scalars[0]
                    frames[index, item] = source[frame]

        outs = [shape(matrix.shape[0], width), shape(2, split, lay.places, width)]
        scratch = [pltpu.VMEM((count * WINDOW, width), LOW)]
        return self.call(body, outs, [clips, cotangents, matrix], scratch=scratch, after=wait)

    def temporal_start(self, clips, come, matrix):
        lay, width = self.layout, self.width
        count, rows_in = lay.natural_blocks, lay.natural_blocks * WINDOW
        more = 0 if come is None else come.shape[0]

        def body(scalars, clips_ref, *refs):
            matrix_ref, start_ref, normed_ref, rows = refs[-4:]
            self.place_natural(scalars, rows, clips_ref)
            if more:
                rows[rows_in:] = refs[0][...]
            start = nn(matrix_ref[...], rows[...])
            start_ref[...] = start.astype(LOW)
            unit, _ = unit_of(start)
            swap = swapper(scalars, self.place.paired)
            normed_ref[...] = swap(unit).astype(LOW)

        outs = [shape(lay.temporal_rows, width)] * 2
        ins = [clips] + ([come] if more else []) + [matrix]
        scratch = [pltpu.VMEM((rows_in + more, width), LOW)]
        return self.call(body, outs, ins, scratch=scratch)

    def frames_of(self, clips, others, index, matrix, cost, wait=()):
        lay, width = self.layout, self.width
        count, split = lay.natural_blocks, lay.split

        def body(scalars, clips_ref, *refs):
            matrix_ref, out_ref, rows = refs[-3:]
            self.place_natural(scalars, rows, clips_ref)
            for item in range(split):

                @pl.when(jnp.logical_not(self.live(scalars, lay.whole + item)))
                def _(item=item):
                    start = (count + item) * WINDOW
                    rows[start : start + lay.places] = refs[0][index, item]

            out_ref[...] = nn(matrix_ref[...], rows[...]).astype(LOW)

        return self.call(
            body,
            [shape(lay.frame_rows, width)],
            [clips] + ([others] if split else []) + [matrix],
            scratch=[pltpu.VMEM(((count + split) * WINDOW, width), LOW)],
            after=wait,
            cost=cost,
        )[0]


    def chunk(self, refs, n):
        lay = self.layout
        return jnp.concatenate(
            [
                ref[rows_at(frame * lay.slots + n * CHUNK, CHUNK)]
                for ref in refs
                for frame in range(lay.frames)
            ]
        )

    def put_chunk(self, refs, n, values):
        lay = self.layout
        for k, ref in enumerate(refs):
            for frame in range(lay.frames):
                at = (k * lay.frames + frame) * CHUNK
                ref[rows_at(frame * lay.slots + n * CHUNK, CHUNK)] = values[at : at + CHUNK]

    def temporal(self, units, weights, along, shift, wait=()):
        lay, width, group, ranks = self.layout, self.width, self.group, self.ranks
        rows = lay.temporal_rows

        def body(scalars, *refs):
            unit_refs, weight_refs = refs[:ranks], refs[ranks : ranks + len(weights)]
            refs = refs[ranks + len(weights) :]
            along_ref, shift_ref, same, refs = refs[0], refs[1], refs[2], refs[3:]
            qkv_refs, mixed_refs, normed_refs, out_refs = (
                refs[at : at + ranks] for at in range(0, 4 * ranks, ranks)
            )
            swap = swapper(scalars, self.place.paired)
            gain, move = swap(along_ref[0:1]), swap(along_ref[3:4])
            weight = jnp.concatenate([ref[: 3 * group] for ref in weight_refs], -1)
            for k in range(ranks):
                normed_refs[k][...] = (unit_refs[k][...].astype(F32) * gain + move).astype(LOW)
                qkv_refs[k][...] = (nt(normed_refs[k][...], weight) + shift_ref[...]).astype(LOW)

            @pl.loop(0, lay.slots // CHUNK, unroll=True)
            def _(n):
                values = self.chunk(qkv_refs, n)
                parts = []
                for h in range(self.heads):
                    query, key, value = (values[:, self.lanes(c, h)] for c in range(3))
                    parts.append(attention(query * LOW(SCALE), key, value, same[...]))
                self.put_chunk(mixed_refs, n, jnp.concatenate(parts, -1).astype(LOW))

            weight = jnp.concatenate([ref[3 * group : 4 * group] for ref in weight_refs], -1)
            for k in range(ranks):
                out_refs[k][...] = nn(mixed_refs[k][...], weight).astype(LOW)

        outs = [shape(rows, 3 * group)] * ranks + [shape(rows, group)] * ranks
        outs += [shape(rows, width)] * (2 * ranks)
        ins = list(units) + list(weights) + [along, shift, self.same_place]
        flops = 8 * ranks * rows * width * group
        flops += 4 * ranks * rows * self.same_place.shape[0] * group
        outs = self.call(body, outs, ins, flops, after=wait)
        return [outs[at : at + ranks] for at in range(0, 4 * ranks, ranks)]

    def temporal_out(self, parts, along, matrix, wait=()):
        lay, width = self.layout, self.width
        far = [] if matrix is None else [matrix]

        def body(scalars, *refs):
            part_refs, along_ref, refs = refs[: self.ranks], refs[self.ranks], refs[self.ranks + 1 :]
            swap = swapper(scalars, self.place.paired)
            total = swap(sum(ref[...].astype(F32) for ref in part_refs)) + along_ref[6:7]
            out_ref = refs[len(far)]
            out_ref[...] = total.astype(LOW)
            if far:
                refs[2][...] = nn(refs[0][...], out_ref[...]).astype(LOW)

        outs = [shape(lay.temporal_rows, width)] + [shape(item.shape[0], width) for item in far]
        return self.call(body, outs, list(parts) + [along] + far, after=wait)

    def temporal_grad(self, parts, matrix, wait=()):
        lay, width = self.layout, self.width

        def body(scalars, *refs):
            matrix_ref, out_ref = refs[len(parts) :]
            swap = swapper(scalars, self.place.paired)
            source = jnp.concatenate([ref[...] for ref in refs[: len(parts)]])
            out_ref[...] = swap(nn(matrix_ref[...], source)).astype(LOW)

        outs = [shape(lay.temporal_rows, width)]
        return self.call(body, outs, list(parts) + [matrix], after=wait)[0]

    def temporal_back(self, qkv, grads, units, weights, wait=()):
        lay, width, group, ranks = self.layout, self.width, self.group, self.ranks
        rows = lay.temporal_rows

        def body(scalars, *refs):
            qkv_refs, grad_refs, unit_refs = (
                refs[at : at + ranks] for at in range(0, 3 * ranks, ranks)
            )
            refs = refs[3 * ranks :]
            weight_refs, same, refs = refs[: len(weights)], refs[len(weights)], refs[len(weights) + 1 :]
            out_refs, back_refs, sums = refs[:ranks], refs[ranks : 2 * ranks], refs[2 * ranks]
            mixed = refs[2 * ranks + 1 :]
            weight = jnp.concatenate([ref[3 * group : 4 * group] for ref in weight_refs], -1)
            for k in range(ranks):
                mixed[k][...] = nt(grad_refs[k][...], weight).astype(LOW)

            @pl.loop(0, lay.slots // CHUNK, unroll=True)
            def _(n):
                values, grads = self.chunk(qkv_refs, n), self.chunk(mixed, n)
                parts = [[], [], []]
                for h in range(self.heads):
                    query, key, value = (values[:, self.lanes(c, h)] for c in range(3))
                    grad = grads[:, self.lanes(0, h)]
                    got = attention_back(query * LOW(SCALE), key, value, grad, same[...])
                    for part, item in zip(parts, got):
                        part.append(item)
                total = jnp.concatenate(parts[0] + parts[1] + parts[2], -1)
                self.put_chunk(out_refs, n, total.astype(LOW))

            weight = jnp.concatenate([ref[: 3 * group] for ref in weight_refs], -1)
            sums[...] = jnp.zeros_like(sums)
            for k in range(ranks):
                back = nn(out_refs[k][...], weight)
                back_refs[k][...] = back.astype(LOW)
                sums[0:1] += column_sum(back * unit_refs[k][...].astype(F32))
                sums[1:2] += column_sum(back)

        outs = [shape(rows, 3 * group)] * ranks + [shape(rows, width)] * ranks
        outs += [shape(8, width, dtype=F32)]
        ins = list(qkv) + list(grads) + list(units) + list(weights) + [self.same_place]
        flops = 8 * ranks * rows * width * group
        flops += 10 * ranks * rows * self.same_place.shape[0] * group
        scratch = [pltpu.VMEM((rows, group), LOW)] * ranks
        outs = self.call(body, outs, ins, flops, scratch, wait)
        return outs[:ranks], outs[ranks : 2 * ranks], outs[-1]

    def group_weights(self, qkv_grads, normed, mixed=(), out_grads=(), more=(), wait=(), cost=None):
        width, group, count = self.width, self.group, len(qkv_grads)
        parts = 2 if self.place.paired else 1
        size = 3 * group + (group if mixed else 0)

        def body(scalars, *refs):
            refs = list(refs)
            take = lambda n: [refs.pop(0) for _ in range(n)]
            grad_refs, normed_refs = take(count), take(count)
            mixed_refs, out_grad_refs = take(len(mixed)), take(len(mixed))
            more_refs, (spread,), out_refs = take(len(more)), take(1), refs
            columns = width // parts

            def put(start, total):
                for part in range(parts):
                    values = total[:, part * columns : (part + 1) * columns]
                    out_refs[part][start : start + total.shape[0]] = values.astype(LOW)

            total = jnp.zeros((3 * group, width), F32)
            sums = jnp.zeros((1, 3 * group), F32)
            for j in range(count):
                total = total + tn(grad_refs[j][...], normed_refs[j][...])
                sums = sums + column_sum(grad_refs[j][...])
            put(0, total)
            if mixed:
                total = jnp.zeros((group, width), F32)
                for j in range(count):
                    total = total + tn(mixed_refs[j][...], out_grad_refs[j][...])
                put(3 * group, total)
            line = jnp.concatenate([sums[:, :group], sums[:, 2 * group :]], -1)
            top = lax.broadcasted_iota(jnp.int32, (16, 2 * group), 0) == 0
            line = jnp.where(top, line, 0.0).astype(LOW)
            for part in range(parts):
                out_refs[part][size : size + 16] = line if parts == 2 else nn(line, spread[...]).astype(LOW)
                for ref in more_refs:
                    rows = ref[:, part * columns : (part + 1) * columns]
                    rows = jnp.concatenate([rows, jnp.zeros_like(rows)])
                    out_refs[part][size + 16 :] = rows.astype(LOW)
                if not more:
                    out_refs[part][size + 16 :] = jnp.zeros((16, columns), LOW)

        outs = [shape(size + 32, width // parts)] * parts
        rows = qkv_grads[0].shape[0]
        ins = list(qkv_grads) + list(normed) + list(mixed) + list(out_grads) + list(more)
        ins += [self.spread()]
        flops = 2 * count * rows * width * size
        return self.call(body, outs, ins, flops, after=wait, cost=cost)

    def spread(self):
        shards = self.place.shards
        columns, part = self.width // shards, HEAD_DIM // shards
        out = np.zeros((2 * self.group, self.width), np.float32)
        for item in range(2 * self.group):
            head, feature = divmod(item, HEAD_DIM)
            out[item, feature // part * columns + head * part + feature % part] = 1
        return jnp.asarray(out, LOW)

    def temporal_input(self, backs, start, along, matrix, wait=()):
        lay, width = self.layout, self.width
        far = [] if matrix is None else [matrix]

        def body(scalars, *refs):
            back_refs, refs = refs[: self.ranks], refs[self.ranks :]
            start_ref, along_ref, refs = refs[0], refs[1], refs[2:]
            out_ref = refs[len(far)]
            swap = swapper(scalars, self.place.paired)
            unit, inverse = unit_of(start_ref[...].astype(F32))
            grad = swap(sum(ref[...].astype(F32) for ref in back_refs))
            back, _, _ = norm_back(grad, unit, inverse, along_ref[0:1])
            out_ref[...] = back.astype(LOW)
            if far:
                refs[2][...] = nn(refs[0][...], out_ref[...]).astype(LOW)

        outs = [shape(lay.temporal_rows, width)] + [shape(item.shape[0], width) for item in far]
        return self.call(body, outs, list(backs) + [start, along] + far, after=wait)


    def spatial_in(self, sources, matrix, start, fc, along, wait=()):
        lay, width = self.layout, self.width
        rows = lay.frame_rows

        def body(scalars, *refs):
            source_refs, refs = refs[: len(sources)], refs[len(sources) :]
            matrix_ref, start_ref, fc_refs, refs = refs[0], refs[1], refs[2 : 2 + len(fc)], refs[2 + len(fc) :]
            along_ref, after_ref, temporal_ref, normed_ref = refs
            swap = swapper(scalars, self.place.paired)
            source = jnp.concatenate([ref[...] for ref in source_refs])
            temporal = nn(matrix_ref[...], source)
            temporal_ref[...] = temporal.astype(LOW)
            weight = jnp.concatenate([ref[...] for ref in fc_refs])
            after = start_ref[...].astype(F32) + nn(swap(temporal).astype(LOW), weight)
            after = after + along_ref[7:8]
            after_ref[...] = after
            unit, _ = unit_of(after)
            normed_ref[...] = swap(unit * along_ref[1:2] + along_ref[4:5]).astype(LOW)

        outs = [shape(rows, width, dtype=F32), shape(rows, width), shape(rows, width)]
        ins = list(sources) + [matrix, start] + list(fc) + [along]
        return self.call(body, outs, ins, 2 * rows * width * width, after=wait)

    def windows(self, refs, n):
        at = rows_at(n * (WINDOW - 16), WINDOW)
        return jnp.concatenate([ref[at] for ref in refs])

    def window_mask(self, n, axis):
        size = self.quarters * WINDOW
        dims = (size, 1) if axis == 0 else (1, size)
        index = lax.broadcasted_iota(jnp.int32, dims, axis) & (WINDOW - 1)
        start = n * (self.layout.places - WINDOW + 16)
        return (index >= start) & (index < start + self.layout.places)

    def put_windows(self, refs, n, values, mask):
        for j, ref in enumerate(refs):
            at = rows_at(n * (WINDOW - 16), WINDOW)
            part = slice(j * WINDOW, (j + 1) * WINDOW)
            old = ref[at].astype(F32)
            ref[at] = jnp.where(mask[part], values[part], old).astype(LOW)

    def spatial(self, normed, win, shift, wait=()):
        lay, width, quarters, group = self.layout, self.width, self.quarters, self.group

        def body(scalars, *refs):
            normed_refs, refs = refs[:quarters], refs[quarters:]
            win_refs, shift_ref, refs = refs[: len(win)], refs[len(win)], refs[len(win) + 1 :]
            qkv_refs, out_refs = refs[:quarters], refs[quarters:]
            weight = jnp.concatenate([ref[: 3 * group] for ref in win_refs], -1)
            for j in range(quarters):
                qkv_refs[j][...] = (nt(normed_refs[j][...], weight) + shift_ref[...]).astype(LOW)
                out_refs[j][...] = jnp.zeros_like(out_refs[j])

            @pl.loop(0, lay.units, unroll=True)
            def _(n):
                rows = self.windows(qkv_refs, n)
                hide = jnp.where(self.window_mask(n, 0), 0.0, HIDE)
                parts = []
                for h in range(self.heads):
                    query, key, value = (rows[:, self.lanes(c, h)] for c in range(3))
                    parts.append(attention(query * LOW(SCALE), key, value, hide))
                mask = self.window_mask(n, 0)
                self.put_windows(out_refs, n, jnp.concatenate(parts, -1), mask)

        outs = [shape(lay.frame_rows, 3 * group)] * quarters
        outs += [shape(lay.frame_rows, group)] * quarters
        size = quarters * WINDOW
        flops = 6 * quarters * lay.frame_rows * width * group + 4 * lay.units * size * size * group
        outs = self.call(body, outs, list(normed) + list(win) + [shift], flops, after=wait)
        return outs[:quarters], outs[quarters:]

    def spatial_back(self, qkv, grads, win, wait=()):
        lay, width, quarters, group = self.layout, self.width, self.quarters, self.group

        def body(scalars, *refs):
            qkv_refs, grad_refs = refs[:quarters], refs[quarters : 2 * quarters]
            win_refs = refs[2 * quarters : 2 * quarters + len(win)]
            refs = refs[2 * quarters + len(win) :]
            out_refs, back_refs = refs[:quarters], refs[quarters:]
            for ref in out_refs:
                ref[...] = jnp.zeros_like(ref)

            @pl.loop(0, lay.units, unroll=True)
            def _(n):
                rows = self.windows(qkv_refs, n)
                mask = self.window_mask(n, 0)
                grads = self.windows(grad_refs, n) * mask.astype(F32).astype(LOW)
                hide = jnp.where(self.window_mask(n, 0), 0.0, HIDE)
                parts = [[], [], []]
                for h in range(self.heads):
                    query, key, value = (rows[:, self.lanes(c, h)] for c in range(3))
                    grad = grads[:, self.lanes(0, h)]
                    got = attention_back(query * LOW(SCALE), key, value, grad, hide)
                    for part, item in zip(parts, got):
                        part.append(item)
                values = jnp.concatenate(parts[0] + parts[1] + parts[2], -1)
                self.put_windows(out_refs, n, values, mask)

            weight = jnp.concatenate([ref[: 3 * group] for ref in win_refs], -1)
            for j in range(quarters):
                back_refs[j][...] = nn(out_refs[j][...], weight).astype(LOW)

        outs = [shape(lay.frame_rows, 3 * group)] * quarters
        outs += [shape(lay.frame_rows, width)] * quarters
        size = quarters * WINDOW
        flops = 10 * lay.units * size * size * group
        flops += 6 * quarters * lay.frame_rows * width * group
        outs = self.call(body, outs, list(qkv) + list(grads) + list(win), flops, after=wait)
        return outs[:quarters], outs[quarters:]

    def put_groups(self, scalars, out, pieces, first):
        for i in range(self.quarters):
            spot = (scalars[1] ^ i) * self.piece
            for j in range(self.quarters):
                k = group_of(scalars[1]) ^ group_of(j)
                out[rows_at(j * self.group + spot, self.piece)] = pieces[i][
                    k, first : first + self.piece
                ]

    def spatial_out(self, mixed, pieces, first, after, grad, along, wait=()):
        lay, width, group = self.layout, self.width, self.group
        rows, quarters = lay.frame_rows, self.quarters
        size = WINDOW

        def body(scalars, *refs):
            mixed_refs, piece_refs, refs = refs[:quarters], refs[quarters : 2 * quarters], refs[2 * quarters :]
            after_ref, grad_ref, along_ref, out_ref, normed_ref, low_ref, wout = refs
            swap = swapper(scalars, self.place.paired)
            self.put_groups(scalars, wout, piece_refs, 0)
            total = jnp.zeros((rows, width), F32)
            for j in range(quarters):
                total = total + nn(mixed_refs[j][...], wout[j * group : (j + 1) * group])
            after = after_ref[...] + swap(total) + along_ref[8:9]
            out_ref[...] = after
            unit, _ = unit_of(after)
            normed_ref[...] = swap(unit * along_ref[2:3] + along_ref[5:6]).astype(LOW)
            low_ref[...] = swap(grad_ref[...].astype(F32)).astype(LOW)

        outs = [
            shape(rows, width, dtype=F32),
            shape(rows, width),
            shape(rows, width),
            shape(self.all_heads, width),
        ]
        ins = list(mixed) + list(pieces) + [after, grad, along]
        whole = pl.BlockSpec(memory_space=pltpu.VMEM)
        part = pl.BlockSpec((self.ranks, size, width), lambda *_: (0, first // size, 0))
        specs = [whole] * quarters + [part] * quarters + [whole] * 3
        flops = 2 * rows * width * self.all_heads
        return self.call(body, outs, ins, flops, after=wait, specs=specs)

    def feed_forward(self, normed, grad, pieces, shifts, totals):
        lay, width = self.layout, self.width
        rows, count, ranks = lay.frame_rows, len(pieces), self.ranks
        hidden = shifts[0].shape[1]
        unit = hidden // ranks
        tile = hidden

        def body(scalars, normed_ref, grad_ref, *refs):
            refs = list(refs)
            take = lambda n: [refs.pop(0) for _ in range(n)]
            piece_refs, shift_refs = take(count), take(count)
            before = take(2 if totals else 0)
            out_ref, back_ref = take(2)
            grad_refs, sum_refs = take(count), take(count)
            ups, downs, up_grad, down_grad = take(4)
            out_ref[...] = before[0][...] if totals else jnp.zeros_like(out_ref)
            back_ref[...] = before[1][...] if totals else jnp.zeros_like(back_ref)
            for item in range(count):
                for k in range(ranks):
                    at = slice(k * unit, (k + 1) * unit)
                    ups[at] = piece_refs[item][k, :unit]
                    downs[at] = piece_refs[item][k, unit : 2 * unit]

                @pl.loop(0, hidden // tile)
                def _(m, item=item):
                    at = pl.ds(pl.multiple_of(m * tile, tile), tile)
                    up, down = ups[at], downs[at]
                    values = nt(normed_ref[...], up) + shift_refs[item][:, at]
                    half = 0.5 * (1.0 + lax.erf(values * SQRT_HALF))
                    active = (values * half).astype(LOW)
                    slope = half + values * jnp.exp(-0.5 * values * values) * INV_ROOT_TAU
                    out_ref[...] += nn(active, down)
                    down_grad[at] = tn(active, grad_ref[...]).astype(LOW)
                    hidden_grad = (nt(grad_ref[...], down) * slope).astype(LOW)
                    up_grad[at] = tn(hidden_grad, normed_ref[...]).astype(LOW)
                    back_ref[...] += nn(hidden_grad, up)
                    sum_refs[item][:, at] = column_sum(hidden_grad)

                for k in range(ranks):
                    at = slice(k * unit, (k + 1) * unit)
                    grad_refs[item][k, :unit] = up_grad[at]
                    grad_refs[item][k, unit:] = down_grad[at]

        outs = [shape(rows, width, dtype=F32)] * 2
        outs += [shape(ranks, 2 * unit, width)] * count + [shape(1, hidden, dtype=F32)] * count
        ins = [normed, grad] + list(pieces) + list(shifts) + list(totals or ())
        flops = 12 * rows * width * hidden * count
        scratch = [pltpu.VMEM((hidden, width), LOW)] * 4
        outs = self.call(body, outs, ins, flops, scratch)
        return outs[:2], outs[2 : 2 + count], outs[2 + count :]

    def feed_forward_back(self, after, out, back, grad, mixed, wout, along):
        lay, width, group = self.layout, self.width, self.group
        rows, quarters = lay.frame_rows, self.quarters

        def body(scalars, after_ref, out_ref, back_ref, grad_ref, wout_ref, along_ref, *refs):
            mixed_refs, refs = refs[:quarters], refs[quarters:]
            layer_ref, total_ref, sums, wout_grad = refs[:4]
            mixed_grads = refs[4:]
            swap = swapper(scalars, self.place.paired)
            after = after_ref[...]
            layer_ref[...] = (after + swap(out_ref[...]) + along_ref[9:10]).astype(LOW)
            unit, inverse = unit_of(after)
            back, gain, shift = norm_back(swap(back_ref[...]), unit, inverse, along_ref[2:3])
            grad = grad_ref[...].astype(F32)
            total = grad + back
            total_ref[...] = total
            low = total.astype(LOW)
            sums[0:1] = gain
            sums[1:2] = shift
            sums[2:3] = column_sum(low)
            sums[3:4] = column_sum(grad)
            turned = swap(low.astype(F32)).astype(LOW)
            for j in range(quarters):
                at = slice(j * group, (j + 1) * group)
                mixed_grads[j][...] = nt(turned, wout_ref[at]).astype(LOW)
                wout_grad[at] = tn(mixed_refs[j][...], turned).astype(LOW)

        outs = [
            shape(rows, width),
            shape(rows, width, dtype=F32),
            shape(4, width, dtype=F32),
            shape(self.all_heads, width),
        ] + [shape(rows, group)] * quarters
        ins = [after, out, back, grad, wout, along] + list(mixed)
        outs = self.call(body, outs, ins, 4 * rows * width * self.all_heads)
        return outs[:4], outs[4:]

    def spatial_input(self, backs, after, total, along, fc, matrix, wait=()):
        lay, width = self.layout, self.width
        rows, quarters = lay.frame_rows, self.quarters
        far = [] if matrix is None else [matrix]

        def body(scalars, *refs):
            back_refs, refs = refs[:quarters], refs[quarters:]
            after_ref, total_ref, along_ref, refs = refs[0], refs[1], refs[2], refs[3:]
            fc_refs, refs = refs[: len(fc)], refs[len(fc) :]
            low_ref, out_ref, sums = refs[len(far) : len(far) + 3]
            swap = swapper(scalars, self.place.paired)
            grad = swap(sum(ref[...].astype(F32) for ref in back_refs))
            unit, inverse = unit_of(after_ref[...])
            back, gain, shift = norm_back(grad, unit, inverse, along_ref[1:2])
            low = (total_ref[...] + back).astype(LOW)
            low_ref[...] = low
            weight = jnp.concatenate([ref[...] for ref in fc_refs])
            temporal = swap(nt(low, weight)).astype(LOW)
            out_ref[...] = temporal
            sums[0:1] = gain
            sums[1:2] = shift
            sums[2:3] = column_sum(temporal)
            sums[3:4] = column_sum(low)
            if far:
                refs[4][...] = nn(refs[0][...], temporal).astype(LOW)

        outs = [shape(rows, width), shape(rows, width), shape(4, width, dtype=F32)]
        outs += [shape(item.shape[0], width) for item in far]
        ins = list(backs) + [after, total, along] + list(fc) + far
        return self.call(body, outs, ins, 2 * rows * width * width, after=wait)

    def out_weights(self, wout_grad, low, temporal, vectors, wait=()):
        width, group, piece = self.width, self.group, self.piece
        quarters, ranks = self.quarters, self.ranks
        extra, quarter = vectors.shape[1], width // quarters
        each = piece + extra

        def body(scalars, wout_ref, low_ref, temporal_ref, vectors_ref, *refs):
            pieces, fc = refs[:quarters], refs[quarters]
            swap = swapper(scalars, self.place.paired)
            turned = swap(temporal_ref[...].astype(F32)).astype(LOW)
            fc[...] = tn(low_ref[...], turned).astype(LOW)
            for i in range(quarters):
                spot = (scalars[1] ^ i) * piece
                for j in range(quarters):
                    k = group_of(scalars[1]) ^ group_of(j)
                    pieces[i][rows_at(k * each, piece)] = wout_ref[rows_at(j * group + spot, piece)]
                for k in range(ranks):
                    pieces[i][k * each + piece : (k + 1) * each] = vectors_ref[k]
                pieces[i][ranks * each :] = fc[rows_at((scalars[1] ^ i) * quarter, quarter)]

        outs = [shape(ranks * each + quarter, width)] * quarters
        ins = [wout_grad, low, temporal, vectors]
        flops = 2 * low.shape[0] * width * width
        return self.call(body, outs, ins, flops, [pltpu.VMEM((width, width), LOW)], wait)

    def unpack(self, hidden_rows, shared_rows, each):
        columns, quarter = hidden_rows[0].shape[2], self.width // self.quarters
        unit, group, piece = self.unit, self.group, self.piece
        hidden = unit * self.quarters
        at = [0, unit, 0, piece, each, each + quarter]

        def body(scalars, *refs):
            hidden_refs, shared_refs, refs = refs[:2], refs[2:4], refs[4:]
            up_ref, down_ref, out_ref, fc_ref, *refs = refs
            gain_ref, shift_ref, branch_ref, outer_ref, up, fc = refs
            sums = jnp.zeros((16, columns), F32)
            for j in range(self.quarters):
                def rows(n, size):
                    source = (hidden_refs if n < 2 else shared_refs)[j % 2]
                    return source[j // 2, at[n] : at[n] + size].astype(F32)

                spot = scalars[1] ^ j
                up[rows_at(spot * unit, unit)] = rows(0, unit)
                down_ref[rows_at(spot * unit, unit)] = rows(1, unit)
                out_ref[rows_at(spot * piece, piece)] = rows(2, piece)
                fc[rows_at(spot * quarter, quarter)] = rows(4, quarter)
                sums = sums + rows(5, 16)
            up_ref[...] = up[...].T
            fc_ref[...] = fc[...].T
            vectors = shared_refs[0][0, at[3] : at[3] + 16].astype(F32)
            gain_ref[...] = jnp.concatenate([sums[0:1], vectors[0:2]])
            shift_ref[...] = jnp.concatenate([sums[1:2], vectors[2:4]])
            branch_ref[...] = vectors[4:8]
            outer_ref[...] = vectors[8:9]

        sizes = [(columns, hidden), (hidden, columns), (group, columns), (columns, self.width)]
        sizes += [(3, columns), (3, columns), (4, columns), (1, columns)]
        outs = [shape(*size, dtype=F32) for size in sizes]
        scratch = [pltpu.VMEM((hidden, columns), F32), pltpu.VMEM((self.width, columns), F32)]
        return self.call(body, outs, list(hidden_rows) + list(shared_rows), scratch=scratch, cost=6)

    def natural(self, parts, cost, wait=()):
        lay, width = self.layout, self.width
        count = lay.natural_blocks
        counts = [len(rows) for _, rows in parts]

        def body(scalars, *refs):
            refs = list(refs)
            out_ref = refs.pop()
            total = jnp.zeros((count * WINDOW, width), F32)
            for size in counts:
                matrix = refs.pop(0)
                source = jnp.concatenate([refs.pop(0)[...] for _ in range(size)])
                total = total + nn(matrix[...], source)
            total = total.astype(LOW)
            for item in range(count):
                part = total[item * WINDOW : item * WINDOW + lay.places]
                out_ref[item] = part

                @pl.when(jnp.logical_not(self.live(scalars, item // lay.frames)))
                def _(item=item):
                    out_ref[item] = jnp.zeros((lay.places, width), LOW)


        ins = []
        for matrix, rows in parts:
            ins += [matrix] + list(rows)
        return self.call(body, [shape(count, lay.places, width)], ins, after=wait, cost=cost)[0]


def body(
    clip_input,
    clip_slot,
    norm_gain,
    norm_shift,
    attention_in,
    attention_bias,
    attention_out,
    branch_bias,
    temporal_fc,
    hidden_in,
    hidden_bias,
    hidden_out,
    output_grad,
):
    place = Place()
    shards, quarters, ranks = place.shards, place.quarters, place.ranks
    shard, context, tensor = place.shard, place.context, place.tensor
    clips, cotangents = clip_input[:, 0], output_grad[:, 0]
    lay = Layout(place, clips)
    columns = attention_in.shape[1]
    width = columns * shards
    group = attention_in.shape[3]
    heads = group // HEAD_DIM
    hidden = hidden_in.shape[1]
    piece = group // quarters
    scalars = jnp.concatenate([jnp.stack([shard, context, tensor]), clip_slot[:, 0]])
    prog = Program(place, lay, width, group, scalars.astype(jnp.int32))
    moves = lay.matrices()
    split = lay.split > 0

    def beside(rows):
        return [rows, hop(rows, SHARD, 1)] if split else [rows]

    def swapped(rows, axis):
        return [rows[0]] + [hop(rows[k], axis, k) for k in range(1, len(rows))]

    def to_all(rows, axis):
        if axis == CONTEXT:
            far = hop(rows, axis, 2)
            return [rows, hop(rows, axis, 1), far, hop(far, axis, 1)]
        return [rows] + [hop(rows, axis, k) for k in range(1, ranks)]

    def shard_parts(block, axis=1):
        if place.paired:
            return [block, hop(block, SHARD, 1)]
        return [lax.all_gather(block, SHARD, axis=axis, tiled=True)]

    def bias_rows(index):
        rows = attention_bias[index].reshape(-1)
        return jnp.pad(rows, (0, columns - rows.size))[None]

    def in_rows(index):
        return jnp.transpose(attention_in[index], (1, 2, 0)).reshape(3 * group, columns)

    def bias_of(parts, row):
        kinds = 2 * heads * (HEAD_DIM // shards)
        if place.paired:
            lines = [part[row, :kinds] for part in parts]
            lines = jnp.where(shard == 0, jnp.stack(lines), jnp.stack(lines[::-1]))
        else:
            lines = parts[0][row].reshape(shards, columns)[:, :kinds]
        lines = lines.reshape(shards, 2, heads, HEAD_DIM // shards)
        lines = jnp.transpose(lines, (1, 2, 0, 3)).reshape(2, group).astype(F32)
        return jnp.concatenate([lines[0], jnp.zeros(group, F32), lines[1]])[None]

    flat = lambda rows: rows.reshape((-1,) + rows.shape[2:])
    clips, cotangents = flat(clips), flat(cotangents)
    quarter = lambda rows: pick(rows.reshape(quarters, -1, columns), context)
    up_part = pick(hidden_in.reshape(columns, quarters, -1), context, 1).T
    unit = up_part.shape[0]
    block = [up_part, quarter(hidden_out), quarter(attention_out[1])]
    block.append(jnp.pad(hidden_bias.reshape(1, -1), ((0, 15), (0, 0))))
    gather_c = Gather(place, jnp.concatenate(block))

    along = jnp.concatenate([norm_gain, norm_shift, branch_bias, bias_rows(0)])
    along = shard_parts(jnp.pad(along, ((0, 16 - along.shape[0]), (0, 0))))
    shift_a = bias_of(along, 10)
    if place.paired:
        along = jnp.where(shard == 0, *[jnp.concatenate(pair, -1) for pair in (along, along[::-1])])
    else:
        along = along[0]
    along = along[:10].astype(F32)

    come, others = None, None
    if split:
        sent, others = prog.send_rows(clips, cotangents, moves[Move.begin_far])
        come = hop(sent, SHARD, 1)
    weights_a = jnp.concatenate([in_rows(0), attention_out[0]])
    weights_a = shard_parts(tie(weights_a, come) if split else weights_a)
    start_t, unit_a = prog.temporal_start(clips, come, moves[Move.beginning])
    units_a = to_all(unit_a, TENSOR)
    gather_c.columns(unit_a)
    gather_c.rows()

    qkv_a, mixed_a, normed_a, parts = prog.temporal(
        units_a, weights_a, along, shift_a
    )
    fc = shard_parts(tie(temporal_fc, parts[0]), 0)
    if split:
        others = hop(tie(others, units_a[1]), SHARD, 1)
    temporal_t = prog.temporal_out(
        swapped(parts, TENSOR), along, moves.get(Move.return_far), gather_c.far
    )
    sources = [temporal_t[0]] + [hop(rows, SHARD, 1) for rows in temporal_t[1:]]
    in_b = jnp.concatenate([in_rows(1), jnp.pad(bias_rows(1), ((0, 15), (0, 0)))])
    in_b = hop_group(tie(in_b, sources[-1]))
    weights_b = shard_parts(in_b)
    shift_b = bias_of(weights_b, 3 * group)

    start = prog.frames_of(clips, others, 0, moves[Move.starting], Cost.frames_start, [units_a[1]])
    after_a, temporal, normed_b = prog.spatial_in(
        sources, moves[Move.returning], start, fc, along
    )
    normed_b = to_all(normed_b, CONTEXT)
    qkv_b, mixed = prog.spatial(normed_b, weights_b, shift_b)
    mixed = swapped(mixed, CONTEXT)
    grad = prog.frames_of(
        cotangents, others, 1, moves[Move.starting], Cost.frames_grad, [parts[0]]
    )
    pieces_c = gather_c.cores(after_a)
    line = gather_c.first[:, 2 * unit + piece].astype(F32)
    up_shift = line.reshape((ranks, shards) + hidden_bias.shape)
    if place.paired:
        up_shift = jnp.where(shard == 0, up_shift, up_shift[:, ::-1])
    up_shift = jnp.swapaxes(up_shift, 1, 2).reshape(ranks, quarters, unit)
    up_shift = [pick(up_shift, context ^ j, 1).reshape(1, -1) for j in range(quarters)]
    after_b, normed_c, low, wout_b = prog.spatial_out(
        mixed, pieces_c, 2 * unit, after_a, grad, along
    )

    totals = None
    piece_grads, up_bias_grads = [None] * quarters, [None] * quarters
    for pair in ((1, 3), (0, 2)):
        totals, grads, sums = prog.feed_forward(
            normed_c, low, [pieces_c[j] for j in pair], [up_shift[j] for j in pair], totals
        )
        for index, j in enumerate(pair):
            piece_grads[j] = grads[index]
            up_bias_grads[j] = sums[index]
    reduce_c = ReduceHidden(place, piece_grads)
    kept, mixed_grads = prog.feed_forward_back(
        after_b, totals[0], totals[1], grad, mixed, wout_b, along
    )
    layer_rows, total, sums_c, wout_grad = kept
    wait = reduce_c.cores(layer_rows)

    mixed_grads = swapped(mixed_grads, CONTEXT)
    qkv_grads, backs = prog.spatial_back(qkv_b, mixed_grads, weights_b, wait)
    done = backs[0]
    reduce_c.start_low(done)
    backs = swapped(backs, CONTEXT)
    group_grads = prog.group_weights(qkv_grads, normed_b, wait=[reduce_c.come_top] if split else ())
    low_total, temporal_grad, sums_b, *sent = prog.spatial_input(
        backs, after_a, total, along, fc, moves.get(Move.arrive_far), [group_grads[0]]
    )

    sources = [temporal_grad] + [hop(rows, SHARD, 1) for rows in sent]
    out_grad = prog.temporal_grad(sources, moves[Move.arriving])
    out_grads = to_all(out_grad, TENSOR)
    layer_out, home = [(moves[Move.ending], [layer_rows])], [(moves[Move.ending], [low_total])]
    if split:
        far = hop(tie(jnp.concatenate([layer_rows[lay.own :], low_total[lay.own :]]), out_grad), SHARD, 1)
        layer_out.append((moves[Move.end_far], [far[: far.shape[0] // 2]]))
        home.append((moves[Move.end_far], [far[far.shape[0] // 2 :]]))
    layer_out = prog.natural(layer_out, Cost.natural_first, [out_grad])
    grads_b = group_grads
    sums = [sums_b[0], sums_c[0], sums_b[1], sums_c[1], sums_b[2], sums_b[3], sums_c[2], sums_c[3]]
    outer = ordered([item.reshape(ranks, -1) for item in up_bias_grads], context, 1)
    outer = outer.reshape(ranks, -1, shards, hidden_bias.shape[1])
    outer = jnp.swapaxes(outer, 1, 2).reshape(ranks, 1, width)
    sums = jnp.stack(sums)
    vectors = jnp.concatenate([jnp.broadcast_to(sums, (ranks,) + sums.shape), outer], 1)
    if place.paired:
        flipped = jnp.concatenate([vectors[..., columns:], vectors[..., :columns]], -1)
        vectors = jnp.where(shard == 0, vectors, flipped)
    vectors = jnp.pad(vectors, ((0, 0), (0, 16 - vectors.shape[1]), (0, 0))).astype(LOW)
    pieces = prog.out_weights(wout_grad, low_total, temporal, vectors, [out_grad, reduce_c.come_low])
    reduce_out = ReduceShared(place, pieces, piece + vectors.shape[1])
    reduce_out.cores(out_grads[1])
    wait = [layer_out, pieces[0]] + reduce_c.low_leg(out_grad) + reduce_c.top_leg(out_grad)
    qkv_grads, backs, sums_a = prog.temporal_back(qkv_a, out_grads, units_a, weights_a, wait)
    done = backs[0]
    backs = swapped(backs, TENSOR)
    group_grads = prog.group_weights(
        qkv_grads, normed_a, mixed_a, out_grads, [sums_a], cost=Cost.group_weights_last
    )
    back, *sent = prog.temporal_input(
        backs, start_t, along, moves.get(Move.home_far), reduce_out.rows(done) + [group_grads[0]]
    )
    reduce_c.both(back)
    total_in_b = hop_group(sum_columns(place, grads_b[0], grads_b[-1], back))
    total_in_a = sum_columns(place, group_grads[0], group_grads[-1])
    home.append((moves[Move.homing], [back] + [hop(rows, SHARD, 1) for rows in sent]))
    input_grad = prog.natural(home, Cost.natural_last)

    reduce_out.columns(total_in_a[4 * group + 16 :])
    sum_in = SumContext(place, jnp.concatenate([total_in_a, tie(total_in_b, back)]))
    sum_in.cores()
    reduce_c.hops()
    reduce_out.hops()
    prog.unit = unit
    hidden_rows, shared_rows = reduce_c.finish(), reduce_out.finish()
    up_total, down_total, out_b, fc_total, gains, shifts, branch, outer = prog.unpack(
        hidden_rows, shared_rows, reduce_out.each
    )
    total_in = sum_in.finish()
    total_in_a, total_in_b = total_in[: total_in_a.shape[0]], total_in[total_in_a.shape[0] :]

    def in_grad(total):
        part = total[: 3 * group].reshape(3, group, columns)
        return jnp.transpose(part, (2, 0, 1))

    def bias_grad(line):
        part = HEAD_DIM // shards
        if place.paired:
            return pick(line.reshape(2, heads, shards, part), shard, 2)
        return line[: 2 * heads * part].reshape(2, heads, part)

    in_total = jnp.stack([in_grad(total_in_a), in_grad(total_in_b)])
    inner = jnp.stack([bias_grad(total_in_a[4 * group]), bias_grad(total_in_b[3 * group])])
    out_total = jnp.stack([total_in_a[3 * group : 4 * group], out_b])
    rows_shape = clip_input.shape
    return (
        layer_out.reshape(rows_shape),
        input_grad.reshape(rows_shape),
        gains,
        shifts,
        in_total,
        inner,
        out_total,
        branch,
        fc_total,
        up_total,
        outer.reshape(hidden_bias.shape),
        down_total,
    )


def solution(mesh):
    rows = P(None, SHARD, TENSOR, CONTEXT, None)
    weights = (
        P(None, SHARD),
        P(None, SHARD),
        P(None, SHARD, None, TENSOR),
        P(None, None, TENSOR, SHARD),
        P(None, TENSOR, SHARD),
        P(None, SHARD),
        P(SHARD, None),
        P(SHARD, TENSOR),
        P(TENSOR, SHARD),
        P(TENSOR, SHARD),
    )
    return jax.shard_map(
        body,
        mesh=mesh,
        in_specs=(rows, P(None, SHARD)) + weights + (rows,),
        out_specs=(rows, rows) + weights,
        check_vma=False,
    )
```
